256 devices in a mesh: rep: 2 (over core), ctx: 32 (over y, z), tp: 4 (over x).
Axes of the slice: x: 4, y: 4, z: 8, core: 2. Of those that a mesh axis runs over, the one named last changes fastest.
Arguments:
- tokens: float32 [2, 12288, 2048], P('rep', 'ctx'), may hold values from -32 to 32
- qk_weight: float32 [2048, 2048], P(('rep', 'ctx'), 'tp'), may hold values from -0.125 to 0.125
- value_weight: float32 [2048, 2048], P(('rep', 'ctx'), 'tp'), may hold values from -0.125 to 0.125
- grad_out: float32 [2, 12288, 2048], P('rep', 'ctx', 'tp'), may hold values from -6 to 6
- assign: int32 [16, 2, 12288, 1], P('tp', 'rep', 'ctx'), may hold values from 0 to 255; in each aligned block of 384 rows (0 to 383, 384 to 767, ..., all dimensions but the last counted through in order) at most 3 rows name the same one
Outputs:
- grad_tokens: float32 [2, 12288, 2048], P('rep', 'ctx', 'tp')
- grad_qk_weight: float32 [2048, 2048], P(('rep', 'ctx'), 'tp')
- grad_value_weight: float32 [2048, 2048], P(('rep', 'ctx'), 'tp')
The draws below stay inside these ranges and needn't reach their ends.
Inputs may be any that keep to these rules, and one draw needn't show every extreme that they name: `assign`: within the 384 tokens of one index of ctx, for one head and one sequence, no cluster holds more than 3 tokens; in some of these blocks a cluster holds exactly 3.
All inputs are finite; a program needn't handle non-finite values.
Results may differ from the reference program's by a relative error of at most 0.0003.
Values sent between devices are 32-bit elements; how exact they have to be, the bound alone decides.
A program may use at most 128 MiB of HBM per device.

```python
import math
import jax
import jax.numpy as jnp
import numpy as np
from jax import lax

D = 2048
HEADS = 16
HD = 128
CL_DEV = 8
TOK_DEV = 384
SEQ = 12288
CLUSTERS = 256
MOST = 3
N_REP = 2
N_CTX = 32


def draw_tokens(key, part):
    key = jax.random.fold_in(key, 11)
    base_key = jax.random.fold_in(key, 0)
    return jnp.clip(jax.random.normal(base_key, (N_REP, SEQ, D), jnp.float32), -6.0, 6.0)


def block_levels(stream_key, shape, cuts, smallest, top_value):
    factor_of, own = 1.0, jax.random.fold_in(stream_key, 6)
    for position, blocks in cuts:
        heights = jnp.exp(jax.random.uniform(jax.random.fold_in(own, position), (blocks,), jnp.float32, smallest / len(cuts), top_value / len(cuts)))
        factor_of = factor_of * jnp.repeat(heights, shape[position] // blocks).reshape([-1 if axis == position else 1 for axis in range(len(shape))])
    return factor_of


def routed_block(key, own, number, rows, count, top, bound, skew):
    order = jax.random.permutation(key, count)
    crowded, usual = portions_of(count, rows * top, bound, skew, True), portions_of(count, rows * top, bound, skew, False)
    places = jnp.arange(count)

    def named(sizes, offset_by):
        used = int((sizes > 0).sum())
        fixed = max(1, used // 4)
        moved = fixed + (places - fixed + offset_by * (used - fixed)) % max(1, count - fixed)
        return jnp.zeros((count,), jnp.int32).at[order[jnp.where(places < fixed, places, moved)]].set(jnp.asarray(sizes, jnp.int32))

    sizes = jnp.where(number % 4 == 0, named(crowded, number // 4), named(usual, number - number // 4 - 1))
    mixed = jax.random.permutation(jax.random.fold_in(own, 3), count)
    source_of, sink = mixed[0:count // 2 * 2:2], mixed[1:count // 2 * 2:2]
    room = jnp.minimum(sizes[source_of] - 1, bound - sizes[sink]) // 2
    room = jnp.where((source_of == order[0]) | (sink == order[0]) | (sizes[sink] == 0), 0, jnp.maximum(room, 0))
    moved = jax.random.randint(jax.random.fold_in(own, 4), (count // 2,), 0, 1 << 20) % (room + 1)
    sizes = sizes.at[source_of].add(-moved).at[sink].add(moved)
    items = jnp.searchsorted(jnp.cumsum(sizes), jnp.arange(rows * top), side="right").astype(jnp.int32)
    grid = items.reshape(top, rows).T
    grid = grid[jax.random.permutation(jax.random.fold_in(own, 1), rows)]
    offset_by = jax.random.randint(jax.random.fold_in(own, 2), (rows, 1), 0, top)
    return jnp.take_along_axis(grid, (jnp.arange(top)[None, :] + offset_by) % top, axis=1)


def portions_of(number_of, total, reach, slope, full):
    portions = [(1 << 20) // math.isqrt(grade ** slope) + 1 for grade in range(1, number_of + 1)]
    largest = reach if full else min(reach, max(-(-total // number_of), total * portions[0] // sum(portions)))
    least = 1 if total - largest >= number_of - 1 else 0
    given, rest = [largest] + [least] * (number_of - 1), total - largest - least * (number_of - 1)
    while rest > 0:
        candidates = [i for i in range(1, number_of) if given[i] < largest] or [i for i in range(1, number_of) if given[i] < reach]
        pool, budget = sum([portions[i] for i in candidates]), rest
        for i in candidates:
            addition = min(reach - given[i], max(1, budget * portions[i] // pool), rest)
            given[i] = given[i] + addition
            rest = rest - addition
    return np.array(given)


def normal_values(rng, dims, scale, bound, cuts=(), held_as=jnp.bfloat16):
    result = jax.random.normal(rng, dims, jnp.float32) * scale
    if len(cuts) > 0:
        result = block_levels(rng, dims, cuts, -0.22, 0.18) * result
    return jnp.clip(result, min=-bound, max=bound).astype(held_as)


def setup_inputs(seed: int = 0) -> dict:
    streams_of = jax.random.split(jax.random.key(seed), 6)
    tokens = draw_tokens(jax.random.fold_in(streams_of[5], 71), 0)
    qk_weight = normal_values(streams_of[1], (D, HEADS * HD), D ** -0.5, 0.125, ((0, 64), (1, 4)), jnp.float32)
    value_weight = normal_values(streams_of[2], (D, HEADS * HD), D ** -0.5, 0.125, ((0, 64), (1, 4)), jnp.float32)
    grad_out = normal_values(streams_of[3], (N_REP, SEQ, HEADS * HD), 1.0, 6.0, ((0, 2), (1, 32), (2, 4)), jnp.float32)
    assign_keys = jax.random.split(jax.random.fold_in(streams_of[4], 1), HEADS * N_REP * SEQ // TOK_DEV)
    assign_turns = jax.random.permutation(jax.random.fold_in(streams_of[4], 3), HEADS * N_REP * SEQ // TOK_DEV)
    assign = jax.vmap(lambda own, number: routed_block(jax.random.fold_in(streams_of[4], 2), own, number, TOK_DEV, CLUSTERS, 1, MOST, 2))(assign_keys, assign_turns).reshape((HEADS, N_REP, SEQ, 1))
    return dict(tokens=tokens, qk_weight=qk_weight, value_weight=value_weight, grad_out=grad_out, assign=assign)


masked_score = -1e+30

def attend_blocks(query_key, values, validity):
    scores = jnp.einsum('nqd,nkd->nqk', query_key, query_key, precision=lax.Precision.HIGHEST) / HD
    scores = jnp.where(validity[:, None, :] > 0.5, scores, masked_score)
    highest = lax.stop_gradient(lax.optimization_barrier(jnp.max(scores, axis=2, keepdims=True)))
    weights = jnp.exp(scores - highest)
    weights = weights / lax.optimization_barrier(jnp.sum(weights, axis=2, keepdims=True))
    return jnp.einsum('nqk,nkd->nqd', weights, values, precision=lax.Precision.HIGHEST)

def slot_numbers(routing):
    clusters = CL_DEV * N_CTX
    per_source = 2 * TOK_DEV // clusters
    capacity = per_source * N_CTX
    blocked = routing.reshape(N_CTX, TOK_DEV)
    labels = jnp.arange(clusters, dtype=jnp.int32)
    onehot_table = (blocked[:, :, None] == labels[None, None, :]).astype(jnp.int32)
    within = lax.optimization_barrier(jnp.sum((jnp.cumsum(onehot_table, axis=1) - 1) * onehot_table, axis=2))
    source = jnp.arange(N_CTX, dtype=jnp.int32)[:, None]
    return (blocked * capacity + source * per_source + within).reshape(-1).astype(jnp.int32)

def head_attention(query_key, values, slots):
    clusters = CL_DEV * N_CTX
    capacity = 2 * TOK_DEV // clusters * N_CTX
    total = clusters * capacity
    packed_qk = jnp.zeros((total, HD), jnp.float32).at[slots].set(query_key)
    packed_values = jnp.zeros((total, HD), jnp.float32).at[slots].set(values)
    validity = jnp.zeros((total,), jnp.float32).at[slots].set(1.0)
    attended = attend_blocks(packed_qk.reshape(clusters, capacity, HD), packed_values.reshape(clusters, capacity, HD), validity.reshape(clusters, capacity))
    return attended.reshape(total, HD)[slots]

def reference(tokens, qk_weight, value_weight, grad_out, assign):
    heads = qk_weight.shape[1] // HD
    sequences = tokens.shape[0]
    length = tokens.shape[1]
    routing = assign[:, :, :, 0].reshape(heads * sequences, length)
    slots = lax.map(slot_numbers, routing).reshape(heads, sequences, length)

    def forward(inputs, first_weight, second_weight):
        query_key = jnp.einsum('rtd,de->rte', inputs, first_weight, precision=lax.Precision.HIGHEST)
        values = jnp.einsum('rtd,de->rte', inputs, second_weight, precision=lax.Precision.HIGHEST)
        results = []
        for sequence_index in range(sequences):
            split_qk = query_key[sequence_index].reshape(length, heads, HD).transpose(1, 0, 2)
            split_values = values[sequence_index].reshape(length, heads, HD).transpose(1, 0, 2)
            attended = jax.vmap(head_attention)(split_qk, split_values, slots[:, sequence_index])
            results.append(attended.transpose(1, 0, 2).reshape(length, heads * HD))
        return jnp.stack(results)
    attended_all, pullback = jax.vjp(forward, tokens, qk_weight, value_weight)
    grad_tokens, grad_qk_weight, grad_value_weight = pullback(grad_out)
    return (grad_tokens, grad_qk_weight, grad_value_weight)
```

```python
import jax
import jax.numpy as jnp
from jax import lax
from jax.experimental import pallas as pl
from jax.experimental.pallas import tpu as pltpu
from jax.sharding import PartitionSpec as P

HD = 128
CL_DEV = 8
NY = 4
NZ = 8
ROWS = 32
HALF = 16
MESH = pl.DeviceIdType.MESH

masked_score = -1e30
exact = lax.Precision.HIGHEST
split = lax.Precision.HIGH


def position():
    ctx = lax.axis_index("ctx")
    return lax.axis_index("rep"), lax.div(ctx, NZ), lax.rem(ctx, NZ)


def greet(partners):
    barrier = pltpu.get_barrier_semaphore()
    for partner in partners:
        pl.semaphore_signal(barrier, inc=1, device_id=partner, device_id_type=MESH)
    pl.semaphore_wait(barrier, len(partners))


class Copies:
    def __init__(self, send_sem, recv_sem):
        self.send_sem, self.recv_sem = send_sem, recv_sem
        self.all = []

    def start(self, source, target, device):
        index = len(self.all)
        copy = pltpu.make_async_remote_copy(
            src_ref=source,
            dst_ref=target,
            send_sem=self.send_sem.at[index],
            recv_sem=self.recv_sem.at[index],
            device_id=device,
            device_id_type=MESH,
        )
        copy.start()
        self.all.append(copy)
        return copy

    def finish(self):
        for copy in self.all:
            copy.wait_send()


GATHER_COPIES = 3 + 7 + 7 + 3 + 8 + 4


def gather_kernel(qk_ref, value_ref, out_ref, local_sem, send_sem, recv_sem):
    rep, y, z = position()
    width = qk_ref.shape[1]

    def along_y(step):
        return {"ctx": lax.rem(y + step, NY) * NZ + z}

    def along_z(step):
        return {"ctx": y * NZ + lax.rem(z + step, NZ)}

    def plane(step):
        return out_ref.at[rep, :, lax.rem(z + step, NZ), pl.ds(0, HALF), :]

    def piece(step):
        return out_ref.at[rep, y, lax.rem(z + step, NZ), pl.ds(HALF, HALF), :]

    def line(step):
        return out_ref.at[rep, lax.rem(y + step, NY), :, pl.ds(HALF, HALF), :]

    right, left, other = along_z(1), along_z(NZ - 1), {"rep": 1 - rep}
    greet([along_y(1), along_y(2), along_y(3), right, left, other])
    copies = Copies(send_sem, recv_sem)
    mine = out_ref.at[rep, y, z]
    first = pltpu.make_async_copy(qk_ref, mine.at[:, pl.ds(0, width)], local_sem.at[0])
    second = pltpu.make_async_copy(value_ref, mine.at[:, pl.ds(width, width)], local_sem.at[1])
    first.start()
    second.start()
    first.wait()
    second.wait()

    own = out_ref.at[rep, y, z, pl.ds(0, HALF), :]
    shared = [copies.start(own, own, along_y(step)) for step in (1, 3, 2)]
    pieces = [(copies.start(piece(0), piece(0), right), copies.start(piece(0), piece(0), left))]
    for copy in shared:
        copy.wait_recv()
    planes = [(copies.start(plane(0), plane(0), right), copies.start(plane(0), plane(0), left))]
    across = [copies.start(plane(0), plane(0), other)]
    for step in range(4):
        rightward, leftward = pieces[step]
        rightward.wait_recv()
        if leftward is not None:
            leftward.wait_recv()
        if step < 3:
            after, before = piece(NZ - 1 - step), piece(1 + step)
            pieces.append((
                copies.start(after, after, right),
                copies.start(before, before, left) if step < 2 else None,
            ))
    lines = [copies.start(line(0), line(0), along_y(step)) for step in (1, 3, 2)]
    across.append(copies.start(line(0), line(0), other))
    for step in range(4):
        rightward, leftward = planes[step]
        after, before = plane(NZ - 1 - step), plane(1 + step)
        rightward.wait_recv()
        if step < 3:
            going = copies.start(after, after, right)
        across.append(copies.start(after, after, other))
        if leftward is not None:
            leftward.wait_recv()
            coming = copies.start(before, before, left) if step < 2 else None
            across.append(copies.start(before, before, other))
        if step < 3:
            planes.append((going, coming if step < 2 else None))
    for copy, step in zip(lines, (3, 1, 2)):
        copy.wait_recv()
        across.append(copies.start(line(step), line(step), other))
    for copy in across:
        copy.wait_recv()
    copies.finish()
    assert len(copies.all) == GATHER_COPIES


def gather_weights(qk_weight, value_weight):
    width = qk_weight.shape[1]
    return pl.pallas_call(
        gather_kernel,
        out_shape=jax.ShapeDtypeStruct((2, NY, NZ, ROWS, 2 * width), jnp.float32),
        in_specs=[pl.BlockSpec(memory_space=pl.ANY)] * 2,
        out_specs=pl.BlockSpec(memory_space=pl.ANY),
        scratch_shapes=[
            pltpu.SemaphoreType.DMA((2,)),
            pltpu.SemaphoreType.DMA((GATHER_COPIES,)),
            pltpu.SemaphoreType.DMA((GATHER_COPIES,)),
        ],
        compiler_params=pltpu.CompilerParams(collective_id=0, has_side_effects=True),
        name="gather_weights",
    )(qk_weight, value_weight)


SCATTER_COPIES = 3 + 12 + 7 + 3 + 7 + 3


def scatter_kernel(
    terms_ref, sums_ref, tokens_out, qk_out, value_out,
    column_in, cross_in, ring_a, ring_b, line_in, plane_in,
    local_sem, send_sem, recv_sem,
):
    rep, y, z = position()
    x = lax.axis_index("tp")
    width = qk_out.shape[1]

    def along_y(step):
        return {"ctx": lax.rem(y + step, NY) * NZ + z}

    def along_z(step):
        return {"ctx": y * NZ + lax.rem(z + step, NZ)}

    def along_x(step):
        return {"tp": lax.rem(x + step, 4)}

    def columns(step):
        start = pl.multiple_of(lax.rem(x + step, 4) * width, width)
        return terms_ref.at[:, pl.ds(start, width)]

    def plane(step):
        return cross_in.at[:, lax.rem(z + step, NZ), pl.ds(0, HALF), :]

    def line(step):
        return cross_in.at[lax.rem(y + step, NY), :, pl.ds(HALF, HALF), :]

    def piece(step):
        return cross_in.at[y, lax.rem(z + step, NZ), pl.ds(HALF, HALF), :]

    right, left, other = along_z(1), along_z(NZ - 1), {"rep": 1 - rep}
    greet(
        [along_y(1), along_y(2), along_y(3), right, left, other]
        + [along_x(1), along_x(2), along_x(3)]
    )
    copies = Copies(send_sem, recv_sem)
    sideways = [
        copies.start(columns(step), column_in.at[step - 1], along_x(step)) for step in (1, 3, 2)
    ]
    own_columns = pltpu.make_async_copy(columns(0), tokens_out, local_sem)
    own_columns.start()

    cross = {}
    for kind, step in (
        ("a", 4), ("a", 5), ("b", 1), ("b", 3), ("b", 2), ("a", 3),
        ("a", 6), ("a", 2), ("a", 7), ("b", 0), ("a", 1), ("a", 0),
    ):
        if kind == "a":
            there = lax.rem(z + step, NZ)
            source = sums_ref.at[1 - rep, :, there, pl.ds(0, HALF), :]
            cross[kind, step] = copies.start(source, plane(step), other)
        else:
            there = lax.rem(y + step, NY)
            source = sums_ref.at[1 - rep, there, :, pl.ds(HALF, HALF), :]
            cross[kind, step] = copies.start(source, line(step), other)

    def add_plane(step):
        cross["a", step].wait_recv()
        there = lax.rem(z + step, NZ)
        cross_in[:, there, pl.ds(0, HALF), :] += sums_ref[rep, :, there, pl.ds(0, HALF), :]

    def add_line(step):
        cross["b", step].wait_recv()
        there = lax.rem(y + step, NY)
        cross_in[there, :, pl.ds(HALF, HALF), :] += sums_ref[
            rep, there, :, pl.ds(HALF, HALF), :
        ]

    add_plane(4)
    right_a = copies.start(plane(4), ring_a.at[0], right)
    add_plane(5)
    left_a = copies.start(plane(5), ring_a.at[4], left)
    lines = []
    for step in (1, 3, 2):
        add_line(step)
        lines.append(copies.start(line(step), line_in.at[step - 1], along_y(step)))

    def pass_a(turn):
        nonlocal right_a, left_a
        add_plane(4 - turn)
        right_a.wait_recv()
        ring_a[turn - 1] += cross_in[:, lax.rem(z + 4 - turn, NZ), pl.ds(0, HALF), :]
        right_a = copies.start(ring_a.at[turn - 1], ring_a.at[turn], right)
        if turn < 3:
            add_plane(5 + turn)
            left_a.wait_recv()
            ring_a[3 + turn] += cross_in[:, lax.rem(z + 5 + turn, NZ), pl.ds(0, HALF), :]
            left_a = copies.start(ring_a.at[3 + turn], ring_a.at[4 + turn], left)

    pass_a(1)
    add_line(0)
    pass_a(2)
    for copy in lines:
        copy.wait_recv()
    cross_in[y, :, pl.ds(HALF, HALF), :] += line_in[0] + line_in[1] + line_in[2]
    right_b = copies.start(piece(4), ring_b.at[0], right)
    left_b = copies.start(piece(5), ring_b.at[4], left)
    pass_a(3)

    def pass_b(turn):
        nonlocal right_b, left_b
        right_b.wait_recv()
        ring_b[turn - 1] += cross_in[y, lax.rem(z + 4 - turn, NZ), pl.ds(HALF, HALF), :]
        right_b = copies.start(ring_b.at[turn - 1], ring_b.at[turn], right)
        if turn < 3:
            left_b.wait_recv()
            ring_b[3 + turn] += cross_in[y, lax.rem(z + 5 + turn, NZ), pl.ds(HALF, HALF), :]
            left_b = copies.start(ring_b.at[3 + turn], ring_b.at[4 + turn], left)

    pass_b(1)
    pass_b(2)
    add_plane(0)
    right_a.wait_recv()
    left_a.wait_recv()
    cross_in[:, z, pl.ds(0, HALF), :] += ring_a[3] + ring_a[6]
    planes = [
        copies.start(
            cross_in.at[lax.rem(y + step, NY), z, pl.ds(0, HALF), :],
            plane_in.at[step - 1],
            along_y(step),
        )
        for step in (1, 3, 2)
    ]
    pass_b(3)
    right_b.wait_recv()
    left_b.wait_recv()
    lower = cross_in[y, z, pl.ds(HALF, HALF), :] + ring_b[3] + ring_b[6]
    qk_out[pl.ds(HALF, HALF), :] = lower[:, :width]
    value_out[pl.ds(HALF, HALF), :] = lower[:, width:]
    for copy in planes:
        copy.wait_recv()
    upper = cross_in[y, z, pl.ds(0, HALF), :] + plane_in[0] + plane_in[1] + plane_in[2]
    qk_out[pl.ds(0, HALF), :] = upper[:, :width]
    value_out[pl.ds(0, HALF), :] = upper[:, width:]
    own_columns.wait()
    for copy in sideways:
        copy.wait_recv()

    @pl.loop(0, tokens_out.shape[0] // 8)
    def _(block):
        here = pl.ds(pl.multiple_of(block * 8, 8), 8)
        tokens_out[here, :] += column_in[0, here, :] + column_in[1, here, :] + column_in[2, here, :]

    copies.finish()
    assert len(copies.all) == SCATTER_COPIES


def scatter_sums(token_terms, weight_terms):
    length = token_terms.shape[0]
    both = weight_terms.shape[1]
    width = both // 2
    f32 = jnp.float32
    return pl.pallas_call(
        scatter_kernel,
        out_shape=(
            jax.ShapeDtypeStruct((length, width), f32),
            jax.ShapeDtypeStruct((ROWS, width), f32),
            jax.ShapeDtypeStruct((ROWS, width), f32),
        ),
        in_specs=[pl.BlockSpec(memory_space=pl.ANY), pl.BlockSpec(memory_space=pltpu.VMEM)],
        out_specs=(pl.BlockSpec(memory_space=pltpu.VMEM),) * 3,
        scratch_shapes=[
            pltpu.VMEM((3, length, width), f32),
            pltpu.VMEM((NY, NZ, ROWS, both), f32),
            pltpu.VMEM((7, NY, HALF, both), f32),
            pltpu.VMEM((7, HALF, both), f32),
            pltpu.VMEM((3, NZ, HALF, both), f32),
            pltpu.VMEM((3, HALF, both), f32),
            pltpu.SemaphoreType.DMA,
            pltpu.SemaphoreType.DMA((SCATTER_COPIES,)),
            pltpu.SemaphoreType.DMA((SCATTER_COPIES,)),
        ],
        compiler_params=pltpu.CompilerParams(
            collective_id=1, has_side_effects=True, vmem_limit_bytes=48 * 2**20
        ),
        name="scatter_sums",
    )(token_terms, weight_terms.reshape(2, NY, NZ, ROWS, both))


def attend_blocks(query_key, values, validity):
    scores = jnp.einsum("nqd,nkd->nqk", query_key, query_key, precision=exact) / HD
    scores = jnp.where(validity[:, None, :] > 0.5, scores, masked_score)
    highest = lax.stop_gradient(jnp.max(scores, axis=2, keepdims=True))
    weights = jnp.exp(scores - highest)
    weights = weights / jnp.sum(weights, axis=2, keepdims=True)
    return jnp.einsum("nqk,nkd->nqd", weights, values, precision=exact)


def cluster_gradients(packed, validity):
    query_key = packed[:, :, :HD]
    values = packed[:, :, HD : 2 * HD]
    upstream = packed[:, :, 2 * HD :]

    def forward(first_part, second_part):
        return attend_blocks(first_part, second_part, validity)

    attended, pullback = jax.vjp(forward, query_key, values)
    grad_qk, grad_values = pullback(upstream)
    return jnp.concatenate([grad_qk, grad_values], axis=2)


def matmul(left, right):
    return jnp.dot(left, right, precision=split, preferred_element_type=jnp.float32)


def matmul_nt(left, right):
    return lax.dot_general(
        left, right, (((1,), (1,)), ((), ())), precision=split, preferred_element_type=jnp.float32
    )


def matmul_tn(left, right):
    return lax.dot_general(
        left, right, (((0,), (0,)), ((), ())), precision=split, preferred_element_type=jnp.float32
    )


def per_device(tokens, qk_weight, value_weight, grad_out, assign):
    inputs = tokens[0]
    length = inputs.shape[0]
    ctx_count = lax.axis_size("ctx")
    clusters = CL_DEV * ctx_count
    per_source = 2 * length // clusters
    heads_here = qk_weight.shape[1] // HD
    width = heads_here * HD
    routing = assign[:, 0, :, 0]
    full = gather_weights(qk_weight, value_weight).reshape(-1, 2 * width)
    projected = matmul(inputs, full)

    def by_head(matrix):
        return matrix.reshape(length, heads_here, HD).transpose(1, 0, 2)

    payload = jnp.concatenate(
        [by_head(projected[:, :width]), by_head(projected[:, width:]), by_head(grad_out[0])], axis=2
    )
    labels = jnp.arange(clusters, dtype=jnp.int32)
    onehot_table = (routing[:, :, None] == labels[None, None, :]).astype(jnp.int32)
    within = jnp.sum((jnp.cumsum(onehot_table, axis=1) - 1) * onehot_table, axis=2)
    head_ids = jnp.arange(heads_here, dtype=jnp.int32)[:, None]
    slots = ((routing * heads_here + head_ids) * per_source + within).reshape(-1)
    total = clusters * heads_here * per_source
    outgoing = jnp.zeros((total, 3 * HD), jnp.float32).at[slots].set(payload.reshape(-1, 3 * HD))
    outgoing = outgoing.reshape(ctx_count, CL_DEV, heads_here, per_source, 3 * HD)
    marks = jnp.zeros((total,), jnp.float32).at[slots].set(1.0)
    marks = marks.reshape(ctx_count, CL_DEV, heads_here, per_source)
    rows_in = lax.all_to_all(outgoing, "ctx", split_axis=0, concat_axis=0, tiled=True)
    marks_in = lax.all_to_all(marks, "ctx", split_axis=0, concat_axis=0, tiled=True)
    owned = rows_in.shape[1]
    senders = rows_in.shape[0]
    packed = rows_in.transpose(1, 2, 0, 3, 4).reshape(
        owned * heads_here, senders * per_source, 3 * HD
    )
    validity = marks_in.transpose(1, 2, 0, 3).reshape(owned * heads_here, senders * per_source)
    gradients = cluster_gradients(packed, validity)
    replies = gradients.reshape(owned, heads_here, senders, per_source, 2 * HD).transpose(
        2, 0, 1, 3, 4
    )
    returned = lax.all_to_all(replies, "ctx", split_axis=0, concat_axis=0, tiled=True)
    picked = returned.reshape(total, 2 * HD)[slots].reshape(heads_here, length, 2 * HD)
    grad_qk = picked[:, :, :HD].transpose(1, 0, 2).reshape(length, width)
    grad_values = picked[:, :, HD:].transpose(1, 0, 2).reshape(length, width)
    combined = jnp.concatenate([grad_qk, grad_values], axis=1)
    token_terms = matmul_nt(combined, full)
    weight_terms = matmul_tn(inputs, combined)
    grad_tokens, grad_qk_weight, grad_value_weight = scatter_sums(token_terms, weight_terms)
    return (grad_tokens[None], grad_qk_weight, grad_value_weight)


def solution(mesh):
    in_specs = (
        P("rep", "ctx", None),
        P(("rep", "ctx"), "tp"),
        P(("rep", "ctx"), "tp"),
        P("rep", "ctx", "tp"),
        P("tp", "rep", "ctx", None),
    )
    out_specs = (P("rep", "ctx", "tp"), P(("rep", "ctx"), "tp"), P(("rep", "ctx"), "tp"))
    return jax.shard_map(
        per_device, mesh=mesh, in_specs=in_specs, out_specs=out_specs, check_vma=False
    )
```

```python
import jax
import jax.numpy as jnp
from jax import lax
from jax.experimental import pallas as pl
from jax.experimental.pallas import tpu as pltpu
from jax.sharding import PartitionSpec as P

HD = 128
CL_DEV = 8
NY = 4
NZ = 8
ROWS = 32
HALF = 16
MESH = pl.DeviceIdType.MESH

masked_score = -1e30
ROOM = 64


def position():
    ctx = lax.axis_index("ctx")
    return lax.axis_index("rep"), lax.div(ctx, NZ), lax.rem(ctx, NZ)


def greet(partners):
    barrier = pltpu.get_barrier_semaphore()
    for partner in partners:
        pl.semaphore_signal(barrier, inc=1, device_id=partner, device_id_type=MESH)
    pl.semaphore_wait(barrier, len(partners))


class Copies:
    def __init__(self, send_sem, recv_sem):
        self.send_sem, self.recv_sem = send_sem, recv_sem
        self.all = []

    def start(self, source, target, device):
        index = len(self.all)
        copy = pltpu.make_async_remote_copy(
            src_ref=source,
            dst_ref=target,
            send_sem=self.send_sem.at[index],
            recv_sem=self.recv_sem.at[index],
            device_id=device,
            device_id_type=MESH,
        )
        copy.start()
        self.all.append(copy)
        return copy

    def finish(self):
        for copy in self.all:
            copy.wait_send()


GATHER_COPIES = 3 + 7 + 7 + 3 + 8 + 4


def gather_kernel(qk_ref, value_ref, out_ref, local_sem, send_sem, recv_sem):
    rep, y, z = position()
    width = qk_ref.shape[1]

    def along_y(step):
        return {"ctx": lax.rem(y + step, NY) * NZ + z}

    def along_z(step):
        return {"ctx": y * NZ + lax.rem(z + step, NZ)}

    def plane(step):
        return out_ref.at[rep, :, lax.rem(z + step, NZ), pl.ds(0, HALF), :]

    def piece(step):
        return out_ref.at[rep, y, lax.rem(z + step, NZ), pl.ds(HALF, HALF), :]

    def line(step):
        return out_ref.at[rep, lax.rem(y + step, NY), :, pl.ds(HALF, HALF), :]

    right, left, other = along_z(1), along_z(NZ - 1), {"rep": 1 - rep}
    greet([along_y(1), along_y(2), along_y(3), right, left, other])
    copies = Copies(send_sem, recv_sem)
    mine = out_ref.at[rep, y, z]
    first = pltpu.make_async_copy(qk_ref, mine.at[:, pl.ds(0, width)], local_sem.at[0])
    second = pltpu.make_async_copy(value_ref, mine.at[:, pl.ds(width, width)], local_sem.at[1])
    first.start()
    second.start()
    first.wait()
    second.wait()

    own = out_ref.at[rep, y, z, pl.ds(0, HALF), :]
    shared = [copies.start(own, own, along_y(step)) for step in (1, 3, 2)]
    pieces = [(copies.start(piece(0), piece(0), right), copies.start(piece(0), piece(0), left))]
    for copy in shared:
        copy.wait_recv()
    planes = [(copies.start(plane(0), plane(0), right), copies.start(plane(0), plane(0), left))]
    across = [copies.start(plane(0), plane(0), other)]
    for step in range(4):
        rightward, leftward = pieces[step]
        rightward.wait_recv()
        if leftward is not None:
            leftward.wait_recv()
        if step < 3:
            after, before = piece(NZ - 1 - step), piece(1 + step)
            pieces.append((
                copies.start(after, after, right),
                copies.start(before, before, left) if step < 2 else None,
            ))
    lines = [copies.start(line(0), line(0), along_y(step)) for step in (1, 3, 2)]
    across.append(copies.start(line(0), line(0), other))
    for step in range(4):
        rightward, leftward = planes[step]
        after, before = plane(NZ - 1 - step), plane(1 + step)
        rightward.wait_recv()
        if step < 3:
            going = copies.start(after, after, right)
        across.append(copies.start(after, after, other))
        if leftward is not None:
            leftward.wait_recv()
            coming = copies.start(before, before, left) if step < 2 else None
            across.append(copies.start(before, before, other))
        if step < 3:
            planes.append((going, coming if step < 2 else None))
    for copy, step in zip(lines, (3, 1, 2)):
        copy.wait_recv()
        across.append(copies.start(line(step), line(step), other))
    for copy in across:
        copy.wait_recv()
    copies.finish()
    assert len(copies.all) == GATHER_COPIES


def gather_weights(qk_weight, value_weight):
    width = qk_weight.shape[1]
    return pl.pallas_call(
        gather_kernel,
        out_shape=jax.ShapeDtypeStruct((2, NY, NZ, ROWS, 2 * width), jnp.float32),
        in_specs=[pl.BlockSpec(memory_space=pl.ANY)] * 2,
        out_specs=pl.BlockSpec(memory_space=pl.ANY),
        scratch_shapes=[
            pltpu.SemaphoreType.DMA((2,)),
            pltpu.SemaphoreType.DMA((GATHER_COPIES,)),
            pltpu.SemaphoreType.DMA((GATHER_COPIES,)),
        ],
        compiler_params=pltpu.CompilerParams(collective_id=0, has_side_effects=True),
        name="gather_weights",
    )(qk_weight, value_weight)


SCATTER_COPIES = 3 + 12 + 7 + 3 + 7 + 3


def scatter_kernel(
    terms_ref, sums_ref, tokens_out, qk_out, value_out,
    column_in, cross_in, ring_a, ring_b, line_in, plane_in,
    local_sem, send_sem, recv_sem,
):
    rep, y, z = position()
    x = lax.axis_index("tp")
    width = qk_out.shape[1]

    def along_y(step):
        return {"ctx": lax.rem(y + step, NY) * NZ + z}

    def along_z(step):
        return {"ctx": y * NZ + lax.rem(z + step, NZ)}

    def along_x(step):
        return {"tp": lax.rem(x + step, 4)}

    def columns(step):
        start = pl.multiple_of(lax.rem(x + step, 4) * width, width)
        return terms_ref.at[:, pl.ds(start, width)]

    def plane(step):
        return cross_in.at[:, lax.rem(z + step, NZ), pl.ds(0, HALF), :]

    def line(step):
        return cross_in.at[lax.rem(y + step, NY), :, pl.ds(HALF, HALF), :]

    def piece(step):
        return cross_in.at[y, lax.rem(z + step, NZ), pl.ds(HALF, HALF), :]

    right, left, other = along_z(1), along_z(NZ - 1), {"rep": 1 - rep}
    greet(
        [along_y(1), along_y(2), along_y(3), right, left, other]
        + [along_x(1), along_x(2), along_x(3)]
    )
    copies = Copies(send_sem, recv_sem)
    sideways = [
        copies.start(columns(step), column_in.at[step - 1], along_x(step)) for step in (1, 3, 2)
    ]
    own_columns = pltpu.make_async_copy(columns(0), tokens_out, local_sem)
    own_columns.start()

    cross = {}
    for kind, step in (
        ("a", 4), ("a", 5), ("b", 1), ("b", 3), ("b", 2), ("a", 3),
        ("a", 6), ("a", 2), ("a", 7), ("b", 0), ("a", 1), ("a", 0),
    ):
        if kind == "a":
            there = lax.rem(z + step, NZ)
            source = sums_ref.at[1 - rep, :, there, pl.ds(0, HALF), :]
            cross[kind, step] = copies.start(source, plane(step), other)
        else:
            there = lax.rem(y + step, NY)
            source = sums_ref.at[1 - rep, there, :, pl.ds(HALF, HALF), :]
            cross[kind, step] = copies.start(source, line(step), other)

    def add_plane(step):
        cross["a", step].wait_recv()
        there = lax.rem(z + step, NZ)
        cross_in[:, there, pl.ds(0, HALF), :] += sums_ref[rep, :, there, pl.ds(0, HALF), :]

    def add_line(step):
        cross["b", step].wait_recv()
        there = lax.rem(y + step, NY)
        cross_in[there, :, pl.ds(HALF, HALF), :] += sums_ref[
            rep, there, :, pl.ds(HALF, HALF), :
        ]

    add_plane(4)
    right_a = copies.start(plane(4), ring_a.at[0], right)
    add_plane(5)
    left_a = copies.start(plane(5), ring_a.at[4], left)
    lines = []
    for step in (1, 3, 2):
        add_line(step)
        lines.append(copies.start(line(step), line_in.at[step - 1], along_y(step)))

    def pass_a(turn):
        nonlocal right_a, left_a
        add_plane(4 - turn)
        right_a.wait_recv()
        ring_a[turn - 1] += cross_in[:, lax.rem(z + 4 - turn, NZ), pl.ds(0, HALF), :]
        right_a = copies.start(ring_a.at[turn - 1], ring_a.at[turn], right)
        if turn < 3:
            add_plane(5 + turn)
            left_a.wait_recv()
            ring_a[3 + turn] += cross_in[:, lax.rem(z + 5 + turn, NZ), pl.ds(0, HALF), :]
            left_a = copies.start(ring_a.at[3 + turn], ring_a.at[4 + turn], left)

    pass_a(1)
    add_line(0)
    pass_a(2)
    for copy in lines:
        copy.wait_recv()
    cross_in[y, :, pl.ds(HALF, HALF), :] += line_in[0] + line_in[1] + line_in[2]
    right_b = copies.start(piece(4), ring_b.at[0], right)
    left_b = copies.start(piece(5), ring_b.at[4], left)
    pass_a(3)

    def pass_b(turn):
        nonlocal right_b, left_b
        right_b.wait_recv()
        ring_b[turn - 1] += cross_in[y, lax.rem(z + 4 - turn, NZ), pl.ds(HALF, HALF), :]
        right_b = copies.start(ring_b.at[turn - 1], ring_b.at[turn], right)
        if turn < 3:
            left_b.wait_recv()
            ring_b[3 + turn] += cross_in[y, lax.rem(z + 5 + turn, NZ), pl.ds(HALF, HALF), :]
            left_b = copies.start(ring_b.at[3 + turn], ring_b.at[4 + turn], left)

    pass_b(1)
    pass_b(2)
    add_plane(0)
    right_a.wait_recv()
    left_a.wait_recv()
    cross_in[:, z, pl.ds(0, HALF), :] += ring_a[3] + ring_a[6]
    planes = [
        copies.start(
            cross_in.at[lax.rem(y + step, NY), z, pl.ds(0, HALF), :],
            plane_in.at[step - 1],
            along_y(step),
        )
        for step in (1, 3, 2)
    ]
    pass_b(3)
    right_b.wait_recv()
    left_b.wait_recv()
    lower = cross_in[y, z, pl.ds(HALF, HALF), :] + ring_b[3] + ring_b[6]
    qk_out[pl.ds(HALF, HALF), :] = lower[:, :width]
    value_out[pl.ds(HALF, HALF), :] = lower[:, width:]
    for copy in planes:
        copy.wait_recv()
    upper = cross_in[y, z, pl.ds(0, HALF), :] + plane_in[0] + plane_in[1] + plane_in[2]
    qk_out[pl.ds(0, HALF), :] = upper[:, :width]
    value_out[pl.ds(0, HALF), :] = upper[:, width:]
    own_columns.wait()
    for copy in sideways:
        copy.wait_recv()

    @pl.loop(0, tokens_out.shape[0] // 8)
    def _(block):
        here = pl.ds(pl.multiple_of(block * 8, 8), 8)
        tokens_out[here, :] += column_in[0, here, :] + column_in[1, here, :] + column_in[2, here, :]

    copies.finish()
    assert len(copies.all) == SCATTER_COPIES


def scatter_sums(token_terms, weight_terms):
    length = token_terms.shape[0]
    both = weight_terms.shape[1]
    width = both // 2
    return pl.pallas_call(
        scatter_kernel,
        out_shape=(
            jax.ShapeDtypeStruct((length, width), f32),
            jax.ShapeDtypeStruct((ROWS, width), f32),
            jax.ShapeDtypeStruct((ROWS, width), f32),
        ),
        in_specs=[pl.BlockSpec(memory_space=pl.ANY), pl.BlockSpec(memory_space=pltpu.VMEM)],
        out_specs=(pl.BlockSpec(memory_space=pltpu.VMEM),) * 3,
        scratch_shapes=[
            pltpu.VMEM((3, length, width), f32),
            pltpu.VMEM((NY, NZ, ROWS, both), f32),
            pltpu.VMEM((7, NY, HALF, both), f32),
            pltpu.VMEM((7, HALF, both), f32),
            pltpu.VMEM((3, NZ, HALF, both), f32),
            pltpu.VMEM((3, HALF, both), f32),
            pltpu.SemaphoreType.DMA,
            pltpu.SemaphoreType.DMA((SCATTER_COPIES,)),
            pltpu.SemaphoreType.DMA((SCATTER_COPIES,)),
        ],
        compiler_params=pltpu.CompilerParams(
            collective_id=1, has_side_effects=True, vmem_limit_bytes=48 * 2**20
        ),
        name="scatter_sums",
    )(token_terms, weight_terms.reshape(2, NY, NZ, ROWS, both))


LANES = 128
GROUP = 8
SLOTS = 96
TALL = 768
MIXERS = (1, 77, 181, 111)
f32, bf16 = jnp.float32, jnp.bfloat16
NN = (((1,), (0,)), ((), ()))
NT = (((1,), (1,)), ((), ()))
TN = (((0,), (0,)), ((), ()))
BIG = 48 * 2**20


def dot(left, right, dims=NN):
    return lax.dot_general(left, right, dims, preferred_element_type=f32)


def halves(matrix):
    upper = matrix.astype(bf16)
    return upper, (matrix - upper.astype(f32)).astype(bf16)


def dot3(left, right, dims=NN):
    a, b = left
    c, d = right
    first = jnp.concatenate([a, b, a], axis=dims[0][0][0])
    second = jnp.concatenate([c, c, d], axis=dims[0][1][0])
    return dot(first, second, dims)


def pack_kernel(tokens_ref, full_ref, grad_ref, slots_ref, ids_ref, rows_ref, marks_ref, acc, pay):
    step = pl.program_id(0)
    width = grad_ref.shape[1]
    length = grad_ref.shape[0]
    rows = rows_ref.shape[0]

    @pl.when(step == 0)
    def _():
        acc[...] = jnp.zeros_like(acc)

    @pl.when(step < 8)
    def _():
        acc[...] += dot3(halves(tokens_ref[...]), halves(full_ref[...]))

    @pl.when(step == 7)
    def _():
        for head in range(width // HD):
            here = pl.ds(head * length, length)
            for part, source in enumerate((
                acc[:, head * HD : (head + 1) * HD],
                acc[:, width + head * HD : width + (head + 1) * HD],
                grad_ref[:, head * HD : (head + 1) * HD],
            )):
                upper, lower = halves(source)
                pay[here, part * HD : (part + 1) * HD] = upper
                pay[here, (3 + part) * HD : (4 + part) * HD] = lower

    @pl.when(step >= 8)
    def _():
        place = lax.broadcasted_iota(jnp.int32, (rows, slots_ref.shape[1]), 0) + (step - 8) * rows
        chosen = (place == slots_ref[...]).astype(f32).astype(bf16)
        both = dot(chosen, pay[...])
        rows_ref[...] = both[:, : 3 * HD] + both[:, 3 * HD :]
        marks_ref[0] = dot(ids_ref[...].astype(bf16), chosen, NT)


def pack_rows(inputs, full, upstream, slots, ids, room):
    length, depth = inputs.shape
    width = upstream.shape[1]
    total = slots.shape[1]
    return pl.pallas_call(
        pack_kernel,
        grid=(16,),
        out_shape=(
            jax.ShapeDtypeStruct((32 * room, 3 * HD), f32),
            jax.ShapeDtypeStruct((8, 8, 4 * room), f32),
        ),
        in_specs=[
            pl.BlockSpec((length, depth // 8), lambda i: (0, jnp.minimum(i, 7))),
            pl.BlockSpec((depth // 8, 2 * width), lambda i: (jnp.minimum(i, 7), 0)),
            pl.BlockSpec((length, width), lambda i: (0, 0)),
            pl.BlockSpec((1, total), lambda i: (0, 0)),
            pl.BlockSpec((8, total), lambda i: (0, 0)),
        ],
        out_specs=(
            pl.BlockSpec((4 * room, 3 * HD), lambda i: (jnp.maximum(i - 8, 0), 0)),
            pl.BlockSpec((1, 8, 4 * room), lambda i: (jnp.maximum(i - 8, 0), 0, 0)),
        ),
        scratch_shapes=[pltpu.VMEM((length, 2 * width), f32), pltpu.VMEM((total, 6 * HD), bf16)],
        compiler_params=pltpu.CompilerParams(vmem_limit_bytes=BIG),
        name="project_and_pack",
    )(inputs, full, upstream, slots, ids)


def attend_kernel(marks_ref, rows_ref, replies_ref, spread, seats, valid, answer):
    groups = marks_ref.shape[0]
    wide = marks_ref.shape[2]
    owned = spread.shape[1]
    seat = spread.shape[2]
    size = groups * seat

    @pl.loop(0, groups)
    def _(group):
        here = pl.ds(pl.multiple_of(group * wide, wide), wide)
        place = lax.broadcasted_iota(jnp.int32, (TALL, wide), 0)
        chosen = (place == marks_ref[group]).astype(f32).astype(bf16)
        seats[group] = chosen
        upper, lower = halves(rows_ref[here, :])
        moved = dot(chosen, jnp.concatenate([upper, lower, jnp.ones((wide, LANES), bf16)], axis=1))
        spread[group] = (moved[:, : 3 * HD] + moved[:, 3 * HD : 6 * HD]).reshape(owned, seat, 3 * HD)
        valid[group] = moved[:, 6 * HD :].reshape(owned, seat, LANES)

    @pl.loop(0, owned // 4)
    def _(block):
        for lane in range(4):
            index = block * 4 + lane
            rows = spread[:, index].reshape(size, 3 * HD)
            present = valid[:, index].reshape(size, LANES)[:, :size] > 0.5
            qk = halves(rows[:, :HD])
            value = halves(rows[:, HD : 2 * HD])
            upstream = halves(rows[:, 2 * HD :])
            scores = jnp.where(present, dot3(qk, qk, NT) / HD, masked_score)
            weights = jnp.exp(scores - jnp.max(scores, axis=0, keepdims=True))
            weights = weights / jnp.sum(weights, axis=0, keepdims=True)
            slopes = dot3(value, upstream, NT)
            middle = jnp.sum(weights * slopes, axis=0, keepdims=True)
            slopes = weights * (slopes - middle)
            grad_qk = dot3(halves(slopes + slopes.T), qk) / HD
            grad_value = dot3(halves(weights), upstream)
            answer[:, index] = jnp.concatenate([grad_qk, grad_value], axis=1).reshape(
                groups, seat, 2 * HD
            )

    @pl.loop(0, groups)
    def _(group):
        here = pl.ds(pl.multiple_of(group * wide, wide), wide)
        upper, lower = halves(answer[group].reshape(TALL, 2 * HD))
        moved = dot(seats[group], jnp.concatenate([upper, lower], axis=1), TN)
        replies_ref[here, :] = moved[:, : 2 * HD] + moved[:, 2 * HD :]


def attend(rows, marks, room):
    groups = 32 // GROUP
    owned = TALL // (3 * GROUP)
    seat = 3 * GROUP
    return pl.pallas_call(
        attend_kernel,
        out_shape=jax.ShapeDtypeStruct((32 * room, 2 * HD), f32),
        in_specs=[pl.BlockSpec(memory_space=pltpu.VMEM)] * 2,
        out_specs=pl.BlockSpec(memory_space=pltpu.VMEM),
        scratch_shapes=[
            pltpu.VMEM((groups, owned, seat, 3 * HD), f32),
            pltpu.VMEM((groups, TALL, GROUP * room), bf16),
            pltpu.VMEM((groups, owned, seat, LANES), f32),
            pltpu.VMEM((groups, owned, seat, 2 * HD), f32),
        ],
        compiler_params=pltpu.CompilerParams(vmem_limit_bytes=BIG),
        name="attend",
    )(marks, rows)


def grads_kernel(returned_ref, slots_ref, tokens_ref, full_ref, terms_ref, sums_ref, high, low):
    length = tokens_ref.shape[0]
    width = high.shape[1] // 2
    total = returned_ref.shape[0]

    @pl.when(pl.program_id(0) == 0)
    def _():
        upper, lower = halves(returned_ref[...])
        source = jnp.concatenate([upper, lower], axis=1)
        for head in range(width // HD):
            place = lax.broadcasted_iota(jnp.int32, (length, total), 1)
            chosen = (place == slots_ref[:, head : head + 1]).astype(f32).astype(bf16)
            both = dot(chosen, source)
            upper, lower = halves(both[:, : 2 * HD] + both[:, 2 * HD :])
            for part in range(2):
                there = pl.ds(part * width + head * HD, HD)
                high[:, there] = upper[:, part * HD : (part + 1) * HD]
                low[:, there] = lower[:, part * HD : (part + 1) * HD]

    combined = high[...], low[...]
    terms_ref[...] = dot3(combined, halves(full_ref[...]), NT)
    sums_ref[...] = dot3(halves(tokens_ref[...]), combined, TN)


def local_grads(returned, slots, inputs, full):
    length, depth = inputs.shape
    both = full.shape[1]
    total = returned.shape[0]
    return pl.pallas_call(
        grads_kernel,
        grid=(8,),
        out_shape=(
            jax.ShapeDtypeStruct((length, depth), f32),
            jax.ShapeDtypeStruct((depth, both), f32),
        ),
        in_specs=[
            pl.BlockSpec((total, 2 * HD), lambda i: (0, 0)),
            pl.BlockSpec(slots.shape, lambda i: (0, 0)),
            pl.BlockSpec((length, depth // 8), lambda i: (0, i)),
            pl.BlockSpec((depth // 8, both), lambda i: (i, 0)),
        ],
        out_specs=(
            pl.BlockSpec((length, depth // 8), lambda i: (0, i)),
            pl.BlockSpec((depth // 8, both), lambda i: (i, 0)),
        ),
        scratch_shapes=[pltpu.VMEM((length, both), bf16)] * 2,
        compiler_params=pltpu.CompilerParams(vmem_limit_bytes=BIG),
        name="unpack_and_grads",
    )(returned, slots, inputs, full)


def exchange(array):
    return lax.all_to_all(array, "ctx", split_axis=0, concat_axis=0, tiled=True)


def middle_part(room, inputs, full, upstream, owner, rank, ids):
    heads_here, length = owner.shape
    slots = owner * room + rank
    rows, marks = pack_rows(
        inputs, full, upstream, slots.reshape(1, -1),
        jnp.broadcast_to((ids + 1).astype(f32).reshape(1, -1), (8, ids.size)), room,
    )
    marks = exchange(marks[:, 0, :].reshape(32, room))
    rows = exchange(rows.reshape(32, room, 3 * HD)).reshape(32 * room, 3 * HD)
    marks = marks.astype(jnp.int32) - 1
    source = lax.broadcasted_iota(jnp.int32, marks.shape, 0) % GROUP
    seats = (marks // 3) * (3 * GROUP) + source * 3 + marks % 3
    seats = jnp.where(marks < 0, -1, seats).reshape(32 // GROUP, 1, GROUP * room)
    replies = attend(rows, seats, room)
    returned = exchange(replies.reshape(32, room, 2 * HD)).reshape(32 * room, 2 * HD)
    return local_grads(returned, slots.T, inputs, full)


def per_device(tokens, qk_weight, value_weight, grad_out, assign):
    inputs = tokens[0]
    length = inputs.shape[0]
    clusters = CL_DEV * lax.axis_size("ctx")
    heads_here = qk_weight.shape[1] // HD
    width = heads_here * HD
    mixers = jnp.asarray(MIXERS, jnp.int32)[:, None]
    cluster = (assign[:, 0, :, 0] * mixers) % clusters
    owner = cluster // CL_DEV
    order = jnp.arange(length, dtype=jnp.int32)
    earlier = order[:, None] < order[None, :]
    within = jnp.sum(
        ((cluster[:, :, None] == cluster[:, None, :]) & earlier).astype(jnp.int32), axis=1
    )
    flat = owner.reshape(-1)
    order = jnp.arange(flat.size, dtype=jnp.int32)
    earlier = order[:, None] < order[None, :]
    rank = jnp.sum(((flat[:, None] == flat[None, :]) & earlier).astype(jnp.int32), axis=0)
    rank = rank.reshape(owner.shape)
    head_ids = jnp.arange(heads_here, dtype=jnp.int32)[:, None]
    ids = (head_ids * CL_DEV + cluster % CL_DEV) * 3 + within
    fullest = lax.pmax(jnp.max(rank) + 1, ("rep", "ctx", "tp"))
    full = gather_weights(qk_weight, value_weight).reshape(-1, 2 * width)
    token_terms, weight_terms = lax.cond(
        fullest <= ROOM,
        lambda *operands: middle_part(ROOM, *operands),
        lambda *operands: middle_part(SLOTS, *operands),
        inputs, full, grad_out[0], owner, rank, ids,
    )
    grad_tokens, grad_qk_weight, grad_value_weight = scatter_sums(token_terms, weight_terms)
    return (grad_tokens[None], grad_qk_weight, grad_value_weight)


def solution(mesh):
    in_specs = (
        P("rep", "ctx", None),
        P(("rep", "ctx"), "tp"),
        P(("rep", "ctx"), "tp"),
        P("rep", "ctx", "tp"),
        P("tp", "rep", "ctx", None),
    )
    out_specs = (P("rep", "ctx", "tp"), P(("rep", "ctx"), "tp"), P(("rep", "ctx"), "tp"))
    return jax.shard_map(
        per_device, mesh=mesh, in_specs=in_specs, out_specs=out_specs, check_vma=False
    )
```

```python
import jax
import jax.numpy as jnp
from jax import lax
from jax.experimental import pallas as pl
from jax.experimental.pallas import tpu as pltpu
from jax.sharding import PartitionSpec as P

HD = 128
CL_DEV = 8
NY = 4
NZ = 8
ROWS = 32
HALF = 16
MESH = pl.DeviceIdType.MESH

masked_score = -1e30
ROOM = 56
LANES = 128
GROUP = 8
SLOTS = 96
TALL = 768
f32, bf16 = jnp.float32, jnp.bfloat16
NN = (((1,), (0,)), ((), ()))
NT = (((1,), (1,)), ((), ()))
TN = (((0,), (0,)), ((), ()))
BIG = 48 * 2**20


def dot(left, right, dims=NN):
    return lax.dot_general(left, right, dims, preferred_element_type=f32)


def halves(matrix):
    upper = matrix.astype(bf16)
    return upper, (matrix - upper.astype(f32)).astype(bf16)


def dot3(left, right, dims=NN):
    a, b = left
    c, d = right
    first = jnp.concatenate([a, b, a], axis=dims[0][0][0])
    second = jnp.concatenate([c, c, d], axis=dims[0][1][0])
    return dot(first, second, dims)


def position():
    ctx = lax.axis_index("ctx")
    return lax.axis_index("rep"), lax.div(ctx, NZ), lax.rem(ctx, NZ)


def greet(partners):
    barrier = pltpu.get_barrier_semaphore()
    for partner in partners:
        pl.semaphore_signal(barrier, inc=1, device_id=partner, device_id_type=MESH)
    pl.semaphore_wait(barrier, len(partners))


class Copies:
    def __init__(self, send_sem, recv_sem):
        self.send_sem, self.recv_sem = send_sem, recv_sem
        self.all = []

    def start(self, source, target, device):
        index = len(self.all)
        copy = pltpu.make_async_remote_copy(
            src_ref=source,
            dst_ref=target,
            send_sem=self.send_sem.at[index],
            recv_sem=self.recv_sem.at[index],
            device_id=device,
            device_id_type=MESH,
        )
        copy.start()
        self.all.append(copy)
        return copy

    def finish(self):
        for copy in self.all:
            copy.wait_send()


GATHER_COPIES = 3 + 7 + 7 + 3 + 8 + 4
ROUTE_COPIES = 3 + 7 + 3 + 1
CLUSTERS = 256
OWNERS = 32
PITCH = 64


def count_rows(cluster_ref, heads):
    length = cluster_ref.shape[1]
    line = lax.broadcasted_iota(jnp.int32, (8, length), 0)
    counts = jnp.zeros((8, CLUSTERS), f32)
    for head in range(heads):
        counts += dot(one(line == head), members(cluster_ref, head), NT)
    return counts


def one(condition):
    return jnp.where(condition, 1.0, 0.0).astype(bf16)


def members(cluster_ref, head):
    length = cluster_ref.shape[1]
    label = lax.broadcasted_iota(jnp.int32, (CLUSTERS, length), 0)
    return one(label == cluster_ref[head : head + 1, :])


def deal_order(counts):
    lane = lax.broadcasted_iota(jnp.int32, counts.shape, 1)
    return counts * CLUSTERS + (CLUSTERS - 1 - lane).astype(f32)


def route_head(cluster_ref, head, keys, tall_keys, earlier, base):
    larger = jnp.where(tall_keys[:, head : head + 1] > keys[head : head + 1, :], 1.0, 0.0)
    place = jnp.sum(larger, axis=0, keepdims=True).astype(jnp.int32)
    turn = place // OWNERS
    seat = place % OWNERS
    seat = jnp.where(turn % 2 == 0, seat, OWNERS - 1 - seat)
    seat = (seat + 8 * head) % OWNERS
    line = lax.broadcasted_iota(jnp.int32, (8, CLUSTERS), 0)
    table = jnp.where(line == 0, seat, jnp.where(line == 1, turn, 0)).astype(f32).astype(bf16)
    chosen = members(cluster_ref, head)
    looked = dot(table, chosen).astype(jnp.int32)
    owner, turn = looked[0:1, :], looked[1:2, :]
    within = jnp.sum(chosen.astype(f32) * dot(chosen, earlier), axis=0, keepdims=True)
    label = lax.broadcasted_iota(jnp.int32, (OWNERS, owner.shape[1]), 0)
    owned = one(label == owner)
    many = owned.astype(f32)
    rank = jnp.sum(many * (dot(owned, earlier) + base), axis=0, keepdims=True)
    base = base + jnp.sum(many, axis=1, keepdims=True)
    ids = (head * CL_DEV + turn) * 3 + within.astype(jnp.int32)
    return owner, rank.astype(jnp.int32), ids, base


def gather_kernel(
    qk_ref, value_ref, cluster_ref, grad_ref,
    out_ref, early_ref, slots_ref,
    counts_y, counts_z, most, ids_row, slots_row, pay, early_out,
    local_sem, send_sem, recv_sem, route_send, route_recv, early_send, early_recv,
):
    rep, y, z = position()
    me = lax.axis_index("ctx")
    x = lax.axis_index("tp")
    width = qk_ref.shape[1]
    heads = width // HD
    length = cluster_ref.shape[1]

    def along_y(step):
        return {"ctx": lax.rem(y + step, NY) * NZ + z}

    def along_z(step):
        return {"ctx": y * NZ + lax.rem(z + step, NZ)}

    def along_x(step):
        return {"tp": lax.rem(x + step, 4)}

    def around(step):
        return {"ctx": lax.rem(me + step, OWNERS)}

    def plane(step):
        return out_ref.at[rep, :, lax.rem(z + step, NZ), pl.ds(0, HALF), :]

    def piece(step):
        return out_ref.at[rep, y, lax.rem(z + step, NZ), pl.ds(HALF, HALF), :]

    def line(step):
        return out_ref.at[rep, lax.rem(y + step, NY), :, pl.ds(HALF, HALF), :]

    right, left, other = along_z(1), along_z(NZ - 1), {"rep": 1 - rep}
    mine = out_ref.at[rep, y, z]
    first = pltpu.make_async_copy(qk_ref, mine.at[:, pl.ds(0, width)], local_sem.at[0])
    second = pltpu.make_async_copy(value_ref, mine.at[:, pl.ds(width, width)], local_sem.at[1])
    first.start()
    second.start()
    barrier = pltpu.get_barrier_semaphore()

    @pl.loop(1, OWNERS)
    def _(step):
        pl.semaphore_signal(barrier, inc=1, device_id=around(step), device_id_type=MESH)

    for partner in (other, along_x(1), along_x(2), along_x(3)):
        pl.semaphore_signal(barrier, inc=1, device_id=partner, device_id_type=MESH)
    counts_y[0] = count_rows(cluster_ref, heads)
    pl.semaphore_wait(barrier, OWNERS - 1 + 4)

    routes = Copies(route_send, route_recv)
    counted = [
        routes.start(counts_y.at[0], counts_y.at[step], along_y(step)) for step in (1, 2, 3)
    ]
    first.wait()
    second.wait()
    copies = Copies(send_sem, recv_sem)
    own = out_ref.at[rep, y, z, pl.ds(0, HALF), :]
    shared = [copies.start(own, own, along_y(step)) for step in (1, 3, 2)]
    pieces = [(copies.start(piece(0), piece(0), right), copies.start(piece(0), piece(0), left))]

    for head in range(heads):
        upper, lower = halves(grad_ref[:, head * HD : (head + 1) * HD])
        pay[pl.ds(head * length, length), :HD] = upper
        pay[pl.ds(head * length, length), HD:] = lower

    for copy in counted:
        copy.wait_recv()
    counts_z[0] = counts_y[0] + counts_y[1] + counts_y[2] + counts_y[3]
    counted = [
        routes.start(counts_z.at[0], counts_z.at[step], along_z(step)) for step in range(1, NZ)
    ]
    for copy in shared:
        copy.wait_recv()
    planes = [(copies.start(plane(0), plane(0), right), copies.start(plane(0), plane(0), left))]
    across = [copies.start(plane(0), plane(0), other)]

    def turn_pieces(step):
        rightward, leftward = pieces[step]
        rightward.wait_recv()
        if leftward is not None:
            leftward.wait_recv()
        if step < 3:
            after, before = piece(NZ - 1 - step), piece(1 + step)
            pieces.append((
                copies.start(after, after, right),
                copies.start(before, before, left) if step < 2 else None,
            ))

    def turn_planes(step):
        rightward, leftward = planes[step]
        after, before = plane(NZ - 1 - step), plane(1 + step)
        rightward.wait_recv()
        if step < 3:
            going = copies.start(after, after, right)
        if leftward is not None:
            leftward.wait_recv()
            coming = copies.start(before, before, left) if step < 2 else None
        if step < 3:
            planes.append((going, coming if step < 2 else None))
        across.append(copies.start(after, after, other))
        if leftward is not None:
            across.append(copies.start(before, before, other))

    turn_pieces(0)
    for copy in counted:
        copy.wait_recv()
    total = counts_z[0]
    for step in range(1, NZ):
        total += counts_z[step]
    keys = deal_order(total)
    tall_keys = jnp.concatenate([keys] + [jnp.zeros_like(keys)] * 15, axis=0).T
    earlier = one(
        lax.broadcasted_iota(jnp.int32, (length, length), 0)
        < lax.broadcasted_iota(jnp.int32, (length, length), 1)
    )
    base = jnp.zeros((OWNERS, 1), f32)
    highest = jnp.zeros((1, 1), f32)
    slots_ref[...] = jnp.full(slots_ref.shape, -1, jnp.int32)
    for head in range(heads):
        owner, rank, ids, base = route_head(cluster_ref, head, keys, tall_keys, earlier, base)
        highest = jnp.maximum(highest, jnp.max(rank.astype(f32), axis=1, keepdims=True) + 1)
        slots_ref[head : head + 1, :] = jnp.where(rank < ROOM, owner * ROOM + rank, -1)
        here = pl.ds(head * length, length)
        slots_row[:, here] = jnp.where(rank < ROOM, owner * PITCH + rank, -1)
        ids_row[:, here] = jnp.broadcast_to((ids + 1).astype(f32).astype(bf16), (8, length))
        if head < 3:
            turn_pieces(head + 1)
    most[0] = jnp.broadcast_to(highest, (8, LANES))
    fullest = [routes.start(most.at[0], most.at[step], along_x(step)) for step in (1, 2, 3)]
    lines = [copies.start(line(0), line(0), along_y(step)) for step in (1, 3, 2)]
    across.append(copies.start(line(0), line(0), other))
    turn_planes(0)
    for copy in fullest:
        copy.wait_recv()
    most[4] = jnp.maximum(jnp.maximum(most[0], most[1]), jnp.maximum(most[2], most[3]))
    fullest = routes.start(most.at[4], most.at[5], other)

    @pl.loop(0, OWNERS // 4)
    def _(block):
        rows = 4 * PITCH
        place = lax.broadcasted_iota(jnp.int32, (rows, heads * length), 0) + block * rows
        chosen = one(place == slots_row[...])
        both = dot(chosen, pay[...])
        both = both[:, :HD] + both[:, HD:]
        marks = dot(ids_row[...], chosen, NT)
        for lane in range(4):
            early_out[block * 4 + lane] = both[lane * PITCH : (lane + 1) * PITCH]
            early_out[block * 4 + lane, pl.ds(ROOM, 8), pl.ds(0, PITCH)] = marks[
                :, lane * PITCH : (lane + 1) * PITCH
            ]

    fullest.wait_recv()
    overall = jnp.maximum(most[4], most[5])[:, :PITCH]

    @pl.loop(0, OWNERS)
    def _(block):
        early_out[block, pl.ds(ROOM, 8), pl.ds(PITCH, PITCH)] = overall

    def early(step):
        there = lax.rem(me + step, OWNERS)
        return pltpu.make_async_remote_copy(
            src_ref=early_out.at[there],
            dst_ref=early_ref.at[me],
            send_sem=early_send.at[step],
            recv_sem=early_recv.at[step],
            device_id={"ctx": there},
            device_id_type=MESH,
        )

    @pl.loop(1, OWNERS)
    def _(step):
        early(step).start()

    stay = pltpu.make_async_copy(early_out.at[me], early_ref.at[me], local_sem.at[0])
    stay.start()
    for step in range(1, 4):
        turn_planes(step)
    for copy, step in zip(lines, (3, 1, 2)):
        copy.wait_recv()
        across.append(copies.start(line(step), line(step), other))
    for copy in across:
        copy.wait_recv()
    copies.finish()
    routes.finish()
    stay.wait()

    @pl.loop(1, OWNERS)
    def _(step):
        early(step).wait()

    assert len(copies.all) == GATHER_COPIES and len(routes.all) == ROUTE_COPIES


def gather_weights(qk_weight, value_weight, clusters, upstream):
    width = qk_weight.shape[1]
    length = clusters.shape[1]
    rows = width // HD * length
    return pl.pallas_call(
        gather_kernel,
        out_shape=(
            jax.ShapeDtypeStruct((2, NY, NZ, ROWS, 2 * width), f32),
            jax.ShapeDtypeStruct((OWNERS, PITCH, HD), f32),
            jax.ShapeDtypeStruct((8, length), jnp.int32),
        ),
        in_specs=[pl.BlockSpec(memory_space=pl.ANY)] * 2
        + [pl.BlockSpec(memory_space=pltpu.VMEM)] * 2,
        out_specs=(
            pl.BlockSpec(memory_space=pl.ANY),
            pl.BlockSpec(memory_space=pl.ANY),
            pl.BlockSpec(memory_space=pltpu.VMEM),
        ),
        scratch_shapes=[
            pltpu.VMEM((NY, 8, CLUSTERS), f32),
            pltpu.VMEM((NZ, 8, CLUSTERS), f32),
            pltpu.VMEM((6, 8, LANES), f32),
            pltpu.VMEM((8, rows), bf16),
            pltpu.VMEM((1, rows), jnp.int32),
            pltpu.VMEM((rows, 2 * HD), bf16),
            pltpu.VMEM((OWNERS, PITCH, HD), f32),
            pltpu.SemaphoreType.DMA((2,)),
            pltpu.SemaphoreType.DMA((GATHER_COPIES,)),
            pltpu.SemaphoreType.DMA((GATHER_COPIES,)),
            pltpu.SemaphoreType.DMA((ROUTE_COPIES,)),
            pltpu.SemaphoreType.DMA((ROUTE_COPIES,)),
            pltpu.SemaphoreType.DMA((OWNERS,)),
            pltpu.SemaphoreType.DMA((OWNERS,)),
        ],
        compiler_params=pltpu.CompilerParams(
            collective_id=0, has_side_effects=True, vmem_limit_bytes=BIG
        ),
        name="gather_weights",
    )(qk_weight, value_weight, clusters, upstream)


SCATTER_COPIES = 3 + 12 + 7 + 3 + 7 + 3


def scatter_kernel(
    terms_ref, sums_ref, tokens_out, qk_out, value_out,
    column_in, cross_in, ring_a, ring_b, line_in, plane_in,
    local_sem, send_sem, recv_sem,
):
    rep, y, z = position()
    x = lax.axis_index("tp")
    width = qk_out.shape[1]

    def along_y(step):
        return {"ctx": lax.rem(y + step, NY) * NZ + z}

    def along_z(step):
        return {"ctx": y * NZ + lax.rem(z + step, NZ)}

    def along_x(step):
        return {"tp": lax.rem(x + step, 4)}

    def columns(step):
        start = pl.multiple_of(lax.rem(x + step, 4) * width, width)
        return terms_ref.at[:, pl.ds(start, width)]

    def plane(step):
        return cross_in.at[:, lax.rem(z + step, NZ), pl.ds(0, HALF), :]

    def line(step):
        return cross_in.at[lax.rem(y + step, NY), :, pl.ds(HALF, HALF), :]

    def piece(step):
        return cross_in.at[y, lax.rem(z + step, NZ), pl.ds(HALF, HALF), :]

    right, left, other = along_z(1), along_z(NZ - 1), {"rep": 1 - rep}
    greet(
        [along_y(1), along_y(2), along_y(3), right, left, other]
        + [along_x(1), along_x(2), along_x(3)]
    )
    copies = Copies(send_sem, recv_sem)
    sideways = [
        copies.start(columns(step), column_in.at[step - 1], along_x(step)) for step in (1, 3, 2)
    ]
    own_columns = pltpu.make_async_copy(columns(0), tokens_out, local_sem)
    own_columns.start()

    cross = {}
    for kind, step in (
        ("a", 4), ("a", 5), ("b", 1), ("b", 3), ("b", 2), ("a", 3),
        ("a", 6), ("a", 2), ("a", 7), ("b", 0), ("a", 1), ("a", 0),
    ):
        if kind == "a":
            there = lax.rem(z + step, NZ)
            source = sums_ref.at[1 - rep, :, there, pl.ds(0, HALF), :]
            cross[kind, step] = copies.start(source, plane(step), other)
        else:
            there = lax.rem(y + step, NY)
            source = sums_ref.at[1 - rep, there, :, pl.ds(HALF, HALF), :]
            cross[kind, step] = copies.start(source, line(step), other)

    def add_plane(step):
        cross["a", step].wait_recv()
        there = lax.rem(z + step, NZ)
        cross_in[:, there, pl.ds(0, HALF), :] += sums_ref[rep, :, there, pl.ds(0, HALF), :]

    def add_line(step):
        cross["b", step].wait_recv()
        there = lax.rem(y + step, NY)
        cross_in[there, :, pl.ds(HALF, HALF), :] += sums_ref[
            rep, there, :, pl.ds(HALF, HALF), :
        ]

    add_plane(4)
    right_a = copies.start(plane(4), ring_a.at[0], right)
    add_plane(5)
    left_a = copies.start(plane(5), ring_a.at[4], left)
    lines = []
    for step in (1, 3, 2):
        add_line(step)
        lines.append(copies.start(line(step), line_in.at[step - 1], along_y(step)))

    def pass_a(turn):
        nonlocal right_a, left_a
        add_plane(4 - turn)
        right_a.wait_recv()
        ring_a[turn - 1] += cross_in[:, lax.rem(z + 4 - turn, NZ), pl.ds(0, HALF), :]
        right_a = copies.start(ring_a.at[turn - 1], ring_a.at[turn], right)
        if turn < 3:
            add_plane(5 + turn)
            left_a.wait_recv()
            ring_a[3 + turn] += cross_in[:, lax.rem(z + 5 + turn, NZ), pl.ds(0, HALF), :]
            left_a = copies.start(ring_a.at[3 + turn], ring_a.at[4 + turn], left)

    pass_a(1)
    add_line(0)
    pass_a(2)
    for copy in lines:
        copy.wait_recv()
    cross_in[y, :, pl.ds(HALF, HALF), :] += line_in[0] + line_in[1] + line_in[2]
    right_b = copies.start(piece(4), ring_b.at[0], right)
    left_b = copies.start(piece(5), ring_b.at[4], left)
    pass_a(3)

    def pass_b(turn):
        nonlocal right_b, left_b
        right_b.wait_recv()
        ring_b[turn - 1] += cross_in[y, lax.rem(z + 4 - turn, NZ), pl.ds(HALF, HALF), :]
        right_b = copies.start(ring_b.at[turn - 1], ring_b.at[turn], right)
        if turn < 3:
            left_b.wait_recv()
            ring_b[3 + turn] += cross_in[y, lax.rem(z + 5 + turn, NZ), pl.ds(HALF, HALF), :]
            left_b = copies.start(ring_b.at[3 + turn], ring_b.at[4 + turn], left)

    pass_b(1)
    pass_b(2)
    add_plane(0)
    right_a.wait_recv()
    left_a.wait_recv()
    cross_in[:, z, pl.ds(0, HALF), :] += ring_a[3] + ring_a[6]
    planes = [
        copies.start(
            cross_in.at[lax.rem(y + step, NY), z, pl.ds(0, HALF), :],
            plane_in.at[step - 1],
            along_y(step),
        )
        for step in (1, 3, 2)
    ]
    pass_b(3)
    right_b.wait_recv()
    left_b.wait_recv()
    lower = cross_in[y, z, pl.ds(HALF, HALF), :] + ring_b[3] + ring_b[6]
    qk_out[pl.ds(HALF, HALF), :] = lower[:, :width]
    value_out[pl.ds(HALF, HALF), :] = lower[:, width:]
    for copy in planes:
        copy.wait_recv()
    upper = cross_in[y, z, pl.ds(0, HALF), :] + plane_in[0] + plane_in[1] + plane_in[2]
    qk_out[pl.ds(0, HALF), :] = upper[:, :width]
    value_out[pl.ds(0, HALF), :] = upper[:, width:]
    own_columns.wait()
    for copy in sideways:
        copy.wait_recv()

    @pl.loop(0, tokens_out.shape[0] // 8)
    def _(block):
        here = pl.ds(pl.multiple_of(block * 8, 8), 8)
        tokens_out[here, :] += column_in[0, here, :] + column_in[1, here, :] + column_in[2, here, :]

    copies.finish()
    assert len(copies.all) == SCATTER_COPIES


def scatter_sums(token_terms, weight_terms):
    length = token_terms.shape[0]
    both = weight_terms.shape[1]
    width = both // 2
    return pl.pallas_call(
        scatter_kernel,
        out_shape=(
            jax.ShapeDtypeStruct((length, width), f32),
            jax.ShapeDtypeStruct((ROWS, width), f32),
            jax.ShapeDtypeStruct((ROWS, width), f32),
        ),
        in_specs=[pl.BlockSpec(memory_space=pl.ANY), pl.BlockSpec(memory_space=pltpu.VMEM)],
        out_specs=(pl.BlockSpec(memory_space=pltpu.VMEM),) * 3,
        scratch_shapes=[
            pltpu.VMEM((3, length, width), f32),
            pltpu.VMEM((NY, NZ, ROWS, both), f32),
            pltpu.VMEM((7, NY, HALF, both), f32),
            pltpu.VMEM((7, HALF, both), f32),
            pltpu.VMEM((3, NZ, HALF, both), f32),
            pltpu.VMEM((3, HALF, both), f32),
            pltpu.SemaphoreType.DMA,
            pltpu.SemaphoreType.DMA((SCATTER_COPIES,)),
            pltpu.SemaphoreType.DMA((SCATTER_COPIES,)),
        ],
        compiler_params=pltpu.CompilerParams(
            collective_id=1, has_side_effects=True, vmem_limit_bytes=48 * 2**20
        ),
        name="scatter_sums",
    )(token_terms, weight_terms.reshape(2, NY, NZ, ROWS, both))


def pack_kernel(tokens_ref, full_ref, slots_ref, rows_ref, acc, pay):
    step = pl.program_id(0)
    length, both = acc.shape
    rows = rows_ref.shape[0]

    @pl.when(step == 0)
    def _():
        acc[...] = jnp.zeros_like(acc)

    @pl.when(step < 8)
    def _():
        acc[...] += dot3(halves(tokens_ref[...]), halves(full_ref[...]))

    @pl.when(step == 7)
    def _():
        for head in range(both // (2 * HD)):
            here = pl.ds(head * length, length)
            for part in range(2):
                column = part * both // 2 + head * HD
                upper, lower = halves(acc[:, column : column + HD])
                pay[here, part * HD : (part + 1) * HD] = upper
                pay[here, (2 + part) * HD : (3 + part) * HD] = lower

    @pl.when(step >= 8)
    def _():
        place = lax.broadcasted_iota(jnp.int32, (rows, slots_ref.shape[1]), 0) + (step - 8) * rows
        moved = dot(one(place == slots_ref[...]), pay[...])
        rows_ref[...] = moved[:, : 2 * HD] + moved[:, 2 * HD :]


def pack_rows(inputs, full, slots, room):
    length, depth = inputs.shape
    both = full.shape[1]
    total = slots.shape[1]
    return pl.pallas_call(
        pack_kernel,
        grid=(16,),
        out_shape=jax.ShapeDtypeStruct((OWNERS * room, 2 * HD), f32),
        in_specs=[
            pl.BlockSpec((length, depth // 8), lambda i: (0, jnp.minimum(i, 7))),
            pl.BlockSpec((depth // 8, both), lambda i: (jnp.minimum(i, 7), 0)),
            pl.BlockSpec((1, total), lambda i: (0, 0)),
        ],
        out_specs=pl.BlockSpec((4 * room, 2 * HD), lambda i: (jnp.maximum(i - 8, 0), 0)),
        scratch_shapes=[pltpu.VMEM((length, both), f32), pltpu.VMEM((total, 4 * HD), bf16)],
        compiler_params=pltpu.CompilerParams(vmem_limit_bytes=BIG),
        name="project_and_pack",
    )(inputs, full, slots)


def attend_kernel(marks_ref, rows_ref, early_ref, replies_ref, spread, seats, valid, answer):
    groups = marks_ref.shape[0]
    wide = marks_ref.shape[2]
    owned = spread.shape[1]
    seat = spread.shape[2]
    size = groups * seat

    @pl.loop(0, groups)
    def _(group):
        here = pl.ds(pl.multiple_of(group * wide, wide), wide)
        place = lax.broadcasted_iota(jnp.int32, (TALL, wide), 0)
        chosen = one(place == marks_ref[group])
        seats[group] = chosen
        upper, lower = halves(rows_ref[here, :])
        early = early_ref[pl.ds(group * GROUP, GROUP), pl.ds(0, wide // GROUP), :]
        early_upper, early_lower = halves(early.reshape(wide, HD))
        present = jnp.ones((wide, LANES), bf16)
        moved = dot(
            chosen, jnp.concatenate([upper, early_upper, lower, early_lower, present], axis=1)
        )
        spread[group] = (moved[:, : 3 * HD] + moved[:, 3 * HD : 6 * HD]).reshape(owned, seat, 3 * HD)
        valid[group] = moved[:, 6 * HD :].reshape(owned, seat, LANES)

    @pl.loop(0, owned // 4)
    def _(block):
        for lane in range(4):
            index = block * 4 + lane
            rows = spread[:, index].reshape(size, 3 * HD)
            present = valid[:, index].reshape(size, LANES)[:, :size] > 0.5
            qk = halves(rows[:, :HD])
            value = halves(rows[:, HD : 2 * HD])
            upstream = halves(rows[:, 2 * HD :])
            scores = jnp.where(present, dot3(qk, qk, NT) / HD, masked_score)
            weights = jnp.exp(scores - jnp.max(scores, axis=0, keepdims=True))
            weights = weights / jnp.sum(weights, axis=0, keepdims=True)
            slopes = dot3(value, upstream, NT)
            middle = jnp.sum(weights * slopes, axis=0, keepdims=True)
            slopes = weights * (slopes - middle)
            grad_qk = dot3(halves(slopes + slopes.T), qk) / HD
            grad_value = dot3(halves(weights), upstream)
            answer[:, index] = jnp.concatenate([grad_qk, grad_value], axis=1).reshape(
                groups, seat, 2 * HD
            )

    @pl.loop(0, groups)
    def _(group):
        here = pl.ds(pl.multiple_of(group * wide, wide), wide)
        upper, lower = halves(answer[group].reshape(TALL, 2 * HD))
        moved = dot(seats[group], jnp.concatenate([upper, lower], axis=1), TN)
        replies_ref[here, :] = moved[:, : 2 * HD] + moved[:, 2 * HD :]


def attend(rows, early, marks, room):
    groups = OWNERS // GROUP
    owned = TALL // (3 * GROUP)
    seat = 3 * GROUP
    return pl.pallas_call(
        attend_kernel,
        out_shape=jax.ShapeDtypeStruct((OWNERS * room, 2 * HD), f32),
        in_specs=[pl.BlockSpec(memory_space=pltpu.VMEM)] * 3,
        out_specs=pl.BlockSpec(memory_space=pltpu.VMEM),
        scratch_shapes=[
            pltpu.VMEM((groups, owned, seat, 3 * HD), f32),
            pltpu.VMEM((groups, TALL, GROUP * room), bf16),
            pltpu.VMEM((groups, owned, seat, LANES), f32),
            pltpu.VMEM((groups, owned, seat, 2 * HD), f32),
        ],
        compiler_params=pltpu.CompilerParams(vmem_limit_bytes=BIG),
        name="attend",
    )(marks, rows, early)


def grads_kernel(returned_ref, slots_ref, tokens_ref, full_ref, terms_ref, sums_ref, high, low):
    length = tokens_ref.shape[0]
    width = high.shape[1] // 2
    total = returned_ref.shape[0]

    @pl.when(pl.program_id(0) == 0)
    def _():
        upper, lower = halves(returned_ref[...])
        source = jnp.concatenate([upper, lower], axis=1)
        for head in range(width // HD):
            place = lax.broadcasted_iota(jnp.int32, (length, total), 1)
            chosen = one(place == slots_ref[:, head : head + 1])
            both = dot(chosen, source)
            upper, lower = halves(both[:, : 2 * HD] + both[:, 2 * HD :])
            for part in range(2):
                there = pl.ds(part * width + head * HD, HD)
                high[:, there] = upper[:, part * HD : (part + 1) * HD]
                low[:, there] = lower[:, part * HD : (part + 1) * HD]

    combined = high[...], low[...]
    terms_ref[...] = dot3(combined, halves(full_ref[...]), NT)
    sums_ref[...] = dot3(halves(tokens_ref[...]), combined, TN)


def local_grads(returned, slots, inputs, full):
    length, depth = inputs.shape
    both = full.shape[1]
    total = returned.shape[0]
    return pl.pallas_call(
        grads_kernel,
        grid=(8,),
        out_shape=(
            jax.ShapeDtypeStruct((length, depth), f32),
            jax.ShapeDtypeStruct((depth, both), f32),
        ),
        in_specs=[
            pl.BlockSpec((total, 2 * HD), lambda i: (0, 0)),
            pl.BlockSpec(slots.shape, lambda i: (0, 0)),
            pl.BlockSpec((length, depth // 8), lambda i: (0, i)),
            pl.BlockSpec((depth // 8, both), lambda i: (i, 0)),
        ],
        out_specs=(
            pl.BlockSpec((length, depth // 8), lambda i: (0, i)),
            pl.BlockSpec((depth // 8, both), lambda i: (i, 0)),
        ),
        scratch_shapes=[pltpu.VMEM((length, both), bf16)] * 2,
        compiler_params=pltpu.CompilerParams(vmem_limit_bytes=BIG),
        name="unpack_and_grads",
    )(returned, slots, inputs, full)


def exchange(array):
    return lax.all_to_all(array, "ctx", split_axis=0, concat_axis=0, tiled=True)


def middle_part(room, inputs, full, early, marks, slots):
    rows = pack_rows(inputs, full, slots.reshape(1, -1), room)
    rows = exchange(rows.reshape(OWNERS, room, 2 * HD)).reshape(OWNERS * room, 2 * HD)
    marks = marks.astype(jnp.int32) - 1
    source = lax.broadcasted_iota(jnp.int32, marks.shape, 0) % GROUP
    seats = (marks // 3) * (3 * GROUP) + source * 3 + marks % 3
    seats = jnp.where(marks < 0, -1, seats).reshape(OWNERS // GROUP, 1, GROUP * room)
    replies = attend(rows, early, seats, room)
    returned = exchange(replies.reshape(OWNERS, room, 2 * HD)).reshape(OWNERS * room, 2 * HD)
    return local_grads(returned, slots.T, inputs, full)


def roomy_part(inputs, full, upstream, cluster):
    heads, length = cluster.shape
    order = jnp.arange(length, dtype=jnp.int32)
    earlier = order[:, None] < order[None, :]
    alike = cluster[:, :, None] == cluster[:, None, :]
    within = jnp.sum((alike & earlier).astype(jnp.int32), axis=1)
    head = jnp.arange(heads, dtype=jnp.int32)[:, None]
    ids = (head * CL_DEV + cluster % CL_DEV) * 3 + within
    slots = cluster // CL_DEV * SLOTS + ids
    marks = jnp.zeros((OWNERS * SLOTS,), f32).at[slots.reshape(-1)].set(
        (ids + 1).astype(f32).reshape(-1)
    )
    rows = upstream.reshape(length, heads, HD).transpose(1, 0, 2).reshape(-1, HD)
    early = jnp.zeros((OWNERS * SLOTS, HD), f32).at[slots.reshape(-1)].set(rows)
    early = exchange(early.reshape(OWNERS, SLOTS, HD))
    marks = exchange(marks.reshape(OWNERS, SLOTS))
    return middle_part(SLOTS, inputs, full, early, marks, slots)


def per_device(tokens, qk_weight, value_weight, grad_out, assign):
    inputs = tokens[0]
    heads_here = qk_weight.shape[1] // HD
    width = heads_here * HD
    cluster = assign[:, 0, :, 0]
    full, early, slots = gather_weights(
        qk_weight, value_weight, jnp.pad(cluster, ((0, 8 - heads_here), (0, 0))), grad_out[0]
    )
    full = full.reshape(-1, 2 * width)
    fullest = jnp.max(early[:, ROOM, PITCH])

    def snug(inputs, full, upstream, cluster, early, slots):
        marks = early[:, ROOM, :ROOM]
        return middle_part(ROOM, inputs, full, early, marks, slots[:heads_here])

    def roomy(inputs, full, upstream, cluster, early, slots):
        return roomy_part(inputs, full, upstream, cluster)

    token_terms, weight_terms = lax.cond(
        fullest <= ROOM, snug, roomy, inputs, full, grad_out[0], cluster, early, slots
    )
    grad_tokens, grad_qk_weight, grad_value_weight = scatter_sums(token_terms, weight_terms)
    return (grad_tokens[None], grad_qk_weight, grad_value_weight)


def solution(mesh):
    in_specs = (
        P("rep", "ctx", None),
        P(("rep", "ctx"), "tp"),
        P(("rep", "ctx"), "tp"),
        P("rep", "ctx", "tp"),
        P("tp", "rep", "ctx", None),
    )
    out_specs = (P("rep", "ctx", "tp"), P(("rep", "ctx"), "tp"), P(("rep", "ctx"), "tp"))
    return jax.shard_map(
        per_device, mesh=mesh, in_specs=in_specs, out_specs=out_specs, check_vma=False
    )
```

```python
import jax
import jax.numpy as jnp
from jax import lax
from jax.experimental import pallas as pl
from jax.experimental.pallas import tpu as pltpu
from jax.sharding import PartitionSpec as P

HD = 128
CL_DEV = 8
NY = 4
NZ = 8
ROWS = 32
HALF = 16
MESH = pl.DeviceIdType.MESH

masked_score = -1e30
ROOM = 56
LANES = 128
GROUP = 8
SLOTS = 96
TALL = 768
f32, bf16 = jnp.float32, jnp.bfloat16
NN = (((1,), (0,)), ((), ()))
NT = (((1,), (1,)), ((), ()))
TN = (((0,), (0,)), ((), ()))
BIG = 48 * 2**20


def dot(left, right, dims=NN):
    return lax.dot_general(left, right, dims, preferred_element_type=f32)


def halves(matrix):
    upper = matrix.astype(bf16)
    return upper, (matrix - upper.astype(f32)).astype(bf16)


def dot3(left, right, dims=NN):
    a, b = left
    c, d = right
    first = jnp.concatenate([a, b, a], axis=dims[0][0][0])
    second = jnp.concatenate([c, c, d], axis=dims[0][1][0])
    return dot(first, second, dims)


def position():
    ctx = lax.axis_index("ctx")
    return lax.axis_index("rep"), lax.div(ctx, NZ), lax.rem(ctx, NZ)


def greet(partners):
    barrier = pltpu.get_barrier_semaphore()
    for partner in partners:
        pl.semaphore_signal(barrier, inc=1, device_id=partner, device_id_type=MESH)
    pl.semaphore_wait(barrier, len(partners))


class Copies:
    def __init__(self, send_sem, recv_sem):
        self.send_sem, self.recv_sem = send_sem, recv_sem
        self.all = []

    def start(self, source, target, device):
        index = len(self.all)
        copy = pltpu.make_async_remote_copy(
            src_ref=source,
            dst_ref=target,
            send_sem=self.send_sem.at[index],
            recv_sem=self.recv_sem.at[index],
            device_id=device,
            device_id_type=MESH,
        )
        copy.start()
        self.all.append(copy)
        return copy

    def finish(self):
        for copy in self.all:
            copy.wait_send()


GATHER_COPIES = 3 + 7 + 14 + 21 + 16 + 4
ROUTE_COPIES = 3 + 7 + 3 + 1
CLUSTERS = 256
OWNERS = 32
PITCH = 64


def count_rows(cluster_ref, heads):
    length = cluster_ref.shape[1]
    line = lax.broadcasted_iota(jnp.int32, (8, length), 0)
    counts = jnp.zeros((8, CLUSTERS), f32)
    for head in range(heads):
        counts += dot(one(line == head), members(cluster_ref, head), NT)
    return counts


def one(condition):
    return jnp.where(condition, 1.0, 0.0).astype(bf16)


def members(cluster_ref, head):
    length = cluster_ref.shape[1]
    label = lax.broadcasted_iota(jnp.int32, (CLUSTERS, length), 0)
    return one(label == cluster_ref[head : head + 1, :])


def deal_order(counts):
    lane = lax.broadcasted_iota(jnp.int32, counts.shape, 1)
    return counts * CLUSTERS + (CLUSTERS - 1 - lane).astype(f32)


def route_head(cluster_ref, head, keys, tall_keys, earlier, base):
    larger = jnp.where(tall_keys[:, head : head + 1] > keys[head : head + 1, :], 1.0, 0.0)
    place = jnp.sum(larger, axis=0, keepdims=True).astype(jnp.int32)
    turn = place // OWNERS
    seat = place % OWNERS
    seat = jnp.where(turn % 2 == 0, seat, OWNERS - 1 - seat)
    seat = (seat + 8 * head) % OWNERS
    line = lax.broadcasted_iota(jnp.int32, (8, CLUSTERS), 0)
    table = jnp.where(line == 0, seat, jnp.where(line == 1, turn, 0)).astype(f32).astype(bf16)
    chosen = members(cluster_ref, head)
    looked = dot(table, chosen).astype(jnp.int32)
    owner, turn = looked[0:1, :], looked[1:2, :]
    within = jnp.sum(chosen.astype(f32) * dot(chosen, earlier), axis=0, keepdims=True)
    label = lax.broadcasted_iota(jnp.int32, (OWNERS, owner.shape[1]), 0)
    owned = one(label == owner)
    many = owned.astype(f32)
    rank = jnp.sum(many * (dot(owned, earlier) + base), axis=0, keepdims=True)
    base = base + jnp.sum(many, axis=1, keepdims=True)
    return owner, rank.astype(jnp.int32), head * CL_DEV + turn, within, base


def gather_kernel(
    qk_ref, value_ref, cluster_ref, grad_ref, tokens_ref,
    full_ref, early_ref, slots_ref, tall_slots_ref, pay_ref,
    out_ref, tokens, acc, counts_y, counts_z, most, ids_row, slots_row, pay, early_out,
    local_sem, send_sem, recv_sem, route_send, route_recv, early_send, early_recv,
):
    rep, y, z = position()
    me = lax.axis_index("ctx")
    x = lax.axis_index("tp")
    width = qk_ref.shape[1]
    heads = width // HD
    length = cluster_ref.shape[1]

    def along_y(step):
        return {"ctx": lax.rem(y + step, NY) * NZ + z}

    def along_z(step):
        return {"ctx": y * NZ + lax.rem(z + step, NZ)}

    def along_x(step):
        return {"tp": lax.rem(x + step, 4)}

    def around(step):
        return {"ctx": lax.rem(me + step, OWNERS)}

    def plane(step, part):
        there = pl.ds(part * width, width)
        return out_ref.at[rep, :, lax.rem(z + step, NZ), pl.ds(0, HALF), there]

    def piece(step):
        return out_ref.at[rep, y, lax.rem(z + step, NZ), pl.ds(HALF, HALF), :]

    def line(step):
        return out_ref.at[rep, lax.rem(y + step, NY), :, pl.ds(HALF, HALF), :]

    right, left, other = along_z(1), along_z(NZ - 1), {"rep": 1 - rep}
    mine = out_ref.at[rep, y, z]
    fetch = pltpu.make_async_copy(tokens_ref, tokens, local_sem.at[2])
    fetch.start()
    first = pltpu.make_async_copy(qk_ref, mine.at[:, pl.ds(0, width)], local_sem.at[0])
    second = pltpu.make_async_copy(value_ref, mine.at[:, pl.ds(width, width)], local_sem.at[1])
    first.start()
    second.start()
    barrier = pltpu.get_barrier_semaphore()

    @pl.loop(1, OWNERS)
    def _(step):
        pl.semaphore_signal(barrier, inc=1, device_id=around(step), device_id_type=MESH)

    for partner in (other, along_x(1), along_x(2), along_x(3)):
        pl.semaphore_signal(barrier, inc=1, device_id=partner, device_id_type=MESH)
    counts_y[0] = count_rows(cluster_ref, heads)
    pl.semaphore_wait(barrier, OWNERS - 1 + 4)

    routes = Copies(route_send, route_recv)
    counted = [
        routes.start(counts_y.at[0], counts_y.at[step], along_y(step)) for step in (1, 2, 3)
    ]
    first.wait()
    second.wait()
    copies = Copies(send_sem, recv_sem)
    shared = [copies.start(mine, mine, along_y(step)) for step in (1, 3, 2)]
    pieces = [(copies.start(piece(0), piece(0), right), copies.start(piece(0), piece(0), left))]

    for head in range(heads):
        upper, lower = halves(grad_ref[:, head * HD : (head + 1) * HD])
        pay[pl.ds(head * length, length), :HD] = upper
        pay[pl.ds(head * length, length), HD:] = lower

    for copy in counted:
        copy.wait_recv()
    counts_z[0] = counts_y[0] + counts_y[1] + counts_y[2] + counts_y[3]
    counted = [
        routes.start(counts_z.at[0], counts_z.at[step], along_z(step)) for step in range(1, NZ)
    ]
    for copy in shared:
        copy.wait_recv()
    planes = []
    for part in range(2):
        here = plane(0, part)
        planes.append([(copies.start(here, here, right), copies.start(here, here, left))])
    across = [copies.start(plane(0, part), plane(0, part), other) for part in range(2)]
    passed = {1: [], 2: [], 3: []}

    def pass_on(here):
        for step in (1, 3, 2):
            passed[step].append(copies.start(here, here, along_y(step)))

    def turn_pieces(step):
        rightward, leftward = pieces[step]
        after, before = piece(NZ - 1 - step), piece(1 + step)
        rightward.wait_recv()
        if leftward is not None:
            leftward.wait_recv()
        if step < 3:
            pieces.append((
                copies.start(after, after, right),
                copies.start(before, before, left) if step < 2 else None,
            ))
        pass_on(after)
        if leftward is not None:
            pass_on(before)

    def turn_planes(step):
        for part in range(2):
            turn_plane(step, part)

    def turn_plane(step, part):
        rightward, leftward = planes[part][step]
        after, before = plane(NZ - 1 - step, part), plane(1 + step, part)
        rightward.wait_recv()
        if step < 3:
            going = copies.start(after, after, right)
        if leftward is not None:
            leftward.wait_recv()
            coming = copies.start(before, before, left) if step < 2 else None
        if step < 3:
            planes[part].append((going, coming if step < 2 else None))
        across.append(copies.start(after, after, other))
        if leftward is not None:
            across.append(copies.start(before, before, other))

    turn_pieces(0)
    for copy in counted:
        copy.wait_recv()
    total = counts_z[0]
    for step in range(1, NZ):
        total += counts_z[step]
    keys = deal_order(total)
    tall_keys = jnp.concatenate([keys] + [jnp.zeros_like(keys)] * 15, axis=0).T
    earlier = one(
        lax.broadcasted_iota(jnp.int32, (length, length), 0)
        < lax.broadcasted_iota(jnp.int32, (length, length), 1)
    )
    base = jnp.zeros((OWNERS, 1), f32)
    highest = jnp.zeros((1, 1), f32)
    row = lax.broadcasted_iota(jnp.int32, (8, length), 0)
    slots_list = []
    for head in range(heads):
        owner, rank, held, within, base = route_head(
            cluster_ref, head, keys, tall_keys, earlier, base
        )
        highest = jnp.maximum(highest, jnp.max(rank.astype(f32), axis=1, keepdims=True) + 1)
        here = pl.ds(head * length, length)
        slots_ref[:, here] = jnp.where(rank < ROOM, owner * ROOM + rank, -1)
        slots_row[:, here] = jnp.where(rank < ROOM, owner * PITCH + rank, -1)
        within = within + (3 * lax.rem(me, GROUP)).astype(f32)
        marked = jnp.where(row == 0, (held + 1).astype(f32), jnp.where(row == 1, within, 0.0))
        ids_row[:, here] = marked.astype(bf16)
        slots_list.append(jnp.where(rank < ROOM, owner * ROOM + rank, -1))
        if head < 3:
            turn_pieces(head + 1)
    most[0] = jnp.broadcast_to(highest, (8, LANES))
    tall = jnp.concatenate(
        slots_list + [jnp.zeros((LANES - heads, length), jnp.int32)], axis=0
    )
    tall_slots_ref[...] = tall.astype(f32).T.astype(jnp.int32)
    fullest = [routes.start(most.at[0], most.at[step], along_x(step)) for step in (1, 2, 3)]
    across.append(copies.start(line(0), line(0), other))
    turn_planes(0)
    for copy in fullest:
        copy.wait_recv()
    most[4] = jnp.maximum(jnp.maximum(most[0], most[1]), jnp.maximum(most[2], most[3]))
    fullest = routes.start(most.at[4], most.at[5], other)

    @pl.loop(0, OWNERS // 4)
    def _(block):
        rows = 4 * PITCH
        place = lax.broadcasted_iota(jnp.int32, (rows, heads * length), 0) + block * rows
        chosen = one(place == slots_row[...])
        both = dot(chosen, pay[...])
        both = both[:, :HD] + both[:, HD:]
        marks = dot(ids_row[...], chosen, NT)
        for lane in range(4):
            early_out[block * 4 + lane] = both[lane * PITCH : (lane + 1) * PITCH]
            early_out[block * 4 + lane, pl.ds(ROOM, 8), pl.ds(0, PITCH)] = marks[
                :, lane * PITCH : (lane + 1) * PITCH
            ]

    fullest.wait_recv()
    overall = jnp.maximum(most[4], most[5])[:, :PITCH]

    @pl.loop(0, OWNERS)
    def _(block):
        early_out[block, pl.ds(ROOM, 8), pl.ds(PITCH, PITCH)] = overall

    def early(step):
        there = lax.rem(me + step, OWNERS)
        return pltpu.make_async_remote_copy(
            src_ref=early_out.at[there],
            dst_ref=early_ref.at[me],
            send_sem=early_send.at[step],
            recv_sem=early_recv.at[step],
            device_id={"ctx": there},
            device_id_type=MESH,
        )

    @pl.loop(1, OWNERS)
    def _(step):
        early(step).start()

    stay = pltpu.make_async_copy(early_out.at[me], early_ref.at[me], local_sem.at[0])
    stay.start()
    for step in range(1, 4):
        turn_planes(step)
    for step in (1, 3, 2):
        for copy in passed[step]:
            copy.wait_recv()
        across.append(copies.start(line(NY - step), line(NY - step), other))
    fetch.wait()

    def project(half, there):
        start = pl.multiple_of((half * NY + there) * (NZ * ROWS), NZ * ROWS)
        some = halves(tokens[:, pl.ds(start, NZ * ROWS)])
        return dot3(some, halves(out_ref[half, there].reshape(NZ * ROWS, 2 * width)))

    acc[...] = project(rep, 0)

    @pl.loop(1, NY)
    def _(there):
        acc[...] += project(rep, there)

    for copy in across:
        copy.wait_recv()
    save = pltpu.make_async_copy(out_ref, full_ref, local_sem.at[1])
    save.start()

    @pl.loop(0, NY)
    def _(there):
        acc[...] += project(1 - rep, there)

    for part in range(2):
        for head in range(heads):
            here = pl.ds(head * length, length)
            column = part * width + head * HD
            upper, lower = halves(acc[:, column : column + HD])
            pay_ref[part, here, :HD] = upper
            pay_ref[part, here, HD:] = lower
    copies.finish()
    routes.finish()
    stay.wait()
    save.wait()

    @pl.loop(1, OWNERS)
    def _(step):
        early(step).wait()

    assert len(copies.all) == GATHER_COPIES and len(routes.all) == ROUTE_COPIES


def gather_and_project(qk_weight, value_weight, clusters, upstream, inputs):
    width = qk_weight.shape[1]
    length = clusters.shape[1]
    rows = width // HD * length
    vmem, anywhere = pl.BlockSpec(memory_space=pltpu.VMEM), pl.BlockSpec(memory_space=pl.ANY)
    return pl.pallas_call(
        gather_kernel,
        out_shape=(
            jax.ShapeDtypeStruct((2, NY, NZ, ROWS, 2 * width), f32),
            jax.ShapeDtypeStruct((OWNERS, PITCH, HD), f32),
            jax.ShapeDtypeStruct((1, rows), jnp.int32),
            jax.ShapeDtypeStruct((length, LANES), jnp.int32),
            jax.ShapeDtypeStruct((2, rows, 2 * HD), bf16),
        ),
        in_specs=[anywhere, anywhere, vmem, vmem, anywhere],
        out_specs=(anywhere, anywhere, vmem, vmem, vmem),
        scratch_shapes=[
            pltpu.VMEM((2, NY, NZ, ROWS, 2 * width), f32),
            pltpu.VMEM(inputs.shape, f32),
            pltpu.VMEM((length, 2 * width), f32),
            pltpu.VMEM((NY, 8, CLUSTERS), f32),
            pltpu.VMEM((NZ, 8, CLUSTERS), f32),
            pltpu.VMEM((6, 8, LANES), f32),
            pltpu.VMEM((8, rows), bf16),
            pltpu.VMEM((1, rows), jnp.int32),
            pltpu.VMEM((rows, 2 * HD), bf16),
            pltpu.VMEM((OWNERS, PITCH, HD), f32),
            pltpu.SemaphoreType.DMA((3,)),
            pltpu.SemaphoreType.DMA((GATHER_COPIES,)),
            pltpu.SemaphoreType.DMA((GATHER_COPIES,)),
            pltpu.SemaphoreType.DMA((ROUTE_COPIES,)),
            pltpu.SemaphoreType.DMA((ROUTE_COPIES,)),
            pltpu.SemaphoreType.DMA((OWNERS,)),
            pltpu.SemaphoreType.DMA((OWNERS,)),
        ],
        compiler_params=pltpu.CompilerParams(
            collective_id=0, has_side_effects=True, vmem_limit_bytes=BIG
        ),
        name="gather_and_project",
    )(qk_weight, value_weight, clusters, upstream, inputs)


SCATTER_COPIES = 3 + 12 + 7 + 3 + 7 + 3


def scatter_kernel(
    terms_ref, sums_ref, tokens_out, qk_out, value_out,
    column_in, cross_in, ring_a, ring_b, line_in, plane_in,
    local_sem, send_sem, recv_sem,
):
    rep, y, z = position()
    x = lax.axis_index("tp")
    width = qk_out.shape[1]

    def along_y(step):
        return {"ctx": lax.rem(y + step, NY) * NZ + z}

    def along_z(step):
        return {"ctx": y * NZ + lax.rem(z + step, NZ)}

    def along_x(step):
        return {"tp": lax.rem(x + step, 4)}

    def columns(step):
        start = pl.multiple_of(lax.rem(x + step, 4) * width, width)
        return terms_ref.at[:, pl.ds(start, width)]

    def plane(step):
        return cross_in.at[:, lax.rem(z + step, NZ), pl.ds(0, HALF), :]

    def line(step):
        return cross_in.at[lax.rem(y + step, NY), :, pl.ds(HALF, HALF), :]

    def piece(step):
        return cross_in.at[y, lax.rem(z + step, NZ), pl.ds(HALF, HALF), :]

    right, left, other = along_z(1), along_z(NZ - 1), {"rep": 1 - rep}
    greet(
        [along_y(1), along_y(2), along_y(3), right, left, other]
        + [along_x(1), along_x(2), along_x(3)]
    )
    copies = Copies(send_sem, recv_sem)
    sideways = [
        copies.start(columns(step), column_in.at[step - 1], along_x(step)) for step in (1, 3, 2)
    ]
    own_columns = pltpu.make_async_copy(columns(0), tokens_out, local_sem)
    own_columns.start()

    cross = {}
    for kind, step in (
        ("a", 4), ("a", 5), ("b", 1), ("b", 3), ("b", 2), ("a", 3),
        ("a", 6), ("a", 2), ("a", 7), ("b", 0), ("a", 1), ("a", 0),
    ):
        if kind == "a":
            there = lax.rem(z + step, NZ)
            source = sums_ref.at[1 - rep, :, there, pl.ds(0, HALF), :]
            cross[kind, step] = copies.start(source, plane(step), other)
        else:
            there = lax.rem(y + step, NY)
            source = sums_ref.at[1 - rep, there, :, pl.ds(HALF, HALF), :]
            cross[kind, step] = copies.start(source, line(step), other)

    def add_plane(step):
        cross["a", step].wait_recv()
        there = lax.rem(z + step, NZ)
        cross_in[:, there, pl.ds(0, HALF), :] += sums_ref[rep, :, there, pl.ds(0, HALF), :]

    def add_line(step):
        cross["b", step].wait_recv()
        there = lax.rem(y + step, NY)
        cross_in[there, :, pl.ds(HALF, HALF), :] += sums_ref[
            rep, there, :, pl.ds(HALF, HALF), :
        ]

    add_plane(4)
    right_a = copies.start(plane(4), ring_a.at[0], right)
    add_plane(5)
    left_a = copies.start(plane(5), ring_a.at[4], left)
    lines = []
    for step in (1, 3, 2):
        add_line(step)
        lines.append(copies.start(line(step), line_in.at[step - 1], along_y(step)))

    def pass_a(turn):
        nonlocal right_a, left_a
        add_plane(4 - turn)
        right_a.wait_recv()
        ring_a[turn - 1] += cross_in[:, lax.rem(z + 4 - turn, NZ), pl.ds(0, HALF), :]
        right_a = copies.start(ring_a.at[turn - 1], ring_a.at[turn], right)
        if turn < 3:
            add_plane(5 + turn)
            left_a.wait_recv()
            ring_a[3 + turn] += cross_in[:, lax.rem(z + 5 + turn, NZ), pl.ds(0, HALF), :]
            left_a = copies.start(ring_a.at[3 + turn], ring_a.at[4 + turn], left)

    pass_a(1)
    add_line(0)
    pass_a(2)
    for copy in lines:
        copy.wait_recv()
    cross_in[y, :, pl.ds(HALF, HALF), :] += line_in[0] + line_in[1] + line_in[2]
    right_b = copies.start(piece(4), ring_b.at[0], right)
    left_b = copies.start(piece(5), ring_b.at[4], left)
    pass_a(3)

    def pass_b(turn):
        nonlocal right_b, left_b
        right_b.wait_recv()
        ring_b[turn - 1] += cross_in[y, lax.rem(z + 4 - turn, NZ), pl.ds(HALF, HALF), :]
        right_b = copies.start(ring_b.at[turn - 1], ring_b.at[turn], right)
        if turn < 3:
            left_b.wait_recv()
            ring_b[3 + turn] += cross_in[y, lax.rem(z + 5 + turn, NZ), pl.ds(HALF, HALF), :]
            left_b = copies.start(ring_b.at[3 + turn], ring_b.at[4 + turn], left)

    pass_b(1)
    pass_b(2)
    add_plane(0)
    right_a.wait_recv()
    left_a.wait_recv()
    cross_in[:, z, pl.ds(0, HALF), :] += ring_a[3] + ring_a[6]
    planes = [
        copies.start(
            cross_in.at[lax.rem(y + step, NY), z, pl.ds(0, HALF), :],
            plane_in.at[step - 1],
            along_y(step),
        )
        for step in (1, 3, 2)
    ]
    pass_b(3)
    right_b.wait_recv()
    left_b.wait_recv()
    lower = cross_in[y, z, pl.ds(HALF, HALF), :] + ring_b[3] + ring_b[6]
    qk_out[pl.ds(HALF, HALF), :] = lower[:, :width]
    value_out[pl.ds(HALF, HALF), :] = lower[:, width:]
    for copy in planes:
        copy.wait_recv()
    upper = cross_in[y, z, pl.ds(0, HALF), :] + plane_in[0] + plane_in[1] + plane_in[2]
    qk_out[pl.ds(0, HALF), :] = upper[:, :width]
    value_out[pl.ds(0, HALF), :] = upper[:, width:]
    own_columns.wait()
    for copy in sideways:
        copy.wait_recv()

    @pl.loop(0, tokens_out.shape[0] // 8)
    def _(block):
        here = pl.ds(pl.multiple_of(block * 8, 8), 8)
        tokens_out[here, :] += column_in[0, here, :] + column_in[1, here, :] + column_in[2, here, :]

    copies.finish()
    assert len(copies.all) == SCATTER_COPIES


def scatter_sums(token_terms, weight_terms):
    length = token_terms.shape[0]
    both = weight_terms.shape[1]
    width = both // 2
    return pl.pallas_call(
        scatter_kernel,
        out_shape=(
            jax.ShapeDtypeStruct((length, width), f32),
            jax.ShapeDtypeStruct((ROWS, width), f32),
            jax.ShapeDtypeStruct((ROWS, width), f32),
        ),
        in_specs=[pl.BlockSpec(memory_space=pl.ANY), pl.BlockSpec(memory_space=pltpu.VMEM)],
        out_specs=(pl.BlockSpec(memory_space=pltpu.VMEM),) * 3,
        scratch_shapes=[
            pltpu.VMEM((3, length, width), f32),
            pltpu.VMEM((NY, NZ, ROWS, both), f32),
            pltpu.VMEM((7, NY, HALF, both), f32),
            pltpu.VMEM((7, HALF, both), f32),
            pltpu.VMEM((3, NZ, HALF, both), f32),
            pltpu.VMEM((3, HALF, both), f32),
            pltpu.SemaphoreType.DMA,
            pltpu.SemaphoreType.DMA((SCATTER_COPIES,)),
            pltpu.SemaphoreType.DMA((SCATTER_COPIES,)),
        ],
        compiler_params=pltpu.CompilerParams(
            collective_id=1, has_side_effects=True, vmem_limit_bytes=48 * 2**20
        ),
        name="scatter_sums",
    )(token_terms, weight_terms.reshape(2, NY, NZ, ROWS, both))


def pack_kernel(tokens_ref, full_ref, slots_ref, rows_ref, acc, pay):
    step = pl.program_id(0)
    length, both = acc.shape
    rows = rows_ref.shape[0]

    @pl.when(step == 0)
    def _():
        acc[...] = jnp.zeros_like(acc)

    @pl.when(step < 8)
    def _():
        acc[...] += dot3(halves(tokens_ref[...]), halves(full_ref[...]))

    @pl.when(step == 7)
    def _():
        for head in range(both // (2 * HD)):
            here = pl.ds(head * length, length)
            for part in range(2):
                column = part * both // 2 + head * HD
                upper, lower = halves(acc[:, column : column + HD])
                pay[here, part * HD : (part + 1) * HD] = upper
                pay[here, (2 + part) * HD : (3 + part) * HD] = lower

    @pl.when(step >= 8)
    def _():
        place = lax.broadcasted_iota(jnp.int32, (rows, slots_ref.shape[1]), 0) + (step - 8) * rows
        moved = dot(one(place == slots_ref[...]), pay[...])
        rows_ref[...] = moved[:, : 2 * HD] + moved[:, 2 * HD :]


def pack_rows(inputs, full, slots, room):
    length, depth = inputs.shape
    both = full.shape[1]
    total = slots.shape[1]
    return pl.pallas_call(
        pack_kernel,
        grid=(16,),
        out_shape=jax.ShapeDtypeStruct((OWNERS * room, 2 * HD), f32),
        in_specs=[
            pl.BlockSpec((length, depth // 8), lambda i: (0, jnp.minimum(i, 7))),
            pl.BlockSpec((depth // 8, both), lambda i: (jnp.minimum(i, 7), 0)),
            pl.BlockSpec((1, total), lambda i: (0, 0)),
        ],
        out_specs=pl.BlockSpec((4 * room, 2 * HD), lambda i: (jnp.maximum(i - 8, 0), 0)),
        scratch_shapes=[pltpu.VMEM((length, both), f32), pltpu.VMEM((total, 4 * HD), bf16)],
        compiler_params=pltpu.CompilerParams(vmem_limit_bytes=BIG),
        name="project_and_pack",
    )(inputs, full, slots)


def attend_kernel(marks_ref, rows_ref, early_ref, replies_ref, spread, seats, valid, answer):
    groups = marks_ref.shape[0]
    wide = marks_ref.shape[2]
    owned = spread.shape[1]
    seat = spread.shape[2]
    size = groups * seat

    @pl.loop(0, groups)
    def _(group):
        here = pl.ds(pl.multiple_of(group * wide, wide), wide)
        place = lax.broadcasted_iota(jnp.int32, (TALL, wide), 0)
        chosen = one(place == marks_ref[group])
        seats[group] = chosen
        upper, lower = halves(rows_ref[here, :])
        early = early_ref[pl.ds(group * GROUP, GROUP), pl.ds(0, wide // GROUP), :]
        early_upper, early_lower = halves(early.reshape(wide, HD))
        present = jnp.ones((wide, LANES), bf16)
        moved = dot(
            chosen, jnp.concatenate([upper, early_upper, lower, early_lower, present], axis=1)
        )
        spread[group] = (moved[:, : 3 * HD] + moved[:, 3 * HD : 6 * HD]).reshape(owned, seat, 3 * HD)
        valid[group] = moved[:, 6 * HD :].reshape(owned, seat, LANES)

    @pl.loop(0, owned // 4)
    def _(block):
        for lane in range(4):
            index = block * 4 + lane
            rows = spread[:, index].reshape(size, 3 * HD)
            present = valid[:, index].reshape(size, LANES)[:, :size] > 0.5
            qk = halves(rows[:, :HD])
            value = halves(rows[:, HD : 2 * HD])
            upstream = halves(rows[:, 2 * HD :])
            scores = jnp.where(present, dot3(qk, qk, NT) / HD, masked_score)
            weights = jnp.exp(scores - jnp.max(scores, axis=0, keepdims=True))
            weights = weights / jnp.sum(weights, axis=0, keepdims=True)
            slopes = dot3(value, upstream, NT)
            middle = jnp.sum(weights * slopes, axis=0, keepdims=True)
            slopes = weights * (slopes - middle)
            grad_qk = dot3(halves(slopes + slopes.T), qk) / HD
            grad_value = dot3(halves(weights), upstream)
            answer[:, index] = jnp.concatenate([grad_qk, grad_value], axis=1).reshape(
                groups, seat, 2 * HD
            )

    @pl.loop(0, groups)
    def _(group):
        here = pl.ds(pl.multiple_of(group * wide, wide), wide)
        upper, lower = halves(answer[group].reshape(TALL, 2 * HD))
        moved = dot(seats[group], jnp.concatenate([upper, lower], axis=1), TN)
        replies_ref[here, :] = moved[:, : 2 * HD] + moved[:, 2 * HD :]


def attend(rows, early, marks, room):
    groups = OWNERS // GROUP
    owned = TALL // (3 * GROUP)
    seat = 3 * GROUP
    return pl.pallas_call(
        attend_kernel,
        out_shape=jax.ShapeDtypeStruct((OWNERS * room, 2 * HD), f32),
        in_specs=[pl.BlockSpec(memory_space=pltpu.VMEM)] * 3,
        out_specs=pl.BlockSpec(memory_space=pltpu.VMEM),
        scratch_shapes=[
            pltpu.VMEM((groups, owned, seat, 3 * HD), f32),
            pltpu.VMEM((groups, TALL, GROUP * room), bf16),
            pltpu.VMEM((groups, owned, seat, LANES), f32),
            pltpu.VMEM((groups, owned, seat, 2 * HD), f32),
        ],
        compiler_params=pltpu.CompilerParams(vmem_limit_bytes=BIG),
        name="attend",
    )(marks, rows, early)


QK, VALUE, GRAD_VALUE, GRAD_QK = range(4)


def cluster_kernel(
    pay_ref, slots_ref, marks_ref, early_ref, back_qk_ref, back_value_ref,
    leaving, landed, seats, spread, valid, weights, answer,
    local_sem, send_sem, recv_sem,
):
    me = lax.axis_index("ctx")
    groups, _, wide = marks_ref.shape
    owned, seat = spread.shape[2], spread.shape[3]
    size = groups * seat
    rows = 4 * ROOM

    barrier = pltpu.get_barrier_semaphore()

    @pl.loop(1, OWNERS)
    def _(step):
        there = {"ctx": lax.rem(me + step, OWNERS)}
        pl.semaphore_signal(barrier, inc=1, device_id=there, device_id_type=MESH)

    def target(kind):
        if kind == GRAD_QK:
            return back_qk_ref
        return back_value_ref if kind == GRAD_VALUE else landed.at[kind]

    def remote(kind, step):
        there = lax.rem(me + step, OWNERS)
        return pltpu.make_async_remote_copy(
            src_ref=leaving.at[kind, there],
            dst_ref=target(kind).at[me],
            send_sem=send_sem.at[kind, step],
            recv_sem=recv_sem.at[kind, step],
            device_id={"ctx": there},
            device_id_type=MESH,
        )

    def stay(kind):
        return pltpu.make_async_copy(leaving.at[kind, me], target(kind).at[me], local_sem.at[kind])

    def start(kind, there):
        @pl.when(there == me)
        def _():
            stay(kind).start()

        @pl.when(there != me)
        def _():
            remote(kind, lax.rem(there - me + OWNERS, OWNERS)).start()

    def arrive(kind):
        stay(kind).wait()

        @pl.loop(1, OWNERS)
        def _(step):
            remote(kind, step).wait_recv()

    def pack(kind, block):
        place = lax.broadcasted_iota(jnp.int32, (rows, slots_ref.shape[1]), 0) + block * rows
        moved = dot(one(place == slots_ref[...]), pay_ref[kind])
        moved = moved[:, :HD] + moved[:, HD:]
        for lane in range(4):
            leaving[kind, block * 4 + lane] = moved[lane * ROOM : (lane + 1) * ROOM]

    def take(kind, group, source):
        upper, lower = halves(source)
        moved = dot(seats[group], jnp.concatenate([upper, lower], axis=1))
        spread[kind, group] = (moved[:, :HD] + moved[:, HD:]).reshape(owned, seat, HD)

    def give(kind):
        @pl.loop(0, groups)
        def _(index):
            group = lax.rem(lax.div(me, GROUP) + index, groups)
            upper, lower = halves(answer[group].reshape(TALL, HD))
            moved = dot(seats[group], jnp.concatenate([upper, lower], axis=1), TN)
            moved = (moved[:, :HD] + moved[:, HD:]).reshape(GROUP, ROOM, HD)
            leaving[kind, pl.ds(group * GROUP, GROUP)] = moved
            for lane in range(GROUP):
                start(kind, group * GROUP + lane)

    def first_block():
        return lax.div(me, 4)

    pack(QK, first_block())
    pl.semaphore_wait(barrier, OWNERS - 1)
    for lane in range(4):
        start(QK, first_block() * 4 + lane)

    @pl.loop(1, OWNERS // 4)
    def _(index):
        block = lax.rem(first_block() + index, OWNERS // 4)
        pack(QK, block)
        for lane in range(4):
            start(QK, block * 4 + lane)

    @pl.loop(0, OWNERS // 4)
    def _(block):
        pack(VALUE, block)

    @pl.loop(0, groups)
    def _(group):
        place = lax.broadcasted_iota(jnp.int32, (TALL, wide), 0)
        chosen = one(place == marks_ref[group])
        seats[group] = chosen
        early = early_ref[pl.ds(group * GROUP, GROUP), pl.ds(0, ROOM), :].reshape(wide, HD)
        upper, lower = halves(early)
        present = jnp.ones((wide, LANES), bf16)
        moved = dot(chosen, jnp.concatenate([upper, lower, present], axis=1))
        spread[2, group] = (moved[:, :HD] + moved[:, HD : 2 * HD]).reshape(owned, seat, HD)
        valid[group] = moved[:, 2 * HD :].reshape(owned, seat, LANES)

    arrive(QK)

    @pl.loop(0, OWNERS)
    def _(index):
        start(VALUE, lax.rem(me + index, OWNERS))

    @pl.loop(0, groups)
    def _(group):
        take(QK, group, landed[QK, pl.ds(group * GROUP, GROUP)].reshape(wide, HD))

    def cluster(kind, index):
        return halves(spread[kind, :, index].reshape(size, HD))

    @pl.loop(0, owned // 4)
    def _(block):
        for lane in range(4):
            index = block * 4 + lane
            present = valid[:, index].reshape(size, LANES)[:, :size] > 0.5
            qk = cluster(QK, index)
            scores = jnp.where(present, dot3(qk, qk, NT) / HD, masked_score)
            raised = jnp.exp(scores - jnp.max(scores, axis=0, keepdims=True))
            raised = raised / jnp.sum(raised, axis=0, keepdims=True)
            weights[index] = raised
            answer[:, index] = dot3(halves(raised), cluster(2, index)).reshape(groups, seat, HD)

    give(GRAD_VALUE)
    arrive(VALUE)

    @pl.loop(0, groups)
    def _(group):
        take(VALUE, group, landed[VALUE, pl.ds(group * GROUP, GROUP)].reshape(wide, HD))

    @pl.loop(0, owned // 4)
    def _(block):
        for lane in range(4):
            index = block * 4 + lane
            raised = weights[index]
            slopes = dot3(cluster(VALUE, index), cluster(2, index), NT)
            middle = jnp.sum(raised * slopes, axis=0, keepdims=True)
            slopes = raised * (slopes - middle)
            grad_qk = dot3(halves(slopes + slopes.T), cluster(QK, index)) / HD
            answer[:, index] = grad_qk.reshape(groups, seat, HD)

    give(GRAD_QK)
    arrive(GRAD_VALUE)
    arrive(GRAD_QK)

    @pl.loop(1, OWNERS)
    def _(step):
        for kind in range(4):
            remote(kind, step).wait_send()


def cluster_part(pay, slots, marks, early):
    groups = OWNERS // GROUP
    owned = TALL // (3 * GROUP)
    seat = 3 * GROUP
    size = groups * seat
    rows = jax.ShapeDtypeStruct((OWNERS, ROOM, HD), f32)
    return pl.pallas_call(
        cluster_kernel,
        out_shape=(rows, rows),
        in_specs=[pl.BlockSpec(memory_space=pltpu.VMEM)] * 4,
        out_specs=(pl.BlockSpec(memory_space=pl.ANY),) * 2,
        scratch_shapes=[
            pltpu.VMEM((4, OWNERS, ROOM, HD), f32),
            pltpu.VMEM((2, OWNERS, ROOM, HD), f32),
            pltpu.VMEM((groups, TALL, GROUP * ROOM), bf16),
            pltpu.VMEM((3, groups, owned, seat, HD), f32),
            pltpu.VMEM((groups, owned, seat, LANES), f32),
            pltpu.VMEM((owned, size, size), f32),
            pltpu.VMEM((groups, owned, seat, HD), f32),
            pltpu.SemaphoreType.DMA((4,)),
            pltpu.SemaphoreType.DMA((4, OWNERS)),
            pltpu.SemaphoreType.DMA((4, OWNERS)),
        ],
        compiler_params=pltpu.CompilerParams(
            collective_id=2, has_side_effects=True, vmem_limit_bytes=BIG
        ),
        name="exchange_and_attend",
    )(pay, slots, marks, early)


def grads_kernel(
    back_qk_ref, back_value_ref, slots_ref, tokens_ref, full_ref, terms_ref, sums_ref, high, low
):
    length = tokens_ref.shape[0]
    width = high.shape[1] // 2
    total = back_qk_ref.shape[0]

    @pl.when(pl.program_id(0) == 0)
    def _():
        qk_upper, qk_lower = halves(back_qk_ref[...])
        upper, lower = halves(back_value_ref[...])
        source = jnp.concatenate([qk_upper, upper, qk_lower, lower], axis=1)
        for head in range(width // HD):
            place = lax.broadcasted_iota(jnp.int32, (length, total), 1)
            chosen = one(place == slots_ref[:, head : head + 1])
            both = dot(chosen, source)
            upper, lower = halves(both[:, : 2 * HD] + both[:, 2 * HD :])
            for part in range(2):
                there = pl.ds(part * width + head * HD, HD)
                high[:, there] = upper[:, part * HD : (part + 1) * HD]
                low[:, there] = lower[:, part * HD : (part + 1) * HD]

    combined = high[...], low[...]
    terms_ref[...] = dot3(combined, halves(full_ref[...]), NT)
    sums_ref[...] = dot3(halves(tokens_ref[...]), combined, TN)


def local_grads(back_qk, back_value, slots, inputs, full):
    length, depth = inputs.shape
    both = full.shape[1]
    total = back_qk.shape[0]
    return pl.pallas_call(
        grads_kernel,
        grid=(8,),
        out_shape=(
            jax.ShapeDtypeStruct((length, depth), f32),
            jax.ShapeDtypeStruct((depth, both), f32),
        ),
        in_specs=[
            pl.BlockSpec((total, HD), lambda i: (0, 0)),
            pl.BlockSpec((total, HD), lambda i: (0, 0)),
            pl.BlockSpec(slots.shape, lambda i: (0, 0)),
            pl.BlockSpec((length, depth // 8), lambda i: (0, i)),
            pl.BlockSpec((depth // 8, both), lambda i: (i, 0)),
        ],
        out_specs=(
            pl.BlockSpec((length, depth // 8), lambda i: (0, i)),
            pl.BlockSpec((depth // 8, both), lambda i: (i, 0)),
        ),
        scratch_shapes=[pltpu.VMEM((length, both), bf16)] * 2,
        compiler_params=pltpu.CompilerParams(vmem_limit_bytes=BIG),
        name="unpack_and_grads",
    )(back_qk, back_value, slots, inputs, full)


FINISH_COPIES = 14 + 7 + 6


def finish_kernel(
    back_qk_ref, back_value_ref, slots_ref, tokens_ref, full_ref,
    tokens_out, qk_out, value_out,
    tokens, full, high, low, terms, away, own, cross_in,
    column_in, ring_a, ring_b, line_in, plane_in,
    load_sem, send_sem, recv_sem, column_send, column_recv, cross_send, cross_recv,
    line_send, line_recv,
):
    rep, y, z = position()
    x = lax.axis_index("tp")
    length = tokens.shape[0]
    both = full.shape[1]
    width = both // 2
    total = back_qk_ref.shape[0]
    per_line = NZ * ROWS

    def along_y(step):
        return {"ctx": lax.rem(y + step, NY) * NZ + z}

    def along_z(step):
        return {"ctx": y * NZ + lax.rem(z + step, NZ)}

    def along_x(step):
        return {"tp": lax.rem(x + step, 4)}

    loads = [
        pltpu.make_async_copy(tokens_ref, tokens, load_sem.at[0]),
        pltpu.make_async_copy(full_ref, full, load_sem.at[1]),
    ]
    for load in loads:
        load.start()
    right, left, other = along_z(1), along_z(NZ - 1), {"rep": 1 - rep}
    barrier = pltpu.get_barrier_semaphore()
    partners = [along_y(1), along_y(2), along_y(3), right, left, other]
    partners += [along_x(1), along_x(2), along_x(3)]
    for partner in partners:
        pl.semaphore_signal(barrier, inc=1, device_id=partner, device_id_type=MESH)

    qk_upper, qk_lower = halves(back_qk_ref[...])
    upper, lower = halves(back_value_ref[...])
    source = jnp.concatenate([qk_upper, upper, qk_lower, lower], axis=1)
    for head in range(width // HD):
        place = lax.broadcasted_iota(jnp.int32, (length, total), 1)
        moved = dot(one(place == slots_ref[:, head : head + 1]), source)
        upper, lower = halves(moved[:, : 2 * HD] + moved[:, 2 * HD :])
        for part in range(2):
            there = pl.ds(part * width + head * HD, HD)
            high[:, there] = upper[:, part * HD : (part + 1) * HD]
            low[:, there] = lower[:, part * HD : (part + 1) * HD]

    for load in loads:
        load.wait()
    pl.semaphore_wait(barrier, len(partners))

    def columns(step):
        start = pl.multiple_of(lax.rem(x + step, 4) * width, width)
        return dot3((high[...], low[...]), halves(full[pl.ds(start, width), :]), NT)

    def sideways(step):
        return pltpu.make_async_remote_copy(
            src_ref=terms.at[step - 1],
            dst_ref=column_in.at[step - 1],
            send_sem=column_send.at[step - 1],
            recv_sem=column_recv.at[step - 1],
            device_id=along_x(step),
            device_id_type=MESH,
        )

    @pl.loop(1, 4)
    def _(step):
        terms[step - 1] = columns(step)
        sideways(step).start()

    def line_sum(half, there):
        start = pl.multiple_of(half * (NY * per_line) + there * per_line, per_line)
        some = halves(tokens[:, pl.ds(start, per_line)])
        return dot3(some, (high[...], low[...]), TN).reshape(NZ, ROWS, both)

    def cross(step):
        there = lax.rem(y + step, NY)
        return pltpu.make_async_remote_copy(
            src_ref=away.at[there],
            dst_ref=cross_in.at[there],
            send_sem=cross_send.at[step],
            recv_sem=cross_recv.at[step],
            device_id=other,
            device_id_type=MESH,
        )

    @pl.loop(0, 4)
    def _(index):
        step = lax.rem(index + 1, 4)
        there = lax.rem(y + step, NY)
        away[there] = line_sum(1 - rep, there)
        cross(step).start()

    def depth(turn):
        return lax.rem(z + turn, NZ)

    def piece(step, turn):
        return pltpu.make_async_remote_copy(
            src_ref=own.at[lax.rem(y + step, NY), depth(turn), pl.ds(HALF, HALF), :],
            dst_ref=line_in.at[step - 1, depth(turn)],
            send_sem=line_send.at[step - 1, turn],
            recv_sem=line_recv.at[step - 1, turn],
            device_id=along_y(step),
            device_id_type=MESH,
        )

    def own_line(step):
        there = lax.rem(y + step, NY)
        mine = line_sum(rep, there)
        cross(step).wait_recv()
        own[there] = mine + cross_in[there]

    @pl.loop(1, 4)
    def _(step):
        own_line(step)
        for turn in (4, 5, 3, 6, 2, 7, 1, 0):
            piece(step, turn).start()

    own_line(0)

    copies = Copies(send_sem, recv_sem)

    def plane(turn, part):
        return own.at[:, depth(turn), pl.ds(0, HALF), pl.ds(part * width, width)]

    def turn_a(turn, part, before):
        if turn == 0:
            return (
                copies.start(plane(4, part), ring_a.at[part, 0], right),
                copies.start(plane(5, part), ring_a.at[part, 4], left),
            )
        rightward, leftward = before
        rightward.wait_recv()
        ring_a[part, turn - 1] += plane(4 - turn, part)[...]
        rightward = copies.start(ring_a.at[part, turn - 1], ring_a.at[part, turn], right)
        if turn < 3:
            leftward.wait_recv()
            ring_a[part, 3 + turn] += plane(5 + turn, part)[...]
            leftward = copies.start(ring_a.at[part, 3 + turn], ring_a.at[part, 4 + turn], left)
        return rightward, leftward

    def along_lines(turn):
        for step in (1, 2, 3):
            piece(step, turn).wait_recv()
        here = depth(turn)
        return own[y, here, pl.ds(HALF, HALF), :] + (
            line_in[0, here] + line_in[1, here] + line_in[2, here]
        )

    def turn_b(turn, before):
        if turn == 0:
            own[y, depth(4), pl.ds(HALF, HALF), :] = along_lines(4)
            own[y, depth(5), pl.ds(HALF, HALF), :] = along_lines(5)
            return (
                copies.start(own.at[y, depth(4), pl.ds(HALF, HALF), :], ring_b.at[0], right),
                copies.start(own.at[y, depth(5), pl.ds(HALF, HALF), :], ring_b.at[4], left),
            )
        rightward, leftward = before
        mine = along_lines(4 - turn)
        rightward.wait_recv()
        ring_b[turn - 1] += mine
        rightward = copies.start(ring_b.at[turn - 1], ring_b.at[turn], right)
        if turn < 3:
            mine = along_lines(5 + turn)
            leftward.wait_recv()
            ring_b[3 + turn] += mine
            leftward = copies.start(ring_b.at[3 + turn], ring_b.at[4 + turn], left)
        return rightward, leftward

    flow_a, flow_b = [None, None], None
    for turn in range(4):
        for part in range(2):
            flow_a[part] = turn_a(turn, part, flow_a[part])
        if turn == 0:
            tokens_out[...] = columns(0)
        flow_b = turn_b(turn, flow_b)
    planes = []
    for part in range(2):
        for copy in flow_a[part]:
            copy.wait_recv()
        own[:, z, pl.ds(0, HALF), pl.ds(part * width, width)] = plane(0, part)[...] + (
            ring_a[part, 3] + ring_a[part, 6]
        )
        for step in (1, 3, 2):
            planes.append(copies.start(
                own.at[lax.rem(y + step, NY), z, pl.ds(0, HALF), pl.ds(part * width, width)],
                plane_in.at[part, step - 1],
                along_y(step),
            ))
    mine = along_lines(0)
    for copy in flow_b:
        copy.wait_recv()
    lower = mine + ring_b[3] + ring_b[6]
    qk_out[pl.ds(HALF, HALF), :] = lower[:, :width]
    value_out[pl.ds(HALF, HALF), :] = lower[:, width:]

    @pl.loop(1, 4)
    def _(step):
        sideways(step).wait()

    @pl.loop(0, length // 8)
    def _(block):
        here = pl.ds(pl.multiple_of(block * 8, 8), 8)
        tokens_out[here, :] += column_in[0, here, :] + column_in[1, here, :] + column_in[2, here, :]

    for copy in planes:
        copy.wait_recv()
    for part, out in enumerate((qk_out, value_out)):
        out[pl.ds(0, HALF), :] = own[y, z, pl.ds(0, HALF), pl.ds(part * width, width)] + (
            plane_in[part, 0] + plane_in[part, 1] + plane_in[part, 2]
        )

    @pl.loop(0, 4)
    def _(step):
        cross(step).wait_send()

    @pl.loop(1, 4)
    def _(step):
        for turn in range(NZ):
            piece(step, turn).wait_send()

    copies.finish()
    assert len(copies.all) == FINISH_COPIES


def finish(back_qk, back_value, slots, inputs, full):
    length, depth = inputs.shape
    both = full.shape[1]
    width = both // 2
    vmem, anywhere = pl.BlockSpec(memory_space=pltpu.VMEM), pl.BlockSpec(memory_space=pl.ANY)
    return pl.pallas_call(
        finish_kernel,
        out_shape=(
            jax.ShapeDtypeStruct((length, width), f32),
            jax.ShapeDtypeStruct((ROWS, width), f32),
            jax.ShapeDtypeStruct((ROWS, width), f32),
        ),
        in_specs=[vmem, vmem, vmem, anywhere, anywhere],
        out_specs=(vmem,) * 3,
        scratch_shapes=[
            pltpu.VMEM((length, depth), f32),
            pltpu.VMEM((depth, both), f32),
            pltpu.VMEM((length, both), bf16),
            pltpu.VMEM((length, both), bf16),
            pltpu.VMEM((3, length, width), f32),
            pltpu.VMEM((NY, NZ, ROWS, both), f32),
            pltpu.VMEM((NY, NZ, ROWS, both), f32),
            pltpu.VMEM((NY, NZ, ROWS, both), f32),
            pltpu.VMEM((3, length, width), f32),
            pltpu.VMEM((2, 7, NY, HALF, width), f32),
            pltpu.VMEM((7, HALF, both), f32),
            pltpu.VMEM((3, NZ, HALF, both), f32),
            pltpu.VMEM((2, 3, HALF, width), f32),
            pltpu.SemaphoreType.DMA((2,)),
            pltpu.SemaphoreType.DMA((FINISH_COPIES,)),
            pltpu.SemaphoreType.DMA((FINISH_COPIES,)),
            pltpu.SemaphoreType.DMA((3,)),
            pltpu.SemaphoreType.DMA((3,)),
            pltpu.SemaphoreType.DMA((4,)),
            pltpu.SemaphoreType.DMA((4,)),
            pltpu.SemaphoreType.DMA((3, NZ)),
            pltpu.SemaphoreType.DMA((3, NZ)),
        ],
        compiler_params=pltpu.CompilerParams(
            collective_id=3, has_side_effects=True, vmem_limit_bytes=52 * 2**20
        ),
        name="grads_and_scatter",
    )(back_qk, back_value, slots, inputs, full)


def exchange(array):
    return lax.all_to_all(array, "ctx", split_axis=0, concat_axis=0, tiled=True)


def seat_numbers(marks, room):
    marks = marks.astype(jnp.int32) - 1
    source = lax.broadcasted_iota(jnp.int32, marks.shape, 0) % GROUP
    seats = (marks // 3) * (3 * GROUP) + source * 3 + marks % 3
    return jnp.where(marks < 0, -1, seats).reshape(OWNERS // GROUP, 1, GROUP * room)


def snug_part(inputs, full, pay, early, slots, tall_slots):
    marks = early[:, ROOM : ROOM + 2, :ROOM]
    held, place = marks[:, 0], marks[:, 1]
    seats = jnp.where(held > 0.5, (held - 1) * (3 * GROUP) + place, -1.0).astype(jnp.int32)
    seats = seats.reshape(OWNERS // GROUP, 1, GROUP * ROOM)
    back = cluster_part(pay, slots, seats, early)
    back_qk, back_value = (rows.reshape(OWNERS * ROOM, HD) for rows in back)
    return finish(back_qk, back_value, tall_slots, inputs, full)


def roomy_part(inputs, full, upstream, cluster):
    heads, length = cluster.shape
    order = jnp.arange(length, dtype=jnp.int32)
    earlier = order[:, None] < order[None, :]
    alike = cluster[:, :, None] == cluster[:, None, :]
    within = jnp.sum((alike & earlier).astype(jnp.int32), axis=1)
    head = jnp.arange(heads, dtype=jnp.int32)[:, None]
    ids = (head * CL_DEV + cluster % CL_DEV) * 3 + within
    slots = cluster // CL_DEV * SLOTS + ids
    marks = jnp.zeros((OWNERS * SLOTS,), f32).at[slots.reshape(-1)].set(
        (ids + 1).astype(f32).reshape(-1)
    )
    rows = upstream.reshape(length, heads, HD).transpose(1, 0, 2).reshape(-1, HD)
    early = jnp.zeros((OWNERS * SLOTS, HD), f32).at[slots.reshape(-1)].set(rows)
    early = exchange(early.reshape(OWNERS, SLOTS, HD))
    marks = exchange(marks.reshape(OWNERS, SLOTS))
    rows = pack_rows(inputs, full, slots.reshape(1, -1), SLOTS)
    rows = exchange(rows.reshape(OWNERS, SLOTS, 2 * HD)).reshape(OWNERS * SLOTS, 2 * HD)
    replies = attend(rows, early, seat_numbers(marks, SLOTS), SLOTS)
    returned = exchange(replies.reshape(OWNERS, SLOTS, 2 * HD)).reshape(OWNERS * SLOTS, 2 * HD)
    return scatter_sums(
        *local_grads(returned[:, :HD], returned[:, HD:], slots.T, inputs, full)
    )


def per_device(tokens, qk_weight, value_weight, grad_out, assign):
    inputs = tokens[0]
    heads_here = qk_weight.shape[1] // HD
    width = heads_here * HD
    cluster = assign[:, 0, :, 0]
    full, early, slots, tall_slots, pay = gather_and_project(
        qk_weight, value_weight, jnp.pad(cluster, ((0, 8 - heads_here), (0, 0))), grad_out[0],
        inputs,
    )
    full = full.reshape(-1, 2 * width)
    fullest = jnp.max(early[:, ROOM, PITCH])

    def snug(inputs, full, upstream, cluster, *routed):
        return snug_part(inputs, full, *routed)

    def roomy(inputs, full, upstream, cluster, *routed):
        return roomy_part(inputs, full, upstream, cluster)

    grad_tokens, grad_qk_weight, grad_value_weight = lax.cond(
        fullest <= ROOM, snug, roomy,
        inputs, full, grad_out[0], cluster, pay, early, slots, tall_slots,
    )
    return (grad_tokens[None], grad_qk_weight, grad_value_weight)


def solution(mesh):
    in_specs = (
        P("rep", "ctx", None),
        P(("rep", "ctx"), "tp"),
        P(("rep", "ctx"), "tp"),
        P("rep", "ctx", "tp"),
        P("tp", "rep", "ctx", None),
    )
    out_specs = (P("rep", "ctx", "tp"), P(("rep", "ctx"), "tp"), P(("rep", "ctx"), "tp"))
    return jax.shard_map(
        per_device, mesh=mesh, in_specs=in_specs, out_specs=out_specs, check_vma=False
    )
```

```python
import jax
import jax.numpy as jnp
from jax import lax
from jax.experimental import pallas as pl
from jax.experimental.pallas import tpu as pltpu
from jax.sharding import PartitionSpec as P

HD = 128
CL_DEV = 8
NY = 4
NZ = 8
ROWS = 32
HALF = 16
MESH = pl.DeviceIdType.MESH

masked_score = -1e30
ROOM = 56
LANES = 128
GROUP = 8
SLOTS = 96
TALL = 768
f32, bf16 = jnp.float32, jnp.bfloat16
NN = (((1,), (0,)), ((), ()))
NT = (((1,), (1,)), ((), ()))
TN = (((0,), (0,)), ((), ()))
BIG = 48 * 2**20


def dot(left, right, dims=NN):
    return lax.dot_general(left, right, dims, preferred_element_type=f32)


def halves(matrix):
    upper = matrix.astype(bf16)
    return upper, (matrix - upper.astype(f32)).astype(bf16)


def dot3(left, right, dims=NN):
    a, b = left
    c, d = right
    first = jnp.concatenate([a, b, a], axis=dims[0][0][0])
    second = jnp.concatenate([c, c, d], axis=dims[0][1][0])
    return dot(first, second, dims)


def position():
    ctx = lax.axis_index("ctx")
    return lax.axis_index("rep"), lax.div(ctx, NZ), lax.rem(ctx, NZ)


def greet(partners):
    barrier = pltpu.get_barrier_semaphore()
    for partner in partners:
        pl.semaphore_signal(barrier, inc=1, device_id=partner, device_id_type=MESH)
    pl.semaphore_wait(barrier, len(partners))


class Copies:
    def __init__(self, send_sem, recv_sem):
        self.send_sem, self.recv_sem = send_sem, recv_sem
        self.all = []

    def start(self, source, target, device):
        index = len(self.all)
        copy = pltpu.make_async_remote_copy(
            src_ref=source,
            dst_ref=target,
            send_sem=self.send_sem.at[index],
            recv_sem=self.recv_sem.at[index],
            device_id=device,
            device_id_type=MESH,
        )
        copy.start()
        self.all.append(copy)
        return copy

    def finish(self):
        for copy in self.all:
            copy.wait_send()


GATHER_COPIES = 3 + 7 + 14 + 21 + 16 + 4
ROUTE_COPIES = 3 + 7 + 3 + 1
CLUSTERS = 256
OWNERS = 32
PITCH = 64


def count_rows(cluster_ref, heads):
    length = cluster_ref.shape[1]
    line = lax.broadcasted_iota(jnp.int32, (8, length), 0)
    counts = jnp.zeros((8, CLUSTERS), f32)
    for head in range(heads):
        counts += dot(one(line == head), members(cluster_ref, head), NT)
    return counts


def one(condition):
    return jnp.where(condition, 1.0, 0.0).astype(bf16)


def members(cluster_ref, head):
    length = cluster_ref.shape[1]
    label = lax.broadcasted_iota(jnp.int32, (CLUSTERS, length), 0)
    return one(label == cluster_ref[head : head + 1, :])


def deal_order(counts):
    lane = lax.broadcasted_iota(jnp.int32, counts.shape, 1)
    return counts * CLUSTERS + (CLUSTERS - 1 - lane).astype(f32)


def route_head(cluster_ref, head, keys, tall_keys, earlier, base):
    larger = jnp.where(tall_keys[:, head : head + 1] > keys[head : head + 1, :], 1.0, 0.0)
    place = jnp.sum(larger, axis=0, keepdims=True).astype(jnp.int32)
    turn = place // OWNERS
    seat = place % OWNERS
    seat = jnp.where(turn % 2 == 0, seat, OWNERS - 1 - seat)
    seat = (seat + 8 * head) % OWNERS
    line = lax.broadcasted_iota(jnp.int32, (8, CLUSTERS), 0)
    table = jnp.where(line == 0, seat, jnp.where(line == 1, turn, 0)).astype(f32).astype(bf16)
    chosen = members(cluster_ref, head)
    looked = dot(table, chosen).astype(jnp.int32)
    owner, turn = looked[0:1, :], looked[1:2, :]
    within = jnp.sum(chosen.astype(f32) * dot(chosen, earlier), axis=0, keepdims=True)
    label = lax.broadcasted_iota(jnp.int32, (OWNERS, owner.shape[1]), 0)
    owned = one(label == owner)
    many = owned.astype(f32)
    rank = jnp.sum(many * (dot(owned, earlier) + base), axis=0, keepdims=True)
    base = base + jnp.sum(many, axis=1, keepdims=True)
    return owner, rank.astype(jnp.int32), head * CL_DEV + turn, within, base


def gather_kernel(
    qk_ref, value_ref, cluster_ref, grad_ref, tokens_ref,
    full_ref, early_ref, slots_ref, tall_slots_ref, pay_ref,
    out_ref, tokens, acc, counts_y, counts_z, most, ids_row, slots_row, pay, early_out,
    local_sem, send_sem, recv_sem, route_send, route_recv, early_send, early_recv,
):
    rep, y, z = position()
    me = lax.axis_index("ctx")
    x = lax.axis_index("tp")
    width = qk_ref.shape[1]
    heads = width // HD
    length = cluster_ref.shape[1]

    def along_y(step):
        return {"ctx": lax.rem(y + step, NY) * NZ + z}

    def along_z(step):
        return {"ctx": y * NZ + lax.rem(z + step, NZ)}

    def along_x(step):
        return {"tp": lax.rem(x + step, 4)}

    def around(step):
        return {"ctx": lax.rem(me + step, OWNERS)}

    def plane(step, part):
        there = pl.ds(part * width, width)
        return out_ref.at[rep, :, lax.rem(z + step, NZ), pl.ds(0, HALF), there]

    def piece(step):
        return out_ref.at[rep, y, lax.rem(z + step, NZ), pl.ds(HALF, HALF), :]

    def line(step):
        return out_ref.at[rep, lax.rem(y + step, NY), :, pl.ds(HALF, HALF), :]

    right, left, other = along_z(1), along_z(NZ - 1), {"rep": 1 - rep}
    mine = out_ref.at[rep, y, z]
    fetch = pltpu.make_async_copy(tokens_ref, tokens, local_sem.at[2])
    fetch.start()
    first = pltpu.make_async_copy(qk_ref, mine.at[:, pl.ds(0, width)], local_sem.at[0])
    second = pltpu.make_async_copy(value_ref, mine.at[:, pl.ds(width, width)], local_sem.at[1])
    first.start()
    second.start()
    barrier = pltpu.get_barrier_semaphore()

    @pl.loop(1, OWNERS)
    def _(step):
        pl.semaphore_signal(barrier, inc=1, device_id=around(step), device_id_type=MESH)

    for partner in (other, along_x(1), along_x(2), along_x(3)):
        pl.semaphore_signal(barrier, inc=1, device_id=partner, device_id_type=MESH)
    counts_y[0] = count_rows(cluster_ref, heads)
    pl.semaphore_wait(barrier, OWNERS - 1 + 4)

    routes = Copies(route_send, route_recv)
    counted = [
        routes.start(counts_y.at[0], counts_y.at[step], along_y(step)) for step in (1, 2, 3)
    ]
    first.wait()
    second.wait()
    copies = Copies(send_sem, recv_sem)
    shared = [copies.start(mine, mine, along_y(step)) for step in (1, 3, 2)]
    pieces = [(copies.start(piece(0), piece(0), right), copies.start(piece(0), piece(0), left))]

    for head in range(heads):
        upper, lower = halves(grad_ref[:, head * HD : (head + 1) * HD])
        pay[pl.ds(head * length, length), :HD] = upper
        pay[pl.ds(head * length, length), HD:] = lower

    for copy in counted:
        copy.wait_recv()
    counts_z[0] = counts_y[0] + counts_y[1] + counts_y[2] + counts_y[3]
    counted = [
        routes.start(counts_z.at[0], counts_z.at[step], along_z(step)) for step in range(1, NZ)
    ]
    for copy in shared:
        copy.wait_recv()
    planes = []
    for part in range(2):
        here = plane(0, part)
        planes.append([(copies.start(here, here, right), copies.start(here, here, left))])
    across = [copies.start(plane(0, part), plane(0, part), other) for part in range(2)]
    passed = {1: [], 2: [], 3: []}

    def pass_on(here):
        for step in (1, 3, 2):
            passed[step].append(copies.start(here, here, along_y(step)))

    def turn_pieces(step):
        rightward, leftward = pieces[step]
        after, before = piece(NZ - 1 - step), piece(1 + step)
        rightward.wait_recv()
        if leftward is not None:
            leftward.wait_recv()
        if step < 3:
            pieces.append((
                copies.start(after, after, right),
                copies.start(before, before, left) if step < 2 else None,
            ))
        pass_on(after)
        if leftward is not None:
            pass_on(before)

    def turn_planes(step):
        for part in range(2):
            turn_plane(step, part)

    def turn_plane(step, part):
        rightward, leftward = planes[part][step]
        after, before = plane(NZ - 1 - step, part), plane(1 + step, part)
        rightward.wait_recv()
        if step < 3:
            going = copies.start(after, after, right)
        if leftward is not None:
            leftward.wait_recv()
            coming = copies.start(before, before, left) if step < 2 else None
        if step < 3:
            planes[part].append((going, coming if step < 2 else None))
        across.append(copies.start(after, after, other))
        if leftward is not None:
            across.append(copies.start(before, before, other))

    turn_pieces(0)
    for copy in counted:
        copy.wait_recv()
    total = counts_z[0]
    for step in range(1, NZ):
        total += counts_z[step]
    keys = deal_order(total)
    tall_keys = jnp.concatenate([keys] + [jnp.zeros_like(keys)] * 15, axis=0).T
    earlier = one(
        lax.broadcasted_iota(jnp.int32, (length, length), 0)
        < lax.broadcasted_iota(jnp.int32, (length, length), 1)
    )
    base = jnp.zeros((OWNERS, 1), f32)
    highest = jnp.zeros((1, 1), f32)
    row = lax.broadcasted_iota(jnp.int32, (8, length), 0)
    slots_list = []
    for head in range(heads):
        owner, rank, held, within, base = route_head(
            cluster_ref, head, keys, tall_keys, earlier, base
        )
        highest = jnp.maximum(highest, jnp.max(rank.astype(f32), axis=1, keepdims=True) + 1)
        here = pl.ds(head * length, length)
        slots_ref[:, here] = jnp.where(rank < ROOM, owner * ROOM + rank, -1)
        slots_row[:, here] = jnp.where(rank < ROOM, owner * PITCH + rank, -1)
        within = within + (3 * lax.rem(me, GROUP)).astype(f32)
        marked = jnp.where(row == 0, (held + 1).astype(f32), jnp.where(row == 1, within, 0.0))
        ids_row[:, here] = marked.astype(bf16)
        slots_list.append(jnp.where(rank < ROOM, owner * ROOM + rank, -1))
    most[0] = jnp.broadcast_to(highest, (8, LANES))
    tall = jnp.concatenate(
        slots_list + [jnp.zeros((LANES - heads, length), jnp.int32)], axis=0
    )
    tall_slots_ref[...] = tall.astype(f32).T.astype(jnp.int32)
    fullest = [routes.start(most.at[0], most.at[step], along_x(step)) for step in (1, 2, 3)]
    turn_pieces(1)
    turn_planes(0)

    def pack_early(block):
        rows = 4 * PITCH
        place = lax.broadcasted_iota(jnp.int32, (rows, heads * length), 0) + block * rows
        chosen = one(place == slots_row[...])
        both = dot(chosen, pay[...])
        both = both[:, :HD] + both[:, HD:]
        marks = dot(ids_row[...], chosen, NT)
        for lane in range(4):
            early_out[block * 4 + lane] = both[lane * PITCH : (lane + 1) * PITCH]
            early_out[block * 4 + lane, pl.ds(ROOM, 8), pl.ds(0, PITCH)] = marks[
                :, lane * PITCH : (lane + 1) * PITCH
            ]

    @pl.loop(0, OWNERS // 8)
    def _(block):
        pack_early(block)

    for copy in fullest:
        copy.wait_recv()
    most[4] = jnp.maximum(jnp.maximum(most[0], most[1]), jnp.maximum(most[2], most[3]))
    fullest = routes.start(most.at[4], most.at[5], other)
    turn_pieces(2)

    @pl.loop(OWNERS // 8, OWNERS // 4)
    def _(block):
        pack_early(block)

    turn_pieces(3)
    turn_planes(1)
    across.append(copies.start(line(0), line(0), other))
    fullest.wait_recv()
    overall = jnp.maximum(most[4], most[5])[:, :PITCH]

    @pl.loop(0, OWNERS)
    def _(block):
        early_out[block, pl.ds(ROOM, 8), pl.ds(PITCH, PITCH)] = overall

    def early(step):
        there = lax.rem(me + step, OWNERS)
        return pltpu.make_async_remote_copy(
            src_ref=early_out.at[there],
            dst_ref=early_ref.at[me],
            send_sem=early_send.at[step],
            recv_sem=early_recv.at[step],
            device_id={"ctx": there},
            device_id_type=MESH,
        )

    @pl.loop(1, OWNERS // 2)
    def _(step):
        early(step).start()

    stay = pltpu.make_async_copy(early_out.at[me], early_ref.at[me], local_sem.at[0])
    stay.start()
    turn_planes(2)
    turn_planes(3)

    @pl.loop(OWNERS // 2, OWNERS)
    def _(step):
        early(step).start()

    for step in (1, 3, 2):
        for copy in passed[step]:
            copy.wait_recv()
        across.append(copies.start(line(NY - step), line(NY - step), other))
    fetch.wait()

    def project(half, there):
        start = pl.multiple_of((half * NY + there) * (NZ * ROWS), NZ * ROWS)
        some = halves(tokens[:, pl.ds(start, NZ * ROWS)])
        return dot3(some, halves(out_ref[half, there].reshape(NZ * ROWS, 2 * width)))

    acc[...] = project(rep, 0)

    @pl.loop(1, NY)
    def _(there):
        acc[...] += project(rep, there)

    for copy in across:
        copy.wait_recv()
    save = pltpu.make_async_copy(out_ref, full_ref, local_sem.at[1])
    save.start()

    @pl.loop(0, NY)
    def _(there):
        acc[...] += project(1 - rep, there)

    for part in range(2):
        for head in range(heads):
            here = pl.ds(head * length, length)
            column = part * width + head * HD
            upper, lower = halves(acc[:, column : column + HD])
            pay_ref[part, here, :HD] = upper
            pay_ref[part, here, HD:] = lower
    copies.finish()
    routes.finish()
    stay.wait()
    save.wait()

    @pl.loop(1, OWNERS)
    def _(step):
        early(step).wait()

    assert len(copies.all) == GATHER_COPIES and len(routes.all) == ROUTE_COPIES


def gather_and_project(qk_weight, value_weight, clusters, upstream, inputs):
    width = qk_weight.shape[1]
    length = clusters.shape[1]
    rows = width // HD * length
    vmem, anywhere = pl.BlockSpec(memory_space=pltpu.VMEM), pl.BlockSpec(memory_space=pl.ANY)
    return pl.pallas_call(
        gather_kernel,
        out_shape=(
            jax.ShapeDtypeStruct((2, NY, NZ, ROWS, 2 * width), f32),
            jax.ShapeDtypeStruct((OWNERS, PITCH, HD), f32),
            jax.ShapeDtypeStruct((1, rows), jnp.int32),
            jax.ShapeDtypeStruct((length, LANES), jnp.int32),
            jax.ShapeDtypeStruct((2, rows, 2 * HD), bf16),
        ),
        in_specs=[anywhere, anywhere, vmem, vmem, anywhere],
        out_specs=(anywhere, anywhere, vmem, vmem, vmem),
        scratch_shapes=[
            pltpu.VMEM((2, NY, NZ, ROWS, 2 * width), f32),
            pltpu.VMEM(inputs.shape, f32),
            pltpu.VMEM((length, 2 * width), f32),
            pltpu.VMEM((NY, 8, CLUSTERS), f32),
            pltpu.VMEM((NZ, 8, CLUSTERS), f32),
            pltpu.VMEM((6, 8, LANES), f32),
            pltpu.VMEM((8, rows), bf16),
            pltpu.VMEM((1, rows), jnp.int32),
            pltpu.VMEM((rows, 2 * HD), bf16),
            pltpu.VMEM((OWNERS, PITCH, HD), f32),
            pltpu.SemaphoreType.DMA((3,)),
            pltpu.SemaphoreType.DMA((GATHER_COPIES,)),
            pltpu.SemaphoreType.DMA((GATHER_COPIES,)),
            pltpu.SemaphoreType.DMA((ROUTE_COPIES,)),
            pltpu.SemaphoreType.DMA((ROUTE_COPIES,)),
            pltpu.SemaphoreType.DMA((OWNERS,)),
            pltpu.SemaphoreType.DMA((OWNERS,)),
        ],
        compiler_params=pltpu.CompilerParams(
            collective_id=0, has_side_effects=True, vmem_limit_bytes=BIG
        ),
        name="gather_and_project",
    )(qk_weight, value_weight, clusters, upstream, inputs)


SCATTER_COPIES = 3 + 12 + 7 + 3 + 7 + 3


def scatter_kernel(
    terms_ref, sums_ref, tokens_out, qk_out, value_out,
    column_in, cross_in, ring_a, ring_b, line_in, plane_in,
    local_sem, send_sem, recv_sem,
):
    rep, y, z = position()
    x = lax.axis_index("tp")
    width = qk_out.shape[1]

    def along_y(step):
        return {"ctx": lax.rem(y + step, NY) * NZ + z}

    def along_z(step):
        return {"ctx": y * NZ + lax.rem(z + step, NZ)}

    def along_x(step):
        return {"tp": lax.rem(x + step, 4)}

    def columns(step):
        start = pl.multiple_of(lax.rem(x + step, 4) * width, width)
        return terms_ref.at[:, pl.ds(start, width)]

    def plane(step):
        return cross_in.at[:, lax.rem(z + step, NZ), pl.ds(0, HALF), :]

    def line(step):
        return cross_in.at[lax.rem(y + step, NY), :, pl.ds(HALF, HALF), :]

    def piece(step):
        return cross_in.at[y, lax.rem(z + step, NZ), pl.ds(HALF, HALF), :]

    right, left, other = along_z(1), along_z(NZ - 1), {"rep": 1 - rep}
    greet(
        [along_y(1), along_y(2), along_y(3), right, left, other]
        + [along_x(1), along_x(2), along_x(3)]
    )
    copies = Copies(send_sem, recv_sem)
    sideways = [
        copies.start(columns(step), column_in.at[step - 1], along_x(step)) for step in (1, 3, 2)
    ]
    own_columns = pltpu.make_async_copy(columns(0), tokens_out, local_sem)
    own_columns.start()

    cross = {}
    for kind, step in (
        ("a", 4), ("a", 5), ("b", 1), ("b", 3), ("b", 2), ("a", 3),
        ("a", 6), ("a", 2), ("a", 7), ("b", 0), ("a", 1), ("a", 0),
    ):
        if kind == "a":
            there = lax.rem(z + step, NZ)
            source = sums_ref.at[1 - rep, :, there, pl.ds(0, HALF), :]
            cross[kind, step] = copies.start(source, plane(step), other)
        else:
            there = lax.rem(y + step, NY)
            source = sums_ref.at[1 - rep, there, :, pl.ds(HALF, HALF), :]
            cross[kind, step] = copies.start(source, line(step), other)

    def add_plane(step):
        cross["a", step].wait_recv()
        there = lax.rem(z + step, NZ)
        cross_in[:, there, pl.ds(0, HALF), :] += sums_ref[rep, :, there, pl.ds(0, HALF), :]

    def add_line(step):
        cross["b", step].wait_recv()
        there = lax.rem(y + step, NY)
        cross_in[there, :, pl.ds(HALF, HALF), :] += sums_ref[
            rep, there, :, pl.ds(HALF, HALF), :
        ]

    add_plane(4)
    right_a = copies.start(plane(4), ring_a.at[0], right)
    add_plane(5)
    left_a = copies.start(plane(5), ring_a.at[4], left)
    lines = []
    for step in (1, 3, 2):
        add_line(step)
        lines.append(copies.start(line(step), line_in.at[step - 1], along_y(step)))

    def pass_a(turn):
        nonlocal right_a, left_a
        add_plane(4 - turn)
        right_a.wait_recv()
        ring_a[turn - 1] += cross_in[:, lax.rem(z + 4 - turn, NZ), pl.ds(0, HALF), :]
        right_a = copies.start(ring_a.at[turn - 1], ring_a.at[turn], right)
        if turn < 3:
            add_plane(5 + turn)
            left_a.wait_recv()
            ring_a[3 + turn] += cross_in[:, lax.rem(z + 5 + turn, NZ), pl.ds(0, HALF), :]
            left_a = copies.start(ring_a.at[3 + turn], ring_a.at[4 + turn], left)

    pass_a(1)
    add_line(0)
    pass_a(2)
    for copy in lines:
        copy.wait_recv()
    cross_in[y, :, pl.ds(HALF, HALF), :] += line_in[0] + line_in[1] + line_in[2]
    right_b = copies.start(piece(4), ring_b.at[0], right)
    left_b = copies.start(piece(5), ring_b.at[4], left)
    pass_a(3)

    def pass_b(turn):
        nonlocal right_b, left_b
        right_b.wait_recv()
        ring_b[turn - 1] += cross_in[y, lax.rem(z + 4 - turn, NZ), pl.ds(HALF, HALF), :]
        right_b = copies.start(ring_b.at[turn - 1], ring_b.at[turn], right)
        if turn < 3:
            left_b.wait_recv()
            ring_b[3 + turn] += cross_in[y, lax.rem(z + 5 + turn, NZ), pl.ds(HALF, HALF), :]
            left_b = copies.start(ring_b.at[3 + turn], ring_b.at[4 + turn], left)

    pass_b(1)
    pass_b(2)
    add_plane(0)
    right_a.wait_recv()
    left_a.wait_recv()
    cross_in[:, z, pl.ds(0, HALF), :] += ring_a[3] + ring_a[6]
    planes = [
        copies.start(
            cross_in.at[lax.rem(y + step, NY), z, pl.ds(0, HALF), :],
            plane_in.at[step - 1],
            along_y(step),
        )
        for step in (1, 3, 2)
    ]
    pass_b(3)
    right_b.wait_recv()
    left_b.wait_recv()
    lower = cross_in[y, z, pl.ds(HALF, HALF), :] + ring_b[3] + ring_b[6]
    qk_out[pl.ds(HALF, HALF), :] = lower[:, :width]
    value_out[pl.ds(HALF, HALF), :] = lower[:, width:]
    for copy in planes:
        copy.wait_recv()
    upper = cross_in[y, z, pl.ds(0, HALF), :] + plane_in[0] + plane_in[1] + plane_in[2]
    qk_out[pl.ds(0, HALF), :] = upper[:, :width]
    value_out[pl.ds(0, HALF), :] = upper[:, width:]
    own_columns.wait()
    for copy in sideways:
        copy.wait_recv()

    @pl.loop(0, tokens_out.shape[0] // 8)
    def _(block):
        here = pl.ds(pl.multiple_of(block * 8, 8), 8)
        tokens_out[here, :] += column_in[0, here, :] + column_in[1, here, :] + column_in[2, here, :]

    copies.finish()
    assert len(copies.all) == SCATTER_COPIES


def scatter_sums(token_terms, weight_terms):
    length = token_terms.shape[0]
    both = weight_terms.shape[1]
    width = both // 2
    return pl.pallas_call(
        scatter_kernel,
        out_shape=(
            jax.ShapeDtypeStruct((length, width), f32),
            jax.ShapeDtypeStruct((ROWS, width), f32),
            jax.ShapeDtypeStruct((ROWS, width), f32),
        ),
        in_specs=[pl.BlockSpec(memory_space=pl.ANY), pl.BlockSpec(memory_space=pltpu.VMEM)],
        out_specs=(pl.BlockSpec(memory_space=pltpu.VMEM),) * 3,
        scratch_shapes=[
            pltpu.VMEM((3, length, width), f32),
            pltpu.VMEM((NY, NZ, ROWS, both), f32),
            pltpu.VMEM((7, NY, HALF, both), f32),
            pltpu.VMEM((7, HALF, both), f32),
            pltpu.VMEM((3, NZ, HALF, both), f32),
            pltpu.VMEM((3, HALF, both), f32),
            pltpu.SemaphoreType.DMA,
            pltpu.SemaphoreType.DMA((SCATTER_COPIES,)),
            pltpu.SemaphoreType.DMA((SCATTER_COPIES,)),
        ],
        compiler_params=pltpu.CompilerParams(
            collective_id=1, has_side_effects=True, vmem_limit_bytes=48 * 2**20
        ),
        name="scatter_sums",
    )(token_terms, weight_terms.reshape(2, NY, NZ, ROWS, both))


def pack_kernel(tokens_ref, full_ref, slots_ref, rows_ref, acc, pay):
    step = pl.program_id(0)
    length, both = acc.shape
    rows = rows_ref.shape[0]

    @pl.when(step == 0)
    def _():
        acc[...] = jnp.zeros_like(acc)

    @pl.when(step < 8)
    def _():
        acc[...] += dot3(halves(tokens_ref[...]), halves(full_ref[...]))

    @pl.when(step == 7)
    def _():
        for head in range(both // (2 * HD)):
            here = pl.ds(head * length, length)
            for part in range(2):
                column = part * both // 2 + head * HD
                upper, lower = halves(acc[:, column : column + HD])
                pay[here, part * HD : (part + 1) * HD] = upper
                pay[here, (2 + part) * HD : (3 + part) * HD] = lower

    @pl.when(step >= 8)
    def _():
        place = lax.broadcasted_iota(jnp.int32, (rows, slots_ref.shape[1]), 0) + (step - 8) * rows
        moved = dot(one(place == slots_ref[...]), pay[...])
        rows_ref[...] = moved[:, : 2 * HD] + moved[:, 2 * HD :]


def pack_rows(inputs, full, slots, room):
    length, depth = inputs.shape
    both = full.shape[1]
    total = slots.shape[1]
    return pl.pallas_call(
        pack_kernel,
        grid=(16,),
        out_shape=jax.ShapeDtypeStruct((OWNERS * room, 2 * HD), f32),
        in_specs=[
            pl.BlockSpec((length, depth // 8), lambda i: (0, jnp.minimum(i, 7))),
            pl.BlockSpec((depth // 8, both), lambda i: (jnp.minimum(i, 7), 0)),
            pl.BlockSpec((1, total), lambda i: (0, 0)),
        ],
        out_specs=pl.BlockSpec((4 * room, 2 * HD), lambda i: (jnp.maximum(i - 8, 0), 0)),
        scratch_shapes=[pltpu.VMEM((length, both), f32), pltpu.VMEM((total, 4 * HD), bf16)],
        compiler_params=pltpu.CompilerParams(vmem_limit_bytes=BIG),
        name="project_and_pack",
    )(inputs, full, slots)


def attend_kernel(marks_ref, rows_ref, early_ref, replies_ref, spread, seats, valid, answer):
    groups = marks_ref.shape[0]
    wide = marks_ref.shape[2]
    owned = spread.shape[1]
    seat = spread.shape[2]
    size = groups * seat

    @pl.loop(0, groups)
    def _(group):
        here = pl.ds(pl.multiple_of(group * wide, wide), wide)
        place = lax.broadcasted_iota(jnp.int32, (TALL, wide), 0)
        chosen = one(place == marks_ref[group])
        seats[group] = chosen
        upper, lower = halves(rows_ref[here, :])
        early = early_ref[pl.ds(group * GROUP, GROUP), pl.ds(0, wide // GROUP), :]
        early_upper, early_lower = halves(early.reshape(wide, HD))
        present = jnp.ones((wide, LANES), bf16)
        moved = dot(
            chosen, jnp.concatenate([upper, early_upper, lower, early_lower, present], axis=1)
        )
        spread[group] = (moved[:, : 3 * HD] + moved[:, 3 * HD : 6 * HD]).reshape(owned, seat, 3 * HD)
        valid[group] = moved[:, 6 * HD :].reshape(owned, seat, LANES)

    @pl.loop(0, owned // 4)
    def _(block):
        for lane in range(4):
            index = block * 4 + lane
            rows = spread[:, index].reshape(size, 3 * HD)
            present = valid[:, index].reshape(size, LANES)[:, :size] > 0.5
            qk = halves(rows[:, :HD])
            value = halves(rows[:, HD : 2 * HD])
            upstream = halves(rows[:, 2 * HD :])
            scores = jnp.where(present, dot3(qk, qk, NT) / HD, masked_score)
            weights = jnp.exp(scores - jnp.max(scores, axis=0, keepdims=True))
            weights = weights / jnp.sum(weights, axis=0, keepdims=True)
            slopes = dot3(value, upstream, NT)
            middle = jnp.sum(weights * slopes, axis=0, keepdims=True)
            slopes = weights * (slopes - middle)
            grad_qk = dot3(halves(slopes + slopes.T), qk) / HD
            grad_value = dot3(halves(weights), upstream)
            answer[:, index] = jnp.concatenate([grad_qk, grad_value], axis=1).reshape(
                groups, seat, 2 * HD
            )

    @pl.loop(0, groups)
    def _(group):
        here = pl.ds(pl.multiple_of(group * wide, wide), wide)
        upper, lower = halves(answer[group].reshape(TALL, 2 * HD))
        moved = dot(seats[group], jnp.concatenate([upper, lower], axis=1), TN)
        replies_ref[here, :] = moved[:, : 2 * HD] + moved[:, 2 * HD :]


def attend(rows, early, marks, room):
    groups = OWNERS // GROUP
    owned = TALL // (3 * GROUP)
    seat = 3 * GROUP
    return pl.pallas_call(
        attend_kernel,
        out_shape=jax.ShapeDtypeStruct((OWNERS * room, 2 * HD), f32),
        in_specs=[pl.BlockSpec(memory_space=pltpu.VMEM)] * 3,
        out_specs=pl.BlockSpec(memory_space=pltpu.VMEM),
        scratch_shapes=[
            pltpu.VMEM((groups, owned, seat, 3 * HD), f32),
            pltpu.VMEM((groups, TALL, GROUP * room), bf16),
            pltpu.VMEM((groups, owned, seat, LANES), f32),
            pltpu.VMEM((groups, owned, seat, 2 * HD), f32),
        ],
        compiler_params=pltpu.CompilerParams(vmem_limit_bytes=BIG),
        name="attend",
    )(marks, rows, early)


QK, VALUE, GRAD_VALUE, GRAD_QK = range(4)


def cluster_kernel(
    pay_ref, slots_ref, marks_ref, early_ref, back_qk_ref, back_value_ref,
    leaving, landed, seats, spread, valid, weights, answer,
    local_sem, send_sem, recv_sem,
):
    me = lax.axis_index("ctx")
    groups, _, wide = marks_ref.shape
    owned, seat = spread.shape[2], spread.shape[3]
    size = groups * seat
    rows = 4 * ROOM

    barrier = pltpu.get_barrier_semaphore()

    @pl.loop(1, OWNERS)
    def _(step):
        there = {"ctx": lax.rem(me + step, OWNERS)}
        pl.semaphore_signal(barrier, inc=1, device_id=there, device_id_type=MESH)

    def target(kind):
        if kind == GRAD_QK:
            return back_qk_ref
        return back_value_ref if kind == GRAD_VALUE else landed.at[kind]

    def remote(kind, step):
        there = lax.rem(me + step, OWNERS)
        return pltpu.make_async_remote_copy(
            src_ref=leaving.at[kind, there],
            dst_ref=target(kind).at[me],
            send_sem=send_sem.at[kind, step],
            recv_sem=recv_sem.at[kind, step],
            device_id={"ctx": there},
            device_id_type=MESH,
        )

    def stay(kind):
        return pltpu.make_async_copy(leaving.at[kind, me], target(kind).at[me], local_sem.at[kind])

    def start(kind, there):
        @pl.when(there == me)
        def _():
            stay(kind).start()

        @pl.when(there != me)
        def _():
            remote(kind, lax.rem(there - me + OWNERS, OWNERS)).start()

    def arrive(kind):
        stay(kind).wait()

        @pl.loop(1, OWNERS)
        def _(step):
            remote(kind, step).wait_recv()

    def pack(kind, block):
        place = lax.broadcasted_iota(jnp.int32, (rows, slots_ref.shape[1]), 0) + block * rows
        moved = dot(one(place == slots_ref[...]), pay_ref[kind])
        moved = moved[:, :HD] + moved[:, HD:]
        for lane in range(4):
            leaving[kind, block * 4 + lane] = moved[lane * ROOM : (lane + 1) * ROOM]

    def take(kind, group, source):
        upper, lower = halves(source)
        moved = dot(seats[group], jnp.concatenate([upper, lower], axis=1))
        spread[kind, group] = (moved[:, :HD] + moved[:, HD:]).reshape(owned, seat, HD)

    def give(kind):
        @pl.loop(0, groups)
        def _(index):
            group = lax.rem(lax.div(me, GROUP) + index, groups)
            upper, lower = halves(answer[group].reshape(TALL, HD))
            moved = dot(seats[group], jnp.concatenate([upper, lower], axis=1), TN)
            moved = (moved[:, :HD] + moved[:, HD:]).reshape(GROUP, ROOM, HD)
            leaving[kind, pl.ds(group * GROUP, GROUP)] = moved
            for lane in range(GROUP):
                start(kind, group * GROUP + lane)

    def first_block():
        return lax.div(me, 4)

    pack(QK, first_block())
    pl.semaphore_wait(barrier, OWNERS - 1)
    for lane in range(4):
        start(QK, first_block() * 4 + lane)

    @pl.loop(1, OWNERS // 4)
    def _(index):
        block = lax.rem(first_block() + index, OWNERS // 4)
        pack(QK, block)
        for lane in range(4):
            start(QK, block * 4 + lane)

    @pl.loop(0, OWNERS // 4)
    def _(block):
        pack(VALUE, block)

    @pl.loop(0, groups)
    def _(group):
        place = lax.broadcasted_iota(jnp.int32, (TALL, wide), 0)
        chosen = one(place == marks_ref[group])
        seats[group] = chosen
        early = early_ref[pl.ds(group * GROUP, GROUP), pl.ds(0, ROOM), :].reshape(wide, HD)
        upper, lower = halves(early)
        present = jnp.ones((wide, LANES), bf16)
        moved = dot(chosen, jnp.concatenate([upper, lower, present], axis=1))
        spread[2, group] = (moved[:, :HD] + moved[:, HD : 2 * HD]).reshape(owned, seat, HD)
        valid[group] = moved[:, 2 * HD :].reshape(owned, seat, LANES)

    arrive(QK)

    @pl.loop(0, OWNERS)
    def _(index):
        start(VALUE, lax.rem(me + index, OWNERS))

    @pl.loop(0, groups)
    def _(group):
        take(QK, group, landed[QK, pl.ds(group * GROUP, GROUP)].reshape(wide, HD))

    def cluster(kind, index):
        return halves(spread[kind, :, index].reshape(size, HD))

    @pl.loop(0, owned // 4)
    def _(block):
        for lane in range(4):
            index = block * 4 + lane
            present = valid[:, index].reshape(size, LANES)[:, :size] > 0.5
            qk = cluster(QK, index)
            scores = jnp.where(present, dot3(qk, qk, NT) / HD, masked_score)
            raised = jnp.exp(scores - jnp.max(scores, axis=0, keepdims=True))
            raised = raised / jnp.sum(raised, axis=0, keepdims=True)
            weights[index] = raised
            answer[:, index] = dot3(halves(raised), cluster(2, index)).reshape(groups, seat, HD)

    give(GRAD_VALUE)
    arrive(VALUE)

    @pl.loop(0, groups)
    def _(group):
        take(VALUE, group, landed[VALUE, pl.ds(group * GROUP, GROUP)].reshape(wide, HD))

    @pl.loop(0, owned // 4)
    def _(block):
        for lane in range(4):
            index = block * 4 + lane
            raised = weights[index]
            slopes = dot3(cluster(VALUE, index), cluster(2, index), NT)
            middle = jnp.sum(raised * slopes, axis=0, keepdims=True)
            slopes = raised * (slopes - middle)
            grad_qk = dot3(halves(slopes + slopes.T), cluster(QK, index)) / HD
            answer[:, index] = grad_qk.reshape(groups, seat, HD)

    give(GRAD_QK)
    arrive(GRAD_VALUE)
    arrive(GRAD_QK)

    @pl.loop(1, OWNERS)
    def _(step):
        for kind in range(4):
            remote(kind, step).wait_send()


def cluster_part(pay, slots, marks, early):
    groups = OWNERS // GROUP
    owned = TALL // (3 * GROUP)
    seat = 3 * GROUP
    size = groups * seat
    rows = jax.ShapeDtypeStruct((OWNERS, ROOM, HD), f32)
    return pl.pallas_call(
        cluster_kernel,
        out_shape=(rows, rows),
        in_specs=[pl.BlockSpec(memory_space=pltpu.VMEM)] * 4,
        out_specs=(pl.BlockSpec(memory_space=pl.ANY),) * 2,
        scratch_shapes=[
            pltpu.VMEM((4, OWNERS, ROOM, HD), f32),
            pltpu.VMEM((2, OWNERS, ROOM, HD), f32),
            pltpu.VMEM((groups, TALL, GROUP * ROOM), bf16),
            pltpu.VMEM((3, groups, owned, seat, HD), f32),
            pltpu.VMEM((groups, owned, seat, LANES), f32),
            pltpu.VMEM((owned, size, size), f32),
            pltpu.VMEM((groups, owned, seat, HD), f32),
            pltpu.SemaphoreType.DMA((4,)),
            pltpu.SemaphoreType.DMA((4, OWNERS)),
            pltpu.SemaphoreType.DMA((4, OWNERS)),
        ],
        compiler_params=pltpu.CompilerParams(
            collective_id=2, has_side_effects=True, vmem_limit_bytes=BIG
        ),
        name="exchange_and_attend",
    )(pay, slots, marks, early)


def grads_kernel(
    back_qk_ref, back_value_ref, slots_ref, tokens_ref, full_ref, terms_ref, sums_ref, high, low
):
    length = tokens_ref.shape[0]
    width = high.shape[1] // 2
    total = back_qk_ref.shape[0]

    @pl.when(pl.program_id(0) == 0)
    def _():
        qk_upper, qk_lower = halves(back_qk_ref[...])
        upper, lower = halves(back_value_ref[...])
        source = jnp.concatenate([qk_upper, upper, qk_lower, lower], axis=1)
        for head in range(width // HD):
            place = lax.broadcasted_iota(jnp.int32, (length, total), 1)
            chosen = one(place == slots_ref[:, head : head + 1])
            both = dot(chosen, source)
            upper, lower = halves(both[:, : 2 * HD] + both[:, 2 * HD :])
            for part in range(2):
                there = pl.ds(part * width + head * HD, HD)
                high[:, there] = upper[:, part * HD : (part + 1) * HD]
                low[:, there] = lower[:, part * HD : (part + 1) * HD]

    combined = high[...], low[...]
    terms_ref[...] = dot3(combined, halves(full_ref[...]), NT)
    sums_ref[...] = dot3(halves(tokens_ref[...]), combined, TN)


def local_grads(back_qk, back_value, slots, inputs, full):
    length, depth = inputs.shape
    both = full.shape[1]
    total = back_qk.shape[0]
    return pl.pallas_call(
        grads_kernel,
        grid=(8,),
        out_shape=(
            jax.ShapeDtypeStruct((length, depth), f32),
            jax.ShapeDtypeStruct((depth, both), f32),
        ),
        in_specs=[
            pl.BlockSpec((total, HD), lambda i: (0, 0)),
            pl.BlockSpec((total, HD), lambda i: (0, 0)),
            pl.BlockSpec(slots.shape, lambda i: (0, 0)),
            pl.BlockSpec((length, depth // 8), lambda i: (0, i)),
            pl.BlockSpec((depth // 8, both), lambda i: (i, 0)),
        ],
        out_specs=(
            pl.BlockSpec((length, depth // 8), lambda i: (0, i)),
            pl.BlockSpec((depth // 8, both), lambda i: (i, 0)),
        ),
        scratch_shapes=[pltpu.VMEM((length, both), bf16)] * 2,
        compiler_params=pltpu.CompilerParams(vmem_limit_bytes=BIG),
        name="unpack_and_grads",
    )(back_qk, back_value, slots, inputs, full)


FINISH_COPIES = 2 + 14 + 14 + 4 + 6


def finish_kernel(
    back_qk_ref, back_value_ref, slots_ref, tokens_ref, full_ref,
    tokens_out, qk_out, value_out,
    tokens, full, high, low, terms, away, own, cross_in,
    column_in, passing, ring_a, ring_b, line_in, plane_in,
    load_sem, send_sem, recv_sem, cross_send, cross_recv,
    line_send, line_recv,
):
    rep, y, z = position()
    x = lax.axis_index("tp")
    length = tokens.shape[0]
    both = full.shape[1]
    width = both // 2
    total = back_qk_ref.shape[0]
    per_line = NZ * ROWS

    def along_y(step):
        return {"ctx": lax.rem(y + step, NY) * NZ + z}

    def along_z(step):
        return {"ctx": y * NZ + lax.rem(z + step, NZ)}

    def along_x(step):
        return {"tp": lax.rem(x + step, 4)}

    loads = [
        pltpu.make_async_copy(tokens_ref, tokens, load_sem.at[0]),
        pltpu.make_async_copy(full_ref, full, load_sem.at[1]),
    ]
    for load in loads:
        load.start()
    right, left, other = along_z(1), along_z(NZ - 1), {"rep": 1 - rep}
    barrier = pltpu.get_barrier_semaphore()
    partners = [along_y(1), along_y(2), along_y(3), right, left, other]
    partners += [along_x(1), along_x(3)]
    for partner in partners:
        pl.semaphore_signal(barrier, inc=1, device_id=partner, device_id_type=MESH)

    def unpack(part, back_ref):
        source = jnp.concatenate(halves(back_ref[...]), axis=1)
        for head in range(width // HD):
            place = lax.broadcasted_iota(jnp.int32, (length, total), 1)
            moved = dot(one(place == slots_ref[:, head : head + 1]), source)
            there = pl.ds(part * width + head * HD, HD)
            high[:, there], low[:, there] = halves(moved[:, :HD] + moved[:, HD:])

    def line_sum(half, there, part):
        start = pl.multiple_of(half * (NY * per_line) + there * per_line, per_line)
        some = halves(tokens[:, pl.ds(start, per_line)])
        here = pl.ds(part * width, width)
        return dot3(some, (high[:, here], low[:, here]), TN).reshape(NZ, ROWS, width)

    def cross(step, part):
        there = lax.rem(y + step, NY)
        return pltpu.make_async_remote_copy(
            src_ref=away.at[part, there],
            dst_ref=cross_in.at[part, there],
            send_sem=cross_send.at[part, step],
            recv_sem=cross_recv.at[part, step],
            device_id=other,
            device_id_type=MESH,
        )

    def away_lines(part):
        @pl.loop(0, NY)
        def _(step):
            there = lax.rem(y + step, NY)
            away[part, there] = line_sum(1 - rep, there, part)
            cross(step, part).start()

    def own_lines(part):
        @pl.loop(0, NY)
        def _(step):
            there = lax.rem(y + step, NY)
            mine = line_sum(rep, there, part)
            cross(step, part).wait_recv()
            own[part, there] = mine + cross_in[part, there]

    def depth(turn):
        return lax.rem(z + turn, NZ)

    def piece(step, turn, part):
        return pltpu.make_async_remote_copy(
            src_ref=own.at[part, lax.rem(y + step, NY), depth(turn), pl.ds(HALF, HALF), :],
            dst_ref=line_in.at[part, step - 1, depth(turn)],
            send_sem=line_send.at[part, step - 1, turn],
            recv_sem=line_recv.at[part, step - 1, turn],
            device_id=along_y(step),
            device_id_type=MESH,
        )

    def send_pieces(part):
        for turn in (4, 5, 3, 6, 2, 7, 1, 0):
            for step in (1, 3, 2):
                piece(step, turn, part).start()

    copies = Copies(send_sem, recv_sem)

    def plane(turn, part):
        return own.at[part, :, depth(turn), pl.ds(0, HALF), :]

    flow_a, flow_b = [None, None], [None, None]

    def turn_a(turn, part):
        ring = ring_a.at[part]
        if turn == 0:
            flow_a[part] = (
                copies.start(plane(4, part), ring.at[0], right),
                copies.start(plane(5, part), ring.at[4], left),
            )
            return
        rightward, leftward = flow_a[part]
        rightward.wait_recv()
        ring_a[part, turn - 1] += plane(4 - turn, part)[...]
        rightward = copies.start(ring.at[turn - 1], ring.at[turn], right)
        if turn < 3:
            leftward.wait_recv()
            ring_a[part, 3 + turn] += plane(5 + turn, part)[...]
            leftward = copies.start(ring.at[3 + turn], ring.at[4 + turn], left)
        flow_a[part] = rightward, leftward

    def along_lines(turn, part):
        for step in (1, 2, 3):
            piece(step, turn, part).wait_recv()
        here = depth(turn)
        return own[part, y, here, pl.ds(HALF, HALF), :] + (
            line_in[part, 0, here] + line_in[part, 1, here] + line_in[part, 2, here]
        )

    def turn_b(turn, part):
        ring = ring_b.at[part]
        if turn == 0:
            first = own.at[part, y, depth(4), pl.ds(HALF, HALF), :]
            second = own.at[part, y, depth(5), pl.ds(HALF, HALF), :]
            first[...] = along_lines(4, part)
            rightward = copies.start(first, ring.at[0], right)
            second[...] = along_lines(5, part)
            flow_b[part] = rightward, copies.start(second, ring.at[4], left)
            return
        rightward, leftward = flow_b[part]
        mine = along_lines(4 - turn, part)
        rightward.wait_recv()
        ring_b[part, turn - 1] += mine
        rightward = copies.start(ring.at[turn - 1], ring.at[turn], right)
        if turn < 3:
            mine = along_lines(5 + turn, part)
            leftward.wait_recv()
            ring_b[part, 3 + turn] += mine
            leftward = copies.start(ring.at[3 + turn], ring.at[4 + turn], left)
        flow_b[part] = rightward, leftward

    planes = [[], []]

    def end_a(part):
        for copy in flow_a[part]:
            copy.wait_recv()
        own[part, :, z, pl.ds(0, HALF), :] = plane(0, part)[...] + (
            ring_a[part, 3] + ring_a[part, 6]
        )
        for step in (1, 3, 2):
            planes[part].append(copies.start(
                own.at[part, lax.rem(y + step, NY), z, pl.ds(0, HALF), :],
                plane_in.at[part, step - 1],
                along_y(step),
            ))

    def end_b(part, out):
        mine = along_lines(0, part)
        for copy in flow_b[part]:
            copy.wait_recv()
        out[pl.ds(HALF, HALF), :] = mine + ring_b[part, 3] + ring_b[part, 6]

    middle = length // 2
    upper_rows, lower_rows = pl.ds(0, middle), pl.ds(middle, middle)

    def columns(step):
        start = pl.multiple_of(lax.rem(x + step, 4) * width, width)
        return dot3((high[...], low[...]), halves(full[pl.ds(start, width), :]), NT)

    unpack(1, back_value_ref)
    loads[0].wait()
    pl.semaphore_wait(barrier, len(partners))
    away_lines(1)
    own_lines(1)
    turn_a(0, 1)
    send_pieces(1)
    unpack(0, back_qk_ref)
    turn_a(1, 1)
    away_lines(0)
    turn_b(0, 1)
    turn_a(2, 1)
    own_lines(0)
    turn_a(0, 0)
    send_pieces(0)
    turn_b(1, 1)
    loads[1].wait()
    terms[1] = columns(2)
    by_right = copies.start(terms.at[1, upper_rows], passing.at[0], along_x(1))
    by_left = copies.start(terms.at[1, lower_rows], passing.at[1], along_x(3))
    turn_a(3, 1)
    turn_b(2, 1)
    terms[0] = columns(1)
    sideways = [copies.start(terms.at[0, lower_rows], column_in.at[0, lower_rows], along_x(1))]
    turn_a(1, 0)
    turn_b(3, 1)
    terms[2] = columns(3)
    sideways.append(
        copies.start(terms.at[2, upper_rows], column_in.at[1, upper_rows], along_x(3))
    )
    turn_b(0, 0)
    end_a(1)
    turn_a(2, 0)
    by_right.wait_recv()
    terms[0, upper_rows, :] += passing[0]
    sideways.append(
        copies.start(terms.at[0, upper_rows], column_in.at[0, upper_rows], along_x(1))
    )
    by_left.wait_recv()
    terms[2, lower_rows, :] += passing[1]
    sideways.append(
        copies.start(terms.at[2, lower_rows], column_in.at[1, lower_rows], along_x(3))
    )
    turn_b(1, 0)
    turn_a(3, 0)
    end_b(1, value_out)
    turn_b(2, 0)
    tokens_out[...] = columns(0)
    turn_b(3, 0)
    end_a(0)
    end_b(0, qk_out)
    for copy in sideways:
        copy.wait_recv()

    @pl.loop(0, length // 8)
    def _(block):
        here = pl.ds(pl.multiple_of(block * 8, 8), 8)
        tokens_out[here, :] += column_in[0, here, :] + column_in[1, here, :]

    for part, out in ((1, value_out), (0, qk_out)):
        for copy in planes[part]:
            copy.wait_recv()
        out[pl.ds(0, HALF), :] = own[part, y, z, pl.ds(0, HALF), :] + (
            plane_in[part, 0] + plane_in[part, 1] + plane_in[part, 2]
        )

    @pl.loop(0, NY)
    def _(step):
        for part in range(2):
            cross(step, part).wait_send()

    @pl.loop(1, NY)
    def _(step):
        for part in range(2):
            for turn in range(NZ):
                piece(step, turn, part).wait_send()

    copies.finish()
    assert len(copies.all) == FINISH_COPIES


def finish(back_qk, back_value, slots, inputs, full):
    length, depth = inputs.shape
    both = full.shape[1]
    width = both // 2
    vmem, anywhere = pl.BlockSpec(memory_space=pltpu.VMEM), pl.BlockSpec(memory_space=pl.ANY)
    return pl.pallas_call(
        finish_kernel,
        out_shape=(
            jax.ShapeDtypeStruct((length, width), f32),
            jax.ShapeDtypeStruct((ROWS, width), f32),
            jax.ShapeDtypeStruct((ROWS, width), f32),
        ),
        in_specs=[vmem, vmem, vmem, anywhere, anywhere],
        out_specs=(vmem,) * 3,
        scratch_shapes=[
            pltpu.VMEM((length, depth), f32),
            pltpu.VMEM((depth, both), f32),
            pltpu.VMEM((length, both), bf16),
            pltpu.VMEM((length, both), bf16),
            pltpu.VMEM((3, length, width), f32),
            pltpu.VMEM((2, NY, NZ, ROWS, width), f32),
            pltpu.VMEM((2, NY, NZ, ROWS, width), f32),
            pltpu.VMEM((2, NY, NZ, ROWS, width), f32),
            pltpu.VMEM((2, length, width), f32),
            pltpu.VMEM((2, length // 2, width), f32),
            pltpu.VMEM((2, 7, NY, HALF, width), f32),
            pltpu.VMEM((2, 7, HALF, width), f32),
            pltpu.VMEM((2, 3, NZ, HALF, width), f32),
            pltpu.VMEM((2, 3, HALF, width), f32),
            pltpu.SemaphoreType.DMA((2,)),
            pltpu.SemaphoreType.DMA((FINISH_COPIES,)),
            pltpu.SemaphoreType.DMA((FINISH_COPIES,)),
            pltpu.SemaphoreType.DMA((2, NY)),
            pltpu.SemaphoreType.DMA((2, NY)),
            pltpu.SemaphoreType.DMA((2, 3, NZ)),
            pltpu.SemaphoreType.DMA((2, 3, NZ)),
        ],
        compiler_params=pltpu.CompilerParams(
            collective_id=3, has_side_effects=True, vmem_limit_bytes=52 * 2**20
        ),
        name="grads_and_scatter",
    )(back_qk, back_value, slots, inputs, full)


def exchange(array):
    return lax.all_to_all(array, "ctx", split_axis=0, concat_axis=0, tiled=True)


def seat_numbers(marks, room):
    marks = marks.astype(jnp.int32) - 1
    source = lax.broadcasted_iota(jnp.int32, marks.shape, 0) % GROUP
    seats = (marks // 3) * (3 * GROUP) + source * 3 + marks % 3
    return jnp.where(marks < 0, -1, seats).reshape(OWNERS // GROUP, 1, GROUP * room)


def snug_part(inputs, full, pay, early, slots, tall_slots):
    marks = early[:, ROOM : ROOM + 2, :ROOM]
    held, place = marks[:, 0], marks[:, 1]
    seats = jnp.where(held > 0.5, (held - 1) * (3 * GROUP) + place, -1.0).astype(jnp.int32)
    seats = seats.reshape(OWNERS // GROUP, 1, GROUP * ROOM)
    back = cluster_part(pay, slots, seats, early)
    back_qk, back_value = (rows.reshape(OWNERS * ROOM, HD) for rows in back)
    return finish(back_qk, back_value, tall_slots, inputs, full)


def roomy_part(inputs, full, upstream, cluster):
    heads, length = cluster.shape
    order = jnp.arange(length, dtype=jnp.int32)
    earlier = order[:, None] < order[None, :]
    alike = cluster[:, :, None] == cluster[:, None, :]
    within = jnp.sum((alike & earlier).astype(jnp.int32), axis=1)
    head = jnp.arange(heads, dtype=jnp.int32)[:, None]
    ids = (head * CL_DEV + cluster % CL_DEV) * 3 + within
    slots = cluster // CL_DEV * SLOTS + ids
    marks = jnp.zeros((OWNERS * SLOTS,), f32).at[slots.reshape(-1)].set(
        (ids + 1).astype(f32).reshape(-1)
    )
    rows = upstream.reshape(length, heads, HD).transpose(1, 0, 2).reshape(-1, HD)
    early = jnp.zeros((OWNERS * SLOTS, HD), f32).at[slots.reshape(-1)].set(rows)
    early = exchange(early.reshape(OWNERS, SLOTS, HD))
    marks = exchange(marks.reshape(OWNERS, SLOTS))
    rows = pack_rows(inputs, full, slots.reshape(1, -1), SLOTS)
    rows = exchange(rows.reshape(OWNERS, SLOTS, 2 * HD)).reshape(OWNERS * SLOTS, 2 * HD)
    replies = attend(rows, early, seat_numbers(marks, SLOTS), SLOTS)
    returned = exchange(replies.reshape(OWNERS, SLOTS, 2 * HD)).reshape(OWNERS * SLOTS, 2 * HD)
    return scatter_sums(
        *local_grads(returned[:, :HD], returned[:, HD:], slots.T, inputs, full)
    )


def per_device(tokens, qk_weight, value_weight, grad_out, assign):
    inputs = tokens[0]
    heads_here = qk_weight.shape[1] // HD
    width = heads_here * HD
    cluster = assign[:, 0, :, 0]
    full, early, slots, tall_slots, pay = gather_and_project(
        qk_weight, value_weight, jnp.pad(cluster, ((0, 8 - heads_here), (0, 0))), grad_out[0],
        inputs,
    )
    full = full.reshape(-1, 2 * width)
    fullest = jnp.max(early[:, ROOM, PITCH])

    def snug(inputs, full, upstream, cluster, *routed):
        return snug_part(inputs, full, *routed)

    def roomy(inputs, full, upstream, cluster, *routed):
        return roomy_part(inputs, full, upstream, cluster)

    grad_tokens, grad_qk_weight, grad_value_weight = lax.cond(
        fullest <= ROOM, snug, roomy,
        inputs, full, grad_out[0], cluster, pay, early, slots, tall_slots,
    )
    return (grad_tokens[None], grad_qk_weight, grad_value_weight)


def solution(mesh):
    in_specs = (
        P("rep", "ctx", None),
        P(("rep", "ctx"), "tp"),
        P(("rep", "ctx"), "tp"),
        P("rep", "ctx", "tp"),
        P("tp", "rep", "ctx", None),
    )
    out_specs = (P("rep", "ctx", "tp"), P(("rep", "ctx"), "tp"), P(("rep", "ctx"), "tp"))
    return jax.shard_map(
        per_device, mesh=mesh, in_specs=in_specs, out_specs=out_specs, check_vma=False
    )
```

```python
import jax
import jax.numpy as jnp
from jax import lax
from jax.experimental import pallas as pl
from jax.experimental.pallas import tpu as pltpu
from jax.sharding import PartitionSpec as P

HD = 128
CL_DEV = 8
NY = 4
NZ = 8
ROWS = 32
HALF = 16
MESH = pl.DeviceIdType.MESH

masked_score = -1e30
ROOM = 56
LANES = 128
GROUP = 8
SLOTS = 96
TALL = 768
f32, bf16 = jnp.float32, jnp.bfloat16
NN = (((1,), (0,)), ((), ()))
NT = (((1,), (1,)), ((), ()))
TN = (((0,), (0,)), ((), ()))
BIG = 48 * 2**20


def dot(left, right, dims=NN):
    return lax.dot_general(left, right, dims, preferred_element_type=f32)


def halves(matrix):
    upper = matrix.astype(bf16)
    return upper, (matrix - upper.astype(f32)).astype(bf16)


def dot3(left, right, dims=NN):
    a, b = left
    c, d = right
    first = jnp.concatenate([a, b, a], axis=dims[0][0][0])
    second = jnp.concatenate([c, c, d], axis=dims[0][1][0])
    return dot(first, second, dims)


def position():
    ctx = lax.axis_index("ctx")
    return lax.axis_index("rep"), lax.div(ctx, NZ), lax.rem(ctx, NZ)


def greet(partners):
    barrier = pltpu.get_barrier_semaphore()
    for partner in partners:
        pl.semaphore_signal(barrier, inc=1, device_id=partner, device_id_type=MESH)
    pl.semaphore_wait(barrier, len(partners))


class Copies:
    def __init__(self, send_sem, recv_sem):
        self.send_sem, self.recv_sem = send_sem, recv_sem
        self.all = []

    def start(self, source, target, device):
        index = len(self.all)
        copy = pltpu.make_async_remote_copy(
            src_ref=source,
            dst_ref=target,
            send_sem=self.send_sem.at[index],
            recv_sem=self.recv_sem.at[index],
            device_id=device,
            device_id_type=MESH,
        )
        copy.start()
        self.all.append(copy)
        return copy

    def finish(self):
        for copy in self.all:
            copy.wait_send()


GATHER_COPIES = 6 + 7 + 14 + 21 + 16 + 4
ROUTE_COPIES = 3 + 7 + 3 + 1
CLUSTERS = 256
OWNERS = 32
PITCH = 64


def count_rows(cluster_ref, heads):
    length = cluster_ref.shape[1]
    line = lax.broadcasted_iota(jnp.int32, (8, length), 0)
    counts = jnp.zeros((8, CLUSTERS), f32)
    for head in range(heads):
        counts += dot(one(line == head), members(cluster_ref, head), NT)
    return counts


def one(condition):
    return jnp.where(condition, 1.0, 0.0).astype(bf16)


def members(cluster_ref, head):
    length = cluster_ref.shape[1]
    label = lax.broadcasted_iota(jnp.int32, (CLUSTERS, length), 0)
    return one(label == cluster_ref[head : head + 1, :])


def deal_order(counts):
    lane = lax.broadcasted_iota(jnp.int32, counts.shape, 1)
    return counts * CLUSTERS + (CLUSTERS - 1 - lane).astype(f32)


def route_head(cluster_ref, head, keys, tall_keys, earlier, base):
    larger = jnp.where(tall_keys[:, head : head + 1] > keys[head : head + 1, :], 1.0, 0.0)
    place = jnp.sum(larger, axis=0, keepdims=True).astype(jnp.int32)
    turn = place // OWNERS
    seat = place % OWNERS
    seat = jnp.where(turn % 2 == 0, seat, OWNERS - 1 - seat)
    seat = (seat + 8 * head) % OWNERS
    line = lax.broadcasted_iota(jnp.int32, (8, CLUSTERS), 0)
    table = jnp.where(line == 0, seat, jnp.where(line == 1, turn, 0)).astype(f32).astype(bf16)
    chosen = members(cluster_ref, head)
    looked = dot(table, chosen).astype(jnp.int32)
    owner, turn = looked[0:1, :], looked[1:2, :]
    within = jnp.sum(chosen.astype(f32) * dot(chosen, earlier), axis=0, keepdims=True)
    label = lax.broadcasted_iota(jnp.int32, (OWNERS, owner.shape[1]), 0)
    owned = one(label == owner)
    many = owned.astype(f32)
    rank = jnp.sum(many * (dot(owned, earlier) + base), axis=0, keepdims=True)
    base = base + jnp.sum(many, axis=1, keepdims=True)
    return owner, rank.astype(jnp.int32), head * CL_DEV + turn, within, base


def gather_kernel(
    qk_ref, value_ref, cluster_ref, grad_ref, tokens_ref,
    full_ref, early_ref, slots_ref, tall_slots_ref, pay_ref,
    out_ref, tokens, acc, counts_y, counts_z, most, ids_row, slots_row, pay, early_out,
    local_sem, send_sem, recv_sem, route_send, route_recv, early_send, early_recv,
):
    rep, y, z = position()
    me = lax.axis_index("ctx")
    x = lax.axis_index("tp")
    width = qk_ref.shape[1]
    heads = width // HD
    length = cluster_ref.shape[1]

    def along_y(step):
        return {"ctx": lax.rem(y + step, NY) * NZ + z}

    def along_z(step):
        return {"ctx": y * NZ + lax.rem(z + step, NZ)}

    def along_x(step):
        return {"tp": lax.rem(x + step, 4)}

    def around(step):
        return {"ctx": lax.rem(me + step, OWNERS)}

    def plane(step, part):
        there = pl.ds(part * width, width)
        return out_ref.at[rep, :, lax.rem(z + step, NZ), pl.ds(0, HALF), there]

    def piece(step):
        return out_ref.at[rep, y, lax.rem(z + step, NZ), pl.ds(HALF, HALF), :]

    def line(step):
        return out_ref.at[rep, lax.rem(y + step, NY), :, pl.ds(HALF, HALF), :]

    right, left, other = along_z(1), along_z(NZ - 1), {"rep": 1 - rep}
    mine = out_ref.at[rep, y, z]
    fetch = pltpu.make_async_copy(tokens_ref, tokens, local_sem.at[2])
    fetch.start()
    first = pltpu.make_async_copy(qk_ref, mine.at[:, pl.ds(0, width)], local_sem.at[0])
    second = pltpu.make_async_copy(value_ref, mine.at[:, pl.ds(width, width)], local_sem.at[1])
    first.start()
    second.start()
    barrier = pltpu.get_barrier_semaphore()

    @pl.loop(1, OWNERS)
    def _(step):
        pl.semaphore_signal(barrier, inc=1, device_id=around(step), device_id_type=MESH)

    for partner in (other, along_x(1), along_x(2), along_x(3)):
        pl.semaphore_signal(barrier, inc=1, device_id=partner, device_id_type=MESH)
    counts_y[0] = count_rows(cluster_ref, heads)
    pl.semaphore_wait(barrier, OWNERS - 1 + 4)

    routes = Copies(route_send, route_recv)
    counted = [
        routes.start(counts_y.at[0], counts_y.at[step], along_y(step)) for step in (1, 2, 3)
    ]
    first.wait()
    second.wait()
    copies = Copies(send_sem, recv_sem)
    top, bottom = mine.at[pl.ds(0, HALF), :], mine.at[pl.ds(HALF, HALF), :]
    shared = [copies.start(top, top, along_y(step)) for step in (1, 3, 2)]
    pieces = [(copies.start(piece(0), piece(0), right), copies.start(piece(0), piece(0), left))]

    below = [copies.start(bottom, bottom, along_y(step)) for step in (1, 3, 2)]

    for head in range(heads):
        upper, lower = halves(grad_ref[:, head * HD : (head + 1) * HD])
        pay[pl.ds(head * length, length), :HD] = upper
        pay[pl.ds(head * length, length), HD:] = lower

    for copy in counted:
        copy.wait_recv()
    counts_z[0] = counts_y[0] + counts_y[1] + counts_y[2] + counts_y[3]
    counted = [
        routes.start(counts_z.at[0], counts_z.at[step], along_z(step)) for step in range(1, NZ)
    ]
    for copy in shared:
        copy.wait_recv()
    planes = []
    for part in range(2):
        here = plane(0, part)
        planes.append([(copies.start(here, here, right), copies.start(here, here, left))])
    across = [copies.start(plane(0, part), plane(0, part), other) for part in range(2)]
    passed = {1: [], 2: [], 3: []}

    def pass_on(here):
        for step in (1, 3, 2):
            passed[step].append(copies.start(here, here, along_y(step)))

    def turn_pieces(step):
        rightward, leftward = pieces[step]
        after, before = piece(NZ - 1 - step), piece(1 + step)
        rightward.wait_recv()
        if leftward is not None:
            leftward.wait_recv()
        if step < 3:
            pieces.append((
                copies.start(after, after, right),
                copies.start(before, before, left) if step < 2 else None,
            ))
        pass_on(after)
        if leftward is not None:
            pass_on(before)

    def turn_planes(step):
        for part in range(2):
            turn_plane(step, part)

    def turn_plane(step, part):
        rightward, leftward = planes[part][step]
        after, before = plane(NZ - 1 - step, part), plane(1 + step, part)
        rightward.wait_recv()
        if step < 3:
            going = copies.start(after, after, right)
        if leftward is not None:
            leftward.wait_recv()
            coming = copies.start(before, before, left) if step < 2 else None
        if step < 3:
            planes[part].append((going, coming if step < 2 else None))
        across.append(copies.start(after, after, other))
        if leftward is not None:
            across.append(copies.start(before, before, other))

    turn_pieces(0)
    for copy in counted:
        copy.wait_recv()
    total = counts_z[0]
    for step in range(1, NZ):
        total += counts_z[step]
    keys = deal_order(total)
    tall_keys = jnp.concatenate([keys] + [jnp.zeros_like(keys)] * 15, axis=0).T
    earlier = one(
        lax.broadcasted_iota(jnp.int32, (length, length), 0)
        < lax.broadcasted_iota(jnp.int32, (length, length), 1)
    )
    base = jnp.zeros((OWNERS, 1), f32)
    highest = jnp.zeros((1, 1), f32)
    row = lax.broadcasted_iota(jnp.int32, (8, length), 0)
    slots_list = []
    for head in range(heads):
        owner, rank, held, within, base = route_head(
            cluster_ref, head, keys, tall_keys, earlier, base
        )
        highest = jnp.maximum(highest, jnp.max(rank.astype(f32), axis=1, keepdims=True) + 1)
        here = pl.ds(head * length, length)
        slots_ref[:, here] = jnp.where(rank < ROOM, owner * ROOM + rank, -1)
        slots_row[:, here] = jnp.where(rank < ROOM, owner * PITCH + rank, -1)
        within = within + (3 * lax.rem(me, GROUP)).astype(f32)
        marked = jnp.where(row == 0, (held + 1).astype(f32), jnp.where(row == 1, within, 0.0))
        ids_row[:, here] = marked.astype(bf16)
        slots_list.append(jnp.where(rank < ROOM, owner * ROOM + rank, -1))
    most[0] = jnp.broadcast_to(highest, (8, LANES))
    tall = jnp.concatenate(
        slots_list + [jnp.zeros((LANES - heads, length), jnp.int32)], axis=0
    )
    tall_slots_ref[...] = tall.astype(f32).T.astype(jnp.int32)
    fullest = [routes.start(most.at[0], most.at[step], along_x(step)) for step in (1, 2, 3)]
    turn_pieces(1)
    turn_planes(0)

    def pack_early(block):
        rows = 4 * PITCH
        place = lax.broadcasted_iota(jnp.int32, (rows, heads * length), 0) + block * rows
        chosen = one(place == slots_row[...])
        both = dot(chosen, pay[...])
        both = both[:, :HD] + both[:, HD:]
        marks = dot(ids_row[...], chosen, NT)
        for lane in range(4):
            early_out[block * 4 + lane] = both[lane * PITCH : (lane + 1) * PITCH]
            early_out[block * 4 + lane, pl.ds(ROOM, 8), pl.ds(0, PITCH)] = marks[
                :, lane * PITCH : (lane + 1) * PITCH
            ]

    @pl.loop(0, OWNERS // 8)
    def _(block):
        pack_early(block)

    for copy in fullest:
        copy.wait_recv()
    most[4] = jnp.maximum(jnp.maximum(most[0], most[1]), jnp.maximum(most[2], most[3]))
    fullest = routes.start(most.at[4], most.at[5], other)
    turn_pieces(2)

    @pl.loop(OWNERS // 8, OWNERS // 4)
    def _(block):
        pack_early(block)

    turn_pieces(3)
    turn_planes(1)
    across.append(copies.start(line(0), line(0), other))
    fullest.wait_recv()
    overall = jnp.maximum(most[4], most[5])[:, :PITCH]

    @pl.loop(0, OWNERS)
    def _(block):
        early_out[block, pl.ds(ROOM, 8), pl.ds(PITCH, PITCH)] = overall

    def early(step):
        there = lax.rem(me + step, OWNERS)
        return pltpu.make_async_remote_copy(
            src_ref=early_out.at[there],
            dst_ref=early_ref.at[me],
            send_sem=early_send.at[step],
            recv_sem=early_recv.at[step],
            device_id={"ctx": there},
            device_id_type=MESH,
        )

    @pl.loop(1, OWNERS // 4)
    def _(step):
        early(step).start()

    stay = pltpu.make_async_copy(early_out.at[me], early_ref.at[me], local_sem.at[0])
    stay.start()
    turn_planes(2)
    turn_planes(3)

    @pl.loop(OWNERS // 4, OWNERS)
    def _(step):
        early(step).start()

    for copy in below:
        copy.wait_recv()
    for step in (1, 3, 2):
        for copy in passed[step]:
            copy.wait_recv()
        across.append(copies.start(line(NY - step), line(NY - step), other))
    fetch.wait()

    def project(half, there):
        start = pl.multiple_of((half * NY + there) * (NZ * ROWS), NZ * ROWS)
        some = halves(tokens[:, pl.ds(start, NZ * ROWS)])
        return dot3(some, halves(out_ref[half, there].reshape(NZ * ROWS, 2 * width)))

    acc[...] = project(rep, 0)

    @pl.loop(1, NY)
    def _(there):
        acc[...] += project(rep, there)

    for copy in across:
        copy.wait_recv()
    save = pltpu.make_async_copy(out_ref, full_ref, local_sem.at[1])
    save.start()

    @pl.loop(0, NY)
    def _(there):
        acc[...] += project(1 - rep, there)

    for part in range(2):
        for head in range(heads):
            here = pl.ds(head * length, length)
            column = part * width + head * HD
            upper, lower = halves(acc[:, column : column + HD])
            pay_ref[part, here, :HD] = upper
            pay_ref[part, here, HD:] = lower
    copies.finish()
    routes.finish()
    stay.wait()
    save.wait()

    @pl.loop(1, OWNERS)
    def _(step):
        early(step).wait()

    assert len(copies.all) == GATHER_COPIES and len(routes.all) == ROUTE_COPIES


def gather_and_project(qk_weight, value_weight, clusters, upstream, inputs):
    width = qk_weight.shape[1]
    length = clusters.shape[1]
    rows = width // HD * length
    vmem, anywhere = pl.BlockSpec(memory_space=pltpu.VMEM), pl.BlockSpec(memory_space=pl.ANY)
    return pl.pallas_call(
        gather_kernel,
        out_shape=(
            jax.ShapeDtypeStruct((2, NY, NZ, ROWS, 2 * width), f32),
            jax.ShapeDtypeStruct((OWNERS, PITCH, HD), f32),
            jax.ShapeDtypeStruct((1, rows), jnp.int32),
            jax.ShapeDtypeStruct((length, LANES), jnp.int32),
            jax.ShapeDtypeStruct((2, rows, 2 * HD), bf16),
        ),
        in_specs=[anywhere, anywhere, vmem, vmem, anywhere],
        out_specs=(anywhere, anywhere, vmem, vmem, vmem),
        scratch_shapes=[
            pltpu.VMEM((2, NY, NZ, ROWS, 2 * width), f32),
            pltpu.VMEM(inputs.shape, f32),
            pltpu.VMEM((length, 2 * width), f32),
            pltpu.VMEM((NY, 8, CLUSTERS), f32),
            pltpu.VMEM((NZ, 8, CLUSTERS), f32),
            pltpu.VMEM((6, 8, LANES), f32),
            pltpu.VMEM((8, rows), bf16),
            pltpu.VMEM((1, rows), jnp.int32),
            pltpu.VMEM((rows, 2 * HD), bf16),
            pltpu.VMEM((OWNERS, PITCH, HD), f32),
            pltpu.SemaphoreType.DMA((3,)),
            pltpu.SemaphoreType.DMA((GATHER_COPIES,)),
            pltpu.SemaphoreType.DMA((GATHER_COPIES,)),
            pltpu.SemaphoreType.DMA((ROUTE_COPIES,)),
            pltpu.SemaphoreType.DMA((ROUTE_COPIES,)),
            pltpu.SemaphoreType.DMA((OWNERS,)),
            pltpu.SemaphoreType.DMA((OWNERS,)),
        ],
        compiler_params=pltpu.CompilerParams(
            collective_id=0, has_side_effects=True, vmem_limit_bytes=BIG
        ),
        name="gather_and_project",
    )(qk_weight, value_weight, clusters, upstream, inputs)


SCATTER_COPIES = 3 + 12 + 7 + 3 + 7 + 3


def scatter_kernel(
    terms_ref, sums_ref, tokens_out, qk_out, value_out,
    column_in, cross_in, ring_a, ring_b, line_in, plane_in,
    local_sem, send_sem, recv_sem,
):
    rep, y, z = position()
    x = lax.axis_index("tp")
    width = qk_out.shape[1]

    def along_y(step):
        return {"ctx": lax.rem(y + step, NY) * NZ + z}

    def along_z(step):
        return {"ctx": y * NZ + lax.rem(z + step, NZ)}

    def along_x(step):
        return {"tp": lax.rem(x + step, 4)}

    def columns(step):
        start = pl.multiple_of(lax.rem(x + step, 4) * width, width)
        return terms_ref.at[:, pl.ds(start, width)]

    def plane(step):
        return cross_in.at[:, lax.rem(z + step, NZ), pl.ds(0, HALF), :]

    def line(step):
        return cross_in.at[lax.rem(y + step, NY), :, pl.ds(HALF, HALF), :]

    def piece(step):
        return cross_in.at[y, lax.rem(z + step, NZ), pl.ds(HALF, HALF), :]

    right, left, other = along_z(1), along_z(NZ - 1), {"rep": 1 - rep}
    greet(
        [along_y(1), along_y(2), along_y(3), right, left, other]
        + [along_x(1), along_x(2), along_x(3)]
    )
    copies = Copies(send_sem, recv_sem)
    sideways = [
        copies.start(columns(step), column_in.at[step - 1], along_x(step)) for step in (1, 3, 2)
    ]
    own_columns = pltpu.make_async_copy(columns(0), tokens_out, local_sem)
    own_columns.start()

    cross = {}
    for kind, step in (
        ("a", 4), ("a", 5), ("b", 1), ("b", 3), ("b", 2), ("a", 3),
        ("a", 6), ("a", 2), ("a", 7), ("b", 0), ("a", 1), ("a", 0),
    ):
        if kind == "a":
            there = lax.rem(z + step, NZ)
            source = sums_ref.at[1 - rep, :, there, pl.ds(0, HALF), :]
            cross[kind, step] = copies.start(source, plane(step), other)
        else:
            there = lax.rem(y + step, NY)
            source = sums_ref.at[1 - rep, there, :, pl.ds(HALF, HALF), :]
            cross[kind, step] = copies.start(source, line(step), other)

    def add_plane(step):
        cross["a", step].wait_recv()
        there = lax.rem(z + step, NZ)
        cross_in[:, there, pl.ds(0, HALF), :] += sums_ref[rep, :, there, pl.ds(0, HALF), :]

    def add_line(step):
        cross["b", step].wait_recv()
        there = lax.rem(y + step, NY)
        cross_in[there, :, pl.ds(HALF, HALF), :] += sums_ref[
            rep, there, :, pl.ds(HALF, HALF), :
        ]

    add_plane(4)
    right_a = copies.start(plane(4), ring_a.at[0], right)
    add_plane(5)
    left_a = copies.start(plane(5), ring_a.at[4], left)
    lines = []
    for step in (1, 3, 2):
        add_line(step)
        lines.append(copies.start(line(step), line_in.at[step - 1], along_y(step)))

    def pass_a(turn):
        nonlocal right_a, left_a
        add_plane(4 - turn)
        right_a.wait_recv()
        ring_a[turn - 1] += cross_in[:, lax.rem(z + 4 - turn, NZ), pl.ds(0, HALF), :]
        right_a = copies.start(ring_a.at[turn - 1], ring_a.at[turn], right)
        if turn < 3:
            add_plane(5 + turn)
            left_a.wait_recv()
            ring_a[3 + turn] += cross_in[:, lax.rem(z + 5 + turn, NZ), pl.ds(0, HALF), :]
            left_a = copies.start(ring_a.at[3 + turn], ring_a.at[4 + turn], left)

    pass_a(1)
    add_line(0)
    pass_a(2)
    for copy in lines:
        copy.wait_recv()
    cross_in[y, :, pl.ds(HALF, HALF), :] += line_in[0] + line_in[1] + line_in[2]
    right_b = copies.start(piece(4), ring_b.at[0], right)
    left_b = copies.start(piece(5), ring_b.at[4], left)
    pass_a(3)

    def pass_b(turn):
        nonlocal right_b, left_b
        right_b.wait_recv()
        ring_b[turn - 1] += cross_in[y, lax.rem(z + 4 - turn, NZ), pl.ds(HALF, HALF), :]
        right_b = copies.start(ring_b.at[turn - 1], ring_b.at[turn], right)
        if turn < 3:
            left_b.wait_recv()
            ring_b[3 + turn] += cross_in[y, lax.rem(z + 5 + turn, NZ), pl.ds(HALF, HALF), :]
            left_b = copies.start(ring_b.at[3 + turn], ring_b.at[4 + turn], left)

    pass_b(1)
    pass_b(2)
    add_plane(0)
    right_a.wait_recv()
    left_a.wait_recv()
    cross_in[:, z, pl.ds(0, HALF), :] += ring_a[3] + ring_a[6]
    planes = [
        copies.start(
            cross_in.at[lax.rem(y + step, NY), z, pl.ds(0, HALF), :],
            plane_in.at[step - 1],
            along_y(step),
        )
        for step in (1, 3, 2)
    ]
    pass_b(3)
    right_b.wait_recv()
    left_b.wait_recv()
    lower = cross_in[y, z, pl.ds(HALF, HALF), :] + ring_b[3] + ring_b[6]
    qk_out[pl.ds(HALF, HALF), :] = lower[:, :width]
    value_out[pl.ds(HALF, HALF), :] = lower[:, width:]
    for copy in planes:
        copy.wait_recv()
    upper = cross_in[y, z, pl.ds(0, HALF), :] + plane_in[0] + plane_in[1] + plane_in[2]
    qk_out[pl.ds(0, HALF), :] = upper[:, :width]
    value_out[pl.ds(0, HALF), :] = upper[:, width:]
    own_columns.wait()
    for copy in sideways:
        copy.wait_recv()

    @pl.loop(0, tokens_out.shape[0] // 8)
    def _(block):
        here = pl.ds(pl.multiple_of(block * 8, 8), 8)
        tokens_out[here, :] += column_in[0, here, :] + column_in[1, here, :] + column_in[2, here, :]

    copies.finish()
    assert len(copies.all) == SCATTER_COPIES


def scatter_sums(token_terms, weight_terms):
    length = token_terms.shape[0]
    both = weight_terms.shape[1]
    width = both // 2
    return pl.pallas_call(
        scatter_kernel,
        out_shape=(
            jax.ShapeDtypeStruct((length, width), f32),
            jax.ShapeDtypeStruct((ROWS, width), f32),
            jax.ShapeDtypeStruct((ROWS, width), f32),
        ),
        in_specs=[pl.BlockSpec(memory_space=pl.ANY), pl.BlockSpec(memory_space=pltpu.VMEM)],
        out_specs=(pl.BlockSpec(memory_space=pltpu.VMEM),) * 3,
        scratch_shapes=[
            pltpu.VMEM((3, length, width), f32),
            pltpu.VMEM((NY, NZ, ROWS, both), f32),
            pltpu.VMEM((7, NY, HALF, both), f32),
            pltpu.VMEM((7, HALF, both), f32),
            pltpu.VMEM((3, NZ, HALF, both), f32),
            pltpu.VMEM((3, HALF, both), f32),
            pltpu.SemaphoreType.DMA,
            pltpu.SemaphoreType.DMA((SCATTER_COPIES,)),
            pltpu.SemaphoreType.DMA((SCATTER_COPIES,)),
        ],
        compiler_params=pltpu.CompilerParams(
            collective_id=1, has_side_effects=True, vmem_limit_bytes=48 * 2**20
        ),
        name="scatter_sums",
    )(token_terms, weight_terms.reshape(2, NY, NZ, ROWS, both))


def pack_kernel(tokens_ref, full_ref, slots_ref, rows_ref, acc, pay):
    step = pl.program_id(0)
    length, both = acc.shape
    rows = rows_ref.shape[0]

    @pl.when(step == 0)
    def _():
        acc[...] = jnp.zeros_like(acc)

    @pl.when(step < 8)
    def _():
        acc[...] += dot3(halves(tokens_ref[...]), halves(full_ref[...]))

    @pl.when(step == 7)
    def _():
        for head in range(both // (2 * HD)):
            here = pl.ds(head * length, length)
            for part in range(2):
                column = part * both // 2 + head * HD
                upper, lower = halves(acc[:, column : column + HD])
                pay[here, part * HD : (part + 1) * HD] = upper
                pay[here, (2 + part) * HD : (3 + part) * HD] = lower

    @pl.when(step >= 8)
    def _():
        place = lax.broadcasted_iota(jnp.int32, (rows, slots_ref.shape[1]), 0) + (step - 8) * rows
        moved = dot(one(place == slots_ref[...]), pay[...])
        rows_ref[...] = moved[:, : 2 * HD] + moved[:, 2 * HD :]


def pack_rows(inputs, full, slots, room):
    length, depth = inputs.shape
    both = full.shape[1]
    total = slots.shape[1]
    return pl.pallas_call(
        pack_kernel,
        grid=(16,),
        out_shape=jax.ShapeDtypeStruct((OWNERS * room, 2 * HD), f32),
        in_specs=[
            pl.BlockSpec((length, depth // 8), lambda i: (0, jnp.minimum(i, 7))),
            pl.BlockSpec((depth // 8, both), lambda i: (jnp.minimum(i, 7), 0)),
            pl.BlockSpec((1, total), lambda i: (0, 0)),
        ],
        out_specs=pl.BlockSpec((4 * room, 2 * HD), lambda i: (jnp.maximum(i - 8, 0), 0)),
        scratch_shapes=[pltpu.VMEM((length, both), f32), pltpu.VMEM((total, 4 * HD), bf16)],
        compiler_params=pltpu.CompilerParams(vmem_limit_bytes=BIG),
        name="project_and_pack",
    )(inputs, full, slots)


def attend_kernel(marks_ref, rows_ref, early_ref, replies_ref, spread, seats, valid, answer):
    groups = marks_ref.shape[0]
    wide = marks_ref.shape[2]
    owned = spread.shape[1]
    seat = spread.shape[2]
    size = groups * seat

    @pl.loop(0, groups)
    def _(group):
        here = pl.ds(pl.multiple_of(group * wide, wide), wide)
        place = lax.broadcasted_iota(jnp.int32, (TALL, wide), 0)
        chosen = one(place == marks_ref[group])
        seats[group] = chosen
        upper, lower = halves(rows_ref[here, :])
        early = early_ref[pl.ds(group * GROUP, GROUP), pl.ds(0, wide // GROUP), :]
        early_upper, early_lower = halves(early.reshape(wide, HD))
        present = jnp.ones((wide, LANES), bf16)
        moved = dot(
            chosen, jnp.concatenate([upper, early_upper, lower, early_lower, present], axis=1)
        )
        spread[group] = (moved[:, : 3 * HD] + moved[:, 3 * HD : 6 * HD]).reshape(owned, seat, 3 * HD)
        valid[group] = moved[:, 6 * HD :].reshape(owned, seat, LANES)

    @pl.loop(0, owned // 4)
    def _(block):
        for lane in range(4):
            index = block * 4 + lane
            rows = spread[:, index].reshape(size, 3 * HD)
            present = valid[:, index].reshape(size, LANES)[:, :size] > 0.5
            qk = halves(rows[:, :HD])
            value = halves(rows[:, HD : 2 * HD])
            upstream = halves(rows[:, 2 * HD :])
            scores = jnp.where(present, dot3(qk, qk, NT) / HD, masked_score)
            weights = jnp.exp(scores - jnp.max(scores, axis=0, keepdims=True))
            weights = weights / jnp.sum(weights, axis=0, keepdims=True)
            slopes = dot3(value, upstream, NT)
            middle = jnp.sum(weights * slopes, axis=0, keepdims=True)
            slopes = weights * (slopes - middle)
            grad_qk = dot3(halves(slopes + slopes.T), qk) / HD
            grad_value = dot3(halves(weights), upstream)
            answer[:, index] = jnp.concatenate([grad_qk, grad_value], axis=1).reshape(
                groups, seat, 2 * HD
            )

    @pl.loop(0, groups)
    def _(group):
        here = pl.ds(pl.multiple_of(group * wide, wide), wide)
        upper, lower = halves(answer[group].reshape(TALL, 2 * HD))
        moved = dot(seats[group], jnp.concatenate([upper, lower], axis=1), TN)
        replies_ref[here, :] = moved[:, : 2 * HD] + moved[:, 2 * HD :]


def attend(rows, early, marks, room):
    groups = OWNERS // GROUP
    owned = TALL // (3 * GROUP)
    seat = 3 * GROUP
    return pl.pallas_call(
        attend_kernel,
        out_shape=jax.ShapeDtypeStruct((OWNERS * room, 2 * HD), f32),
        in_specs=[pl.BlockSpec(memory_space=pltpu.VMEM)] * 3,
        out_specs=pl.BlockSpec(memory_space=pltpu.VMEM),
        scratch_shapes=[
            pltpu.VMEM((groups, owned, seat, 3 * HD), f32),
            pltpu.VMEM((groups, TALL, GROUP * room), bf16),
            pltpu.VMEM((groups, owned, seat, LANES), f32),
            pltpu.VMEM((groups, owned, seat, 2 * HD), f32),
        ],
        compiler_params=pltpu.CompilerParams(vmem_limit_bytes=BIG),
        name="attend",
    )(marks, rows, early)


def unpack_rows(back, slots_ref, high, low, heads):
    source = jnp.concatenate(halves(back), axis=1)
    length = slots_ref.shape[0]
    for head in range(heads):
        place = lax.broadcasted_iota(jnp.int32, (length, back.shape[0]), 1)
        moved = dot(one(place == slots_ref[:, head : head + 1]), source)
        there = pl.ds(head * HD, HD)
        high[:, there], low[:, there] = halves(moved[:, :HD] + moved[:, HD:])


def line_of_sums(tokens, half, there, gradients):
    per_line = NZ * ROWS
    start = pl.multiple_of((half * NY + there) * per_line, per_line)
    sums = dot3(halves(tokens[:, pl.ds(start, per_line)]), gradients, TN)
    return sums.reshape(NZ, ROWS, sums.shape[1])


QK, VALUE, GRAD_VALUE, GRAD_QK = range(4)


def cluster_kernel(
    pay_ref, slots_ref, marks_ref, early_ref, tall_slots_ref, tokens_ref,
    back_qk_ref, high_ref, low_ref, own_ref,
    leaving, landed, seats, spread, valid, weights, answer, tokens, away, cross_in,
    local_sem, send_sem, recv_sem, cross_send, cross_recv,
):
    me = lax.axis_index("ctx")
    rep, y, _ = position()
    other = {"rep": 1 - rep}
    fetch = pltpu.make_async_copy(tokens_ref, tokens, local_sem.at[4])
    fetch.start()
    groups, _, wide = marks_ref.shape
    owned, seat = spread.shape[2], spread.shape[3]
    size = groups * seat
    rows = 4 * ROOM

    barrier = pltpu.get_barrier_semaphore()

    @pl.loop(1, OWNERS)
    def _(step):
        there = {"ctx": lax.rem(me + step, OWNERS)}
        pl.semaphore_signal(barrier, inc=1, device_id=there, device_id_type=MESH)

    pl.semaphore_signal(barrier, inc=1, device_id=other, device_id_type=MESH)

    def target(kind):
        return back_qk_ref if kind == GRAD_QK else landed.at[kind]

    def remote(kind, step):
        there = lax.rem(me + step, OWNERS)
        return pltpu.make_async_remote_copy(
            src_ref=leaving.at[kind, there],
            dst_ref=target(kind).at[me],
            send_sem=send_sem.at[kind, step],
            recv_sem=recv_sem.at[kind, step],
            device_id={"ctx": there},
            device_id_type=MESH,
        )

    def stay(kind):
        return pltpu.make_async_copy(leaving.at[kind, me], target(kind).at[me], local_sem.at[kind])

    def start(kind, there):
        @pl.when(there == me)
        def _():
            stay(kind).start()

        @pl.when(there != me)
        def _():
            remote(kind, lax.rem(there - me + OWNERS, OWNERS)).start()

    def arrive(kind):
        stay(kind).wait()

        @pl.loop(1, OWNERS)
        def _(step):
            remote(kind, step).wait_recv()

    def pack(kind, block):
        place = lax.broadcasted_iota(jnp.int32, (rows, slots_ref.shape[1]), 0) + block * rows
        moved = dot(one(place == slots_ref[...]), pay_ref[kind])
        moved = moved[:, :HD] + moved[:, HD:]
        for lane in range(4):
            leaving[kind, block * 4 + lane] = moved[lane * ROOM : (lane + 1) * ROOM]

    def take(kind, group, source):
        upper, lower = halves(source)
        moved = dot(seats[group], jnp.concatenate([upper, lower], axis=1))
        spread[kind, group] = (moved[:, :HD] + moved[:, HD:]).reshape(owned, seat, HD)

    def give(kind):
        @pl.loop(0, groups)
        def _(index):
            group = lax.rem(lax.div(me, GROUP) + index, groups)
            upper, lower = halves(answer[group].reshape(TALL, HD))
            moved = dot(seats[group], jnp.concatenate([upper, lower], axis=1), TN)
            moved = (moved[:, :HD] + moved[:, HD:]).reshape(GROUP, ROOM, HD)
            leaving[kind, pl.ds(group * GROUP, GROUP)] = moved
            for lane in range(GROUP):
                start(kind, group * GROUP + lane)

    def first_block():
        return lax.div(me, 4)

    pack(QK, first_block())
    pl.semaphore_wait(barrier, OWNERS)
    for lane in range(4):
        start(QK, first_block() * 4 + lane)

    @pl.loop(1, OWNERS // 4)
    def _(index):
        block = lax.rem(first_block() + index, OWNERS // 4)
        pack(QK, block)
        for lane in range(4):
            start(QK, block * 4 + lane)

    @pl.loop(0, OWNERS // 4)
    def _(block):
        pack(VALUE, block)

    @pl.loop(0, groups)
    def _(group):
        place = lax.broadcasted_iota(jnp.int32, (TALL, wide), 0)
        chosen = one(place == marks_ref[group])
        seats[group] = chosen
        early = early_ref[pl.ds(group * GROUP, GROUP), pl.ds(0, ROOM), :].reshape(wide, HD)
        upper, lower = halves(early)
        present = jnp.ones((wide, LANES), bf16)
        moved = dot(chosen, jnp.concatenate([upper, lower, present], axis=1))
        spread[2, group] = (moved[:, :HD] + moved[:, HD : 2 * HD]).reshape(owned, seat, HD)
        valid[group] = moved[:, 2 * HD :].reshape(owned, seat, LANES)

    arrive(QK)

    @pl.loop(0, OWNERS)
    def _(index):
        start(VALUE, lax.rem(me + index, OWNERS))

    @pl.loop(0, groups)
    def _(group):
        take(QK, group, landed[QK, pl.ds(group * GROUP, GROUP)].reshape(wide, HD))

    def cluster(kind, index):
        return halves(spread[kind, :, index].reshape(size, HD))

    @pl.loop(0, owned // 4)
    def _(block):
        for lane in range(4):
            index = block * 4 + lane
            present = valid[:, index].reshape(size, LANES)[:, :size] > 0.5
            qk = cluster(QK, index)
            scores = jnp.where(present, dot3(qk, qk, NT) / HD, masked_score)
            raised = jnp.exp(scores - jnp.max(scores, axis=0, keepdims=True))
            raised = raised / jnp.sum(raised, axis=0, keepdims=True)
            weights[index] = raised
            answer[:, index] = dot3(halves(raised), cluster(2, index)).reshape(groups, seat, HD)

    give(GRAD_VALUE)
    arrive(VALUE)

    @pl.loop(0, groups)
    def _(group):
        take(VALUE, group, landed[VALUE, pl.ds(group * GROUP, GROUP)].reshape(wide, HD))

    @pl.loop(0, owned // 4)
    def _(block):
        for lane in range(4):
            index = block * 4 + lane
            raised = weights[index]
            slopes = dot3(cluster(VALUE, index), cluster(2, index), NT)
            middle = jnp.sum(raised * slopes, axis=0, keepdims=True)
            slopes = raised * (slopes - middle)
            grad_qk = dot3(halves(slopes + slopes.T), cluster(QK, index)) / HD
            answer[:, index] = grad_qk.reshape(groups, seat, HD)

    give(GRAD_QK)
    arrive(GRAD_VALUE)

    back = landed[GRAD_VALUE].reshape(OWNERS * ROOM, HD)
    unpack_rows(back, tall_slots_ref, high_ref, low_ref, high_ref.shape[1] // HD)
    fetch.wait()

    def cross(step):
        there = lax.rem(y + step, NY)
        return pltpu.make_async_remote_copy(
            src_ref=away.at[there],
            dst_ref=cross_in.at[there],
            send_sem=cross_send.at[step],
            recv_sem=cross_recv.at[step],
            device_id=other,
            device_id_type=MESH,
        )

    @pl.loop(0, NY)
    def _(step):
        there = lax.rem(y + step, NY)
        away[there] = line_of_sums(tokens, 1 - rep, there, (high_ref[...], low_ref[...]))
        cross(step).start()

    @pl.loop(0, NY)
    def _(step):
        there = lax.rem(y + step, NY)
        mine = line_of_sums(tokens, rep, there, (high_ref[...], low_ref[...]))
        cross(step).wait_recv()
        own_ref[there] = mine + cross_in[there]

    arrive(GRAD_QK)

    @pl.loop(0, NY)
    def _(step):
        cross(step).wait_send()

    @pl.loop(1, OWNERS)
    def _(step):
        for kind in range(4):
            remote(kind, step).wait_send()


def cluster_part(pay, slots, marks, early, tall_slots, inputs):
    groups = OWNERS // GROUP
    owned = TALL // (3 * GROUP)
    seat = 3 * GROUP
    size = groups * seat
    length = inputs.shape[0]
    width = pay.shape[1] // length * HD
    vmem, anywhere = pl.BlockSpec(memory_space=pltpu.VMEM), pl.BlockSpec(memory_space=pl.ANY)
    return pl.pallas_call(
        cluster_kernel,
        out_shape=(
            jax.ShapeDtypeStruct((OWNERS, ROOM, HD), f32),
            jax.ShapeDtypeStruct((length, width), bf16),
            jax.ShapeDtypeStruct((length, width), bf16),
            jax.ShapeDtypeStruct((NY, NZ, ROWS, width), f32),
        ),
        in_specs=[vmem, vmem, vmem, vmem, vmem, anywhere],
        out_specs=(anywhere, vmem, vmem, vmem),
        scratch_shapes=[
            pltpu.VMEM((4, OWNERS, ROOM, HD), f32),
            pltpu.VMEM((3, OWNERS, ROOM, HD), f32),
            pltpu.VMEM((groups, TALL, GROUP * ROOM), bf16),
            pltpu.VMEM((3, groups, owned, seat, HD), f32),
            pltpu.VMEM((groups, owned, seat, LANES), f32),
            pltpu.VMEM((owned, size, size), f32),
            pltpu.VMEM((groups, owned, seat, HD), f32),
            pltpu.VMEM(inputs.shape, f32),
            pltpu.VMEM((NY, NZ, ROWS, width), f32),
            pltpu.VMEM((NY, NZ, ROWS, width), f32),
            pltpu.SemaphoreType.DMA((5,)),
            pltpu.SemaphoreType.DMA((4, OWNERS)),
            pltpu.SemaphoreType.DMA((4, OWNERS)),
            pltpu.SemaphoreType.DMA((NY,)),
            pltpu.SemaphoreType.DMA((NY,)),
        ],
        compiler_params=pltpu.CompilerParams(
            collective_id=2, has_side_effects=True, vmem_limit_bytes=BIG
        ),
        name="exchange_and_attend",
    )(pay, slots, marks, early, tall_slots, inputs)


def grads_kernel(
    back_qk_ref, back_value_ref, slots_ref, tokens_ref, full_ref, terms_ref, sums_ref, high, low
):
    length = tokens_ref.shape[0]
    width = high.shape[1] // 2
    total = back_qk_ref.shape[0]

    @pl.when(pl.program_id(0) == 0)
    def _():
        qk_upper, qk_lower = halves(back_qk_ref[...])
        upper, lower = halves(back_value_ref[...])
        source = jnp.concatenate([qk_upper, upper, qk_lower, lower], axis=1)
        for head in range(width // HD):
            place = lax.broadcasted_iota(jnp.int32, (length, total), 1)
            chosen = one(place == slots_ref[:, head : head + 1])
            both = dot(chosen, source)
            upper, lower = halves(both[:, : 2 * HD] + both[:, 2 * HD :])
            for part in range(2):
                there = pl.ds(part * width + head * HD, HD)
                high[:, there] = upper[:, part * HD : (part + 1) * HD]
                low[:, there] = lower[:, part * HD : (part + 1) * HD]

    combined = high[...], low[...]
    terms_ref[...] = dot3(combined, halves(full_ref[...]), NT)
    sums_ref[...] = dot3(halves(tokens_ref[...]), combined, TN)


def local_grads(back_qk, back_value, slots, inputs, full):
    length, depth = inputs.shape
    both = full.shape[1]
    total = back_qk.shape[0]
    return pl.pallas_call(
        grads_kernel,
        grid=(8,),
        out_shape=(
            jax.ShapeDtypeStruct((length, depth), f32),
            jax.ShapeDtypeStruct((depth, both), f32),
        ),
        in_specs=[
            pl.BlockSpec((total, HD), lambda i: (0, 0)),
            pl.BlockSpec((total, HD), lambda i: (0, 0)),
            pl.BlockSpec(slots.shape, lambda i: (0, 0)),
            pl.BlockSpec((length, depth // 8), lambda i: (0, i)),
            pl.BlockSpec((depth // 8, both), lambda i: (i, 0)),
        ],
        out_specs=(
            pl.BlockSpec((length, depth // 8), lambda i: (0, i)),
            pl.BlockSpec((depth // 8, both), lambda i: (i, 0)),
        ),
        scratch_shapes=[pltpu.VMEM((length, both), bf16)] * 2,
        compiler_params=pltpu.CompilerParams(vmem_limit_bytes=BIG),
        name="unpack_and_grads",
    )(back_qk, back_value, slots, inputs, full)


FINISH_COPIES = 2 + 14 + 14 + 4 + 6


def finish_kernel(
    back_qk_ref, high_ref, low_ref, sums_ref, slots_ref, tokens_ref, full_ref,
    tokens_out, qk_out, value_out,
    tokens, full, high, low, terms, away, own, cross_in,
    column_in, passing, ring_a, ring_b, line_in, plane_in,
    load_sem, send_sem, recv_sem, cross_send, cross_recv,
    line_send, line_recv,
):
    rep, y, z = position()
    x = lax.axis_index("tp")
    length = tokens.shape[0]
    both = full.shape[1]
    width = both // 2

    def along_y(step):
        return {"ctx": lax.rem(y + step, NY) * NZ + z}

    def along_z(step):
        return {"ctx": y * NZ + lax.rem(z + step, NZ)}

    def along_x(step):
        return {"tp": lax.rem(x + step, 4)}

    loads = [
        pltpu.make_async_copy(tokens_ref, tokens, load_sem.at[0]),
        pltpu.make_async_copy(full_ref, full, load_sem.at[1]),
        pltpu.make_async_copy(sums_ref, own.at[1], load_sem.at[2]),
    ]
    for load in reversed(loads):
        load.start()
    right, left, other = along_z(1), along_z(NZ - 1), {"rep": 1 - rep}
    barrier = pltpu.get_barrier_semaphore()
    partners = [along_y(1), along_y(2), along_y(3), right, left, other]
    partners += [along_x(1), along_x(3)]
    for partner in partners:
        pl.semaphore_signal(barrier, inc=1, device_id=partner, device_id_type=MESH)

    def cross(step):
        there = lax.rem(y + step, NY)
        return pltpu.make_async_remote_copy(
            src_ref=away.at[there],
            dst_ref=cross_in.at[there],
            send_sem=cross_send.at[step],
            recv_sem=cross_recv.at[step],
            device_id=other,
            device_id_type=MESH,
        )

    def line_sum(half, there):
        return line_of_sums(tokens, half, there, (high[:, :width], low[:, :width]))

    def away_lines():
        @pl.loop(0, NY)
        def _(step):
            there = lax.rem(y + step, NY)
            away[there] = line_sum(1 - rep, there)
            cross(step).start()

    def own_lines():
        @pl.loop(0, NY)
        def _(step):
            there = lax.rem(y + step, NY)
            mine = line_sum(rep, there)
            cross(step).wait_recv()
            own[0, there] = mine + cross_in[there]

    def depth(turn):
        return lax.rem(z + turn, NZ)

    def piece(step, turn, part):
        return pltpu.make_async_remote_copy(
            src_ref=own.at[part, lax.rem(y + step, NY), depth(turn), pl.ds(HALF, HALF), :],
            dst_ref=line_in.at[part, step - 1, depth(turn)],
            send_sem=line_send.at[part, step - 1, turn],
            recv_sem=line_recv.at[part, step - 1, turn],
            device_id=along_y(step),
            device_id_type=MESH,
        )

    def send_pieces(part):
        for turn in (4, 5, 3, 6, 2, 7, 1, 0):
            for step in (1, 3, 2):
                piece(step, turn, part).start()

    copies = Copies(send_sem, recv_sem)

    def plane(turn, part):
        return own.at[part, :, depth(turn), pl.ds(0, HALF), :]

    flow_a, flow_b = [None, None], [None, None]

    def turn_a(turn, part):
        ring = ring_a.at[part]
        if turn == 0:
            flow_a[part] = (
                copies.start(plane(4, part), ring.at[0], right),
                copies.start(plane(5, part), ring.at[4], left),
            )
            return
        rightward, leftward = flow_a[part]
        rightward.wait_recv()
        ring_a[part, turn - 1] += plane(4 - turn, part)[...]
        rightward = copies.start(ring.at[turn - 1], ring.at[turn], right)
        if turn < 3:
            leftward.wait_recv()
            ring_a[part, 3 + turn] += plane(5 + turn, part)[...]
            leftward = copies.start(ring.at[3 + turn], ring.at[4 + turn], left)
        flow_a[part] = rightward, leftward

    def along_lines(turn, part):
        for step in (1, 2, 3):
            piece(step, turn, part).wait_recv()
        here = depth(turn)
        return own[part, y, here, pl.ds(HALF, HALF), :] + (
            line_in[part, 0, here] + line_in[part, 1, here] + line_in[part, 2, here]
        )

    def turn_b(turn, part):
        ring = ring_b.at[part]
        if turn == 0:
            first = own.at[part, y, depth(4), pl.ds(HALF, HALF), :]
            second = own.at[part, y, depth(5), pl.ds(HALF, HALF), :]
            first[...] = along_lines(4, part)
            rightward = copies.start(first, ring.at[0], right)
            second[...] = along_lines(5, part)
            flow_b[part] = rightward, copies.start(second, ring.at[4], left)
            return
        rightward, leftward = flow_b[part]
        mine = along_lines(4 - turn, part)
        rightward.wait_recv()
        ring_b[part, turn - 1] += mine
        rightward = copies.start(ring.at[turn - 1], ring.at[turn], right)
        if turn < 3:
            mine = along_lines(5 + turn, part)
            leftward.wait_recv()
            ring_b[part, 3 + turn] += mine
            leftward = copies.start(ring.at[3 + turn], ring.at[4 + turn], left)
        flow_b[part] = rightward, leftward

    planes = [[], []]

    def end_a(part):
        for copy in flow_a[part]:
            copy.wait_recv()
        own[part, :, z, pl.ds(0, HALF), :] = plane(0, part)[...] + (
            ring_a[part, 3] + ring_a[part, 6]
        )
        for step in (1, 3, 2):
            planes[part].append(copies.start(
                own.at[part, lax.rem(y + step, NY), z, pl.ds(0, HALF), :],
                plane_in.at[part, step - 1],
                along_y(step),
            ))

    def end_b(part, out):
        mine = along_lines(0, part)
        for copy in flow_b[part]:
            copy.wait_recv()
        out[pl.ds(HALF, HALF), :] = mine + ring_b[part, 3] + ring_b[part, 6]

    middle = length // 2
    upper_rows, lower_rows = pl.ds(0, middle), pl.ds(middle, middle)

    def columns(step):
        start = pl.multiple_of(lax.rem(x + step, 4) * width, width)
        return dot3((high[...], low[...]), halves(full[pl.ds(start, width), :]), NT)

    pl.semaphore_wait(barrier, len(partners))
    loads[2].wait()
    turn_a(0, 1)
    send_pieces(1)
    high[:, pl.ds(width, width)] = high_ref[...]
    low[:, pl.ds(width, width)] = low_ref[...]
    unpack_rows(back_qk_ref[...], slots_ref, high, low, width // HD)
    loads[0].wait()
    away_lines()
    turn_a(1, 1)
    own_lines()
    turn_a(0, 0)
    send_pieces(0)
    turn_b(0, 1)
    turn_a(2, 1)
    loads[1].wait()
    terms[1] = columns(2)
    by_right = copies.start(terms.at[1, upper_rows], passing.at[0], along_x(1))
    by_left = copies.start(terms.at[1, lower_rows], passing.at[1], along_x(3))
    turn_b(1, 1)
    turn_a(1, 0)
    turn_a(3, 1)
    terms[0] = columns(1)
    sideways = [copies.start(terms.at[0, lower_rows], column_in.at[0, lower_rows], along_x(1))]
    turn_b(0, 0)
    turn_b(2, 1)
    turn_a(2, 0)
    terms[2] = columns(3)
    sideways.append(
        copies.start(terms.at[2, upper_rows], column_in.at[1, upper_rows], along_x(3))
    )
    turn_b(1, 0)
    end_a(1)
    turn_b(3, 1)
    turn_a(3, 0)
    by_right.wait_recv()
    terms[0, upper_rows, :] += passing[0]
    sideways.append(
        copies.start(terms.at[0, upper_rows], column_in.at[0, upper_rows], along_x(1))
    )
    by_left.wait_recv()
    terms[2, lower_rows, :] += passing[1]
    sideways.append(
        copies.start(terms.at[2, lower_rows], column_in.at[1, lower_rows], along_x(3))
    )
    turn_b(2, 0)
    end_b(1, value_out)
    tokens_out[...] = columns(0)
    turn_b(3, 0)
    end_a(0)
    end_b(0, qk_out)
    for copy in sideways:
        copy.wait_recv()

    @pl.loop(0, length // 8)
    def _(block):
        here = pl.ds(pl.multiple_of(block * 8, 8), 8)
        tokens_out[here, :] += column_in[0, here, :] + column_in[1, here, :]

    for part, out in ((1, value_out), (0, qk_out)):
        for copy in planes[part]:
            copy.wait_recv()
        out[pl.ds(0, HALF), :] = own[part, y, z, pl.ds(0, HALF), :] + (
            plane_in[part, 0] + plane_in[part, 1] + plane_in[part, 2]
        )

    @pl.loop(0, NY)
    def _(step):
        cross(step).wait_send()

    @pl.loop(1, NY)
    def _(step):
        for part in range(2):
            for turn in range(NZ):
                piece(step, turn, part).wait_send()

    copies.finish()
    assert len(copies.all) == FINISH_COPIES


def finish(back_qk, high, low, sums, slots, inputs, full):
    length, depth = inputs.shape
    both = full.shape[1]
    width = both // 2
    vmem, anywhere = pl.BlockSpec(memory_space=pltpu.VMEM), pl.BlockSpec(memory_space=pl.ANY)
    return pl.pallas_call(
        finish_kernel,
        out_shape=(
            jax.ShapeDtypeStruct((length, width), f32),
            jax.ShapeDtypeStruct((ROWS, width), f32),
            jax.ShapeDtypeStruct((ROWS, width), f32),
        ),
        in_specs=[vmem, vmem, vmem, anywhere, vmem, anywhere, anywhere],
        out_specs=(vmem,) * 3,
        scratch_shapes=[
            pltpu.VMEM((length, depth), f32),
            pltpu.VMEM((depth, both), f32),
            pltpu.VMEM((length, both), bf16),
            pltpu.VMEM((length, both), bf16),
            pltpu.VMEM((3, length, width), f32),
            pltpu.VMEM((NY, NZ, ROWS, width), f32),
            pltpu.VMEM((2, NY, NZ, ROWS, width), f32),
            pltpu.VMEM((NY, NZ, ROWS, width), f32),
            pltpu.VMEM((2, length, width), f32),
            pltpu.VMEM((2, length // 2, width), f32),
            pltpu.VMEM((2, 7, NY, HALF, width), f32),
            pltpu.VMEM((2, 7, HALF, width), f32),
            pltpu.VMEM((2, 3, NZ, HALF, width), f32),
            pltpu.VMEM((2, 3, HALF, width), f32),
            pltpu.SemaphoreType.DMA((3,)),
            pltpu.SemaphoreType.DMA((FINISH_COPIES,)),
            pltpu.SemaphoreType.DMA((FINISH_COPIES,)),
            pltpu.SemaphoreType.DMA((NY,)),
            pltpu.SemaphoreType.DMA((NY,)),
            pltpu.SemaphoreType.DMA((2, 3, NZ)),
            pltpu.SemaphoreType.DMA((2, 3, NZ)),
        ],
        compiler_params=pltpu.CompilerParams(
            collective_id=3, has_side_effects=True, vmem_limit_bytes=52 * 2**20
        ),
        name="grads_and_scatter",
    )(back_qk, high, low, sums, slots, inputs, full)


def exchange(array):
    return lax.all_to_all(array, "ctx", split_axis=0, concat_axis=0, tiled=True)


def seat_numbers(marks, room):
    marks = marks.astype(jnp.int32) - 1
    source = lax.broadcasted_iota(jnp.int32, marks.shape, 0) % GROUP
    seats = (marks // 3) * (3 * GROUP) + source * 3 + marks % 3
    return jnp.where(marks < 0, -1, seats).reshape(OWNERS // GROUP, 1, GROUP * room)


def snug_part(inputs, full, pay, early, slots, tall_slots):
    marks = early[:, ROOM : ROOM + 2, :ROOM]
    held, place = marks[:, 0], marks[:, 1]
    seats = jnp.where(held > 0.5, (held - 1) * (3 * GROUP) + place, -1.0).astype(jnp.int32)
    seats = seats.reshape(OWNERS // GROUP, 1, GROUP * ROOM)
    back_qk, high, low, sums = cluster_part(pay, slots, seats, early, tall_slots, inputs)
    back_qk = back_qk.reshape(OWNERS * ROOM, HD)
    return finish(back_qk, high, low, sums, tall_slots, inputs, full)


def roomy_part(inputs, full, upstream, cluster):
    heads, length = cluster.shape
    order = jnp.arange(length, dtype=jnp.int32)
    earlier = order[:, None] < order[None, :]
    alike = cluster[:, :, None] == cluster[:, None, :]
    within = jnp.sum((alike & earlier).astype(jnp.int32), axis=1)
    head = jnp.arange(heads, dtype=jnp.int32)[:, None]
    ids = (head * CL_DEV + cluster % CL_DEV) * 3 + within
    slots = cluster // CL_DEV * SLOTS + ids
    marks = jnp.zeros((OWNERS * SLOTS,), f32).at[slots.reshape(-1)].set(
        (ids + 1).astype(f32).reshape(-1)
    )
    rows = upstream.reshape(length, heads, HD).transpose(1, 0, 2).reshape(-1, HD)
    early = jnp.zeros((OWNERS * SLOTS, HD), f32).at[slots.reshape(-1)].set(rows)
    early = exchange(early.reshape(OWNERS, SLOTS, HD))
    marks = exchange(marks.reshape(OWNERS, SLOTS))
    rows = pack_rows(inputs, full, slots.reshape(1, -1), SLOTS)
    rows = exchange(rows.reshape(OWNERS, SLOTS, 2 * HD)).reshape(OWNERS * SLOTS, 2 * HD)
    replies = attend(rows, early, seat_numbers(marks, SLOTS), SLOTS)
    returned = exchange(replies.reshape(OWNERS, SLOTS, 2 * HD)).reshape(OWNERS * SLOTS, 2 * HD)
    return scatter_sums(
        *local_grads(returned[:, :HD], returned[:, HD:], slots.T, inputs, full)
    )


def per_device(tokens, qk_weight, value_weight, grad_out, assign):
    inputs = tokens[0]
    heads_here = qk_weight.shape[1] // HD
    width = heads_here * HD
    cluster = assign[:, 0, :, 0]
    full, early, slots, tall_slots, pay = gather_and_project(
        qk_weight, value_weight, jnp.pad(cluster, ((0, 8 - heads_here), (0, 0))), grad_out[0],
        inputs,
    )
    full = full.reshape(-1, 2 * width)
    fullest = jnp.max(early[:, ROOM, PITCH])

    def snug(inputs, full, upstream, cluster, *routed):
        return snug_part(inputs, full, *routed)

    def roomy(inputs, full, upstream, cluster, *routed):
        return roomy_part(inputs, full, upstream, cluster)

    grad_tokens, grad_qk_weight, grad_value_weight = lax.cond(
        fullest <= ROOM, snug, roomy,
        inputs, full, grad_out[0], cluster, pay, early, slots, tall_slots,
    )
    return (grad_tokens[None], grad_qk_weight, grad_value_weight)


def solution(mesh):
    in_specs = (
        P("rep", "ctx", None),
        P(("rep", "ctx"), "tp"),
        P(("rep", "ctx"), "tp"),
        P("rep", "ctx", "tp"),
        P("tp", "rep", "ctx", None),
    )
    out_specs = (P("rep", "ctx", "tp"), P(("rep", "ctx"), "tp"), P(("rep", "ctx"), "tp"))
    return jax.shard_map(
        per_device, mesh=mesh, in_specs=in_specs, out_specs=out_specs, check_vma=False
    )
```

```python
import jax
import jax.numpy as jnp
from jax import lax
from jax.experimental import pallas as pl
from jax.experimental.pallas import tpu as pltpu
from jax.sharding import PartitionSpec as P

HD = 128
CL_DEV = 8
NY = 4
NZ = 8
ROWS = 32
HALF = 16
MESH = pl.DeviceIdType.MESH

masked_score = -1e30
ROOM = 56
LANES = 128
GROUP = 8
SLOTS = 96
TALL = 768
f32, bf16 = jnp.float32, jnp.bfloat16
NN = (((1,), (0,)), ((), ()))
NT = (((1,), (1,)), ((), ()))
TN = (((0,), (0,)), ((), ()))
BIG = 48 * 2**20


def dot(left, right, dims=NN):
    return lax.dot_general(left, right, dims, preferred_element_type=f32)


def halves(matrix):
    upper = matrix.astype(bf16)
    return upper, (matrix - upper.astype(f32)).astype(bf16)


def dot3(left, right, dims=NN):
    a, b = left
    c, d = right
    first = jnp.concatenate([a, b, a], axis=dims[0][0][0])
    second = jnp.concatenate([c, c, d], axis=dims[0][1][0])
    return dot(first, second, dims)


def position():
    ctx = lax.axis_index("ctx")
    return lax.axis_index("rep"), lax.div(ctx, NZ), lax.rem(ctx, NZ)


def greet(partners):
    barrier = pltpu.get_barrier_semaphore()
    for partner in partners:
        pl.semaphore_signal(barrier, inc=1, device_id=partner, device_id_type=MESH)
    pl.semaphore_wait(barrier, len(partners))


class Copies:
    def __init__(self, send_sem, recv_sem):
        self.send_sem, self.recv_sem = send_sem, recv_sem
        self.all = []

    def start(self, source, target, device):
        index = len(self.all)
        copy = pltpu.make_async_remote_copy(
            src_ref=source,
            dst_ref=target,
            send_sem=self.send_sem.at[index],
            recv_sem=self.recv_sem.at[index],
            device_id=device,
            device_id_type=MESH,
        )
        copy.start()
        self.all.append(copy)
        return copy

    def finish(self):
        for copy in self.all:
            copy.wait_send()


GATHER_COPIES = 6 + 7 + 14 + 21 + 16 + 4
ROUTE_COPIES = 3 + 7 + 3 + 1
CLUSTERS = 256
OWNERS = 32
PITCH = 64


def count_rows(cluster_ref, heads):
    length = cluster_ref.shape[1]
    line = lax.broadcasted_iota(jnp.int32, (8, length), 0)
    counts = jnp.zeros((8, CLUSTERS), f32)
    for head in range(heads):
        counts += dot(one(line == head), members(cluster_ref, head), NT)
    return counts


def one(condition):
    return jnp.where(condition, 1.0, 0.0).astype(bf16)


def members(cluster_ref, head):
    length = cluster_ref.shape[1]
    label = lax.broadcasted_iota(jnp.int32, (CLUSTERS, length), 0)
    return one(label == cluster_ref[head : head + 1, :])


def deal_order(counts):
    lane = lax.broadcasted_iota(jnp.int32, counts.shape, 1)
    return counts * CLUSTERS + (CLUSTERS - 1 - lane).astype(f32)


def route_head(cluster_ref, head, keys, tall_keys, earlier, base):
    larger = jnp.where(tall_keys[:, head : head + 1] > keys[head : head + 1, :], 1.0, 0.0)
    place = jnp.sum(larger, axis=0, keepdims=True).astype(jnp.int32)
    turn = place // OWNERS
    seat = place % OWNERS
    seat = jnp.where(turn % 2 == 0, seat, OWNERS - 1 - seat)
    seat = (seat + 8 * head) % OWNERS
    line = lax.broadcasted_iota(jnp.int32, (8, CLUSTERS), 0)
    table = jnp.where(line == 0, seat, jnp.where(line == 1, turn, 0)).astype(f32).astype(bf16)
    chosen = members(cluster_ref, head)
    looked = dot(table, chosen).astype(jnp.int32)
    owner, turn = looked[0:1, :], looked[1:2, :]
    within = jnp.sum(chosen.astype(f32) * dot(chosen, earlier), axis=0, keepdims=True)
    label = lax.broadcasted_iota(jnp.int32, (OWNERS, owner.shape[1]), 0)
    owned = one(label == owner)
    many = owned.astype(f32)
    rank = jnp.sum(many * (dot(owned, earlier) + base), axis=0, keepdims=True)
    base = base + jnp.sum(many, axis=1, keepdims=True)
    return owner, rank.astype(jnp.int32), head * CL_DEV + turn, within, base


def gather_kernel(
    qk_ref, value_ref, cluster_ref, grad_ref, tokens_ref,
    full_ref, early_ref, slots_ref, tall_slots_ref, pay_ref,
    out_ref, tokens, acc, counts_y, counts_z, most, ids_row, slots_row, pay, early_out,
    local_sem, send_sem, recv_sem, route_send, route_recv, early_send, early_recv,
):
    rep, y, z = position()
    me = lax.axis_index("ctx")
    x = lax.axis_index("tp")
    width = qk_ref.shape[1]
    heads = width // HD
    length = cluster_ref.shape[1]

    def along_y(step):
        return {"ctx": lax.rem(y + step, NY) * NZ + z}

    def along_z(step):
        return {"ctx": y * NZ + lax.rem(z + step, NZ)}

    def along_x(step):
        return {"tp": lax.rem(x + step, 4)}

    def around(step):
        return {"ctx": lax.rem(me + step, OWNERS)}

    def plane(step, part):
        there = pl.ds(part * width, width)
        return out_ref.at[rep, :, lax.rem(z + step, NZ), pl.ds(0, HALF), there]

    def piece(step):
        return out_ref.at[rep, y, lax.rem(z + step, NZ), pl.ds(HALF, HALF), :]

    def line(step):
        return out_ref.at[rep, lax.rem(y + step, NY), :, pl.ds(HALF, HALF), :]

    right, left, other = along_z(1), along_z(NZ - 1), {"rep": 1 - rep}
    mine = out_ref.at[rep, y, z]
    fetch = pltpu.make_async_copy(tokens_ref, tokens, local_sem.at[2])
    fetch.start()
    first = pltpu.make_async_copy(qk_ref, mine.at[:, pl.ds(0, width)], local_sem.at[0])
    second = pltpu.make_async_copy(value_ref, mine.at[:, pl.ds(width, width)], local_sem.at[1])
    first.start()
    second.start()
    barrier = pltpu.get_barrier_semaphore()

    @pl.loop(1, OWNERS)
    def _(step):
        pl.semaphore_signal(barrier, inc=1, device_id=around(step), device_id_type=MESH)

    for partner in (other, along_x(1), along_x(2), along_x(3)):
        pl.semaphore_signal(barrier, inc=1, device_id=partner, device_id_type=MESH)
    counts_y[0] = count_rows(cluster_ref, heads)
    pl.semaphore_wait(barrier, OWNERS - 1 + 4)

    routes = Copies(route_send, route_recv)
    counted = [
        routes.start(counts_y.at[0], counts_y.at[step], along_y(step)) for step in (1, 2, 3)
    ]
    first.wait()
    second.wait()
    copies = Copies(send_sem, recv_sem)
    top, bottom = mine.at[pl.ds(0, HALF), :], mine.at[pl.ds(HALF, HALF), :]
    shared = [copies.start(top, top, along_y(step)) for step in (1, 3, 2)]
    pieces = [(copies.start(piece(0), piece(0), right), copies.start(piece(0), piece(0), left))]

    below = [copies.start(bottom, bottom, along_y(step)) for step in (1, 3, 2)]

    for head in range(heads):
        upper, lower = halves(grad_ref[:, head * HD : (head + 1) * HD])
        pay[pl.ds(head * length, length), :HD] = upper
        pay[pl.ds(head * length, length), HD:] = lower

    for copy in counted:
        copy.wait_recv()
    counts_z[0] = counts_y[0] + counts_y[1] + counts_y[2] + counts_y[3]
    counted = [
        routes.start(counts_z.at[0], counts_z.at[step], along_z(step)) for step in range(1, NZ)
    ]
    for copy in shared:
        copy.wait_recv()
    planes = []
    for part in range(2):
        here = plane(0, part)
        planes.append([(copies.start(here, here, right), copies.start(here, here, left))])
    across = [copies.start(plane(0, part), plane(0, part), other) for part in range(2)]
    passed = {1: [], 2: [], 3: []}

    def pass_on(here):
        for step in (1, 3, 2):
            passed[step].append(copies.start(here, here, along_y(step)))

    def turn_pieces(step):
        rightward, leftward = pieces[step]
        after, before = piece(NZ - 1 - step), piece(1 + step)
        rightward.wait_recv()
        if leftward is not None:
            leftward.wait_recv()
        if step < 3:
            pieces.append((
                copies.start(after, after, right),
                copies.start(before, before, left) if step < 2 else None,
            ))
        pass_on(after)
        if leftward is not None:
            pass_on(before)

    def turn_planes(step):
        for part in range(2):
            turn_plane(step, part)

    def turn_plane(step, part):
        rightward, leftward = planes[part][step]
        after, before = plane(NZ - 1 - step, part), plane(1 + step, part)
        rightward.wait_recv()
        if step < 3:
            going = copies.start(after, after, right)
        if leftward is not None:
            leftward.wait_recv()
            coming = copies.start(before, before, left) if step < 2 else None
        if step < 3:
            planes[part].append((going, coming if step < 2 else None))
        across.append(copies.start(after, after, other))
        if leftward is not None:
            across.append(copies.start(before, before, other))

    turn_pieces(0)
    for copy in counted:
        copy.wait_recv()
    total = counts_z[0]
    for step in range(1, NZ):
        total += counts_z[step]
    keys = deal_order(total)
    tall_keys = jnp.concatenate([keys] + [jnp.zeros_like(keys)] * 15, axis=0).T
    earlier = one(
        lax.broadcasted_iota(jnp.int32, (length, length), 0)
        < lax.broadcasted_iota(jnp.int32, (length, length), 1)
    )
    base = jnp.zeros((OWNERS, 1), f32)
    highest = jnp.zeros((1, 1), f32)
    row = lax.broadcasted_iota(jnp.int32, (8, length), 0)
    slots_list = []
    for head in range(heads):
        owner, rank, held, within, base = route_head(
            cluster_ref, head, keys, tall_keys, earlier, base
        )
        highest = jnp.maximum(highest, jnp.max(rank.astype(f32), axis=1, keepdims=True) + 1)
        here = pl.ds(head * length, length)
        slots_ref[:, here] = jnp.where(rank < ROOM, owner * ROOM + rank, -1)
        slots_row[:, here] = jnp.where(rank < ROOM, owner * PITCH + rank, -1)
        within = within + (3 * lax.rem(me, GROUP)).astype(f32)
        marked = jnp.where(row == 0, (held + 1).astype(f32), jnp.where(row == 1, within, 0.0))
        ids_row[:, here] = marked.astype(bf16)
        slots_list.append(jnp.where(rank < ROOM, owner * ROOM + rank, -1))
    most[0] = jnp.broadcast_to(highest, (8, LANES))
    tall = jnp.concatenate(
        slots_list + [jnp.zeros((LANES - heads, length), jnp.int32)], axis=0
    )
    tall_slots_ref[...] = tall.astype(f32).T.astype(jnp.int32)
    fullest = [routes.start(most.at[0], most.at[step], along_x(step)) for step in (1, 2, 3)]
    turn_pieces(1)
    turn_planes(0)

    def pack_early(block):
        rows = 4 * PITCH
        place = lax.broadcasted_iota(jnp.int32, (rows, heads * length), 0) + block * rows
        chosen = one(place == slots_row[...])
        both = dot(chosen, pay[...])
        both = both[:, :HD] + both[:, HD:]
        marks = dot(ids_row[...], chosen, NT)
        for lane in range(4):
            early_out[block * 4 + lane] = both[lane * PITCH : (lane + 1) * PITCH]
            early_out[block * 4 + lane, pl.ds(ROOM, 8), pl.ds(0, PITCH)] = marks[
                :, lane * PITCH : (lane + 1) * PITCH
            ]

    @pl.loop(0, OWNERS // 8)
    def _(block):
        pack_early(block)

    for copy in fullest:
        copy.wait_recv()
    most[4] = jnp.maximum(jnp.maximum(most[0], most[1]), jnp.maximum(most[2], most[3]))
    fullest = routes.start(most.at[4], most.at[5], other)
    turn_pieces(2)

    @pl.loop(OWNERS // 8, OWNERS // 4)
    def _(block):
        pack_early(block)

    turn_pieces(3)
    turn_planes(1)
    across.append(copies.start(line(0), line(0), other))
    fullest.wait_recv()
    overall = jnp.maximum(most[4], most[5])[:, :PITCH]

    @pl.loop(0, OWNERS)
    def _(block):
        early_out[block, pl.ds(ROOM, 8), pl.ds(PITCH, PITCH)] = overall

    def early(step):
        there = lax.rem(me + step, OWNERS)
        return pltpu.make_async_remote_copy(
            src_ref=early_out.at[there],
            dst_ref=early_ref.at[me],
            send_sem=early_send.at[step],
            recv_sem=early_recv.at[step],
            device_id={"ctx": there},
            device_id_type=MESH,
        )

    @pl.loop(1, OWNERS // 4)
    def _(step):
        early(step).start()

    stay = pltpu.make_async_copy(early_out.at[me], early_ref.at[me], local_sem.at[0])
    stay.start()
    turn_planes(2)
    turn_planes(3)

    @pl.loop(OWNERS // 4, OWNERS)
    def _(step):
        early(step).start()

    for copy in below:
        copy.wait_recv()
    for step in (1, 3, 2):
        for copy in passed[step]:
            copy.wait_recv()
        across.append(copies.start(line(NY - step), line(NY - step), other))
    fetch.wait()

    def project(half, there):
        start = pl.multiple_of((half * NY + there) * (NZ * ROWS), NZ * ROWS)
        some = halves(tokens[:, pl.ds(start, NZ * ROWS)])
        return dot3(some, halves(out_ref[half, there].reshape(NZ * ROWS, 2 * width)))

    acc[...] = project(rep, 0)

    @pl.loop(1, NY)
    def _(there):
        acc[...] += project(rep, there)

    for copy in across:
        copy.wait_recv()
    save = pltpu.make_async_copy(out_ref, full_ref, local_sem.at[1])
    save.start()

    @pl.loop(0, NY)
    def _(there):
        acc[...] += project(1 - rep, there)

    for part in range(2):
        for head in range(heads):
            here = pl.ds(head * length, length)
            column = part * width + head * HD
            upper, lower = halves(acc[:, column : column + HD])
            pay_ref[part, here, :HD] = upper
            pay_ref[part, here, HD:] = lower
    copies.finish()
    routes.finish()
    stay.wait()
    save.wait()

    @pl.loop(1, OWNERS)
    def _(step):
        early(step).wait()

    assert len(copies.all) == GATHER_COPIES and len(routes.all) == ROUTE_COPIES


def gather_and_project(qk_weight, value_weight, clusters, upstream, inputs):
    width = qk_weight.shape[1]
    length = clusters.shape[1]
    rows = width // HD * length
    vmem, anywhere = pl.BlockSpec(memory_space=pltpu.VMEM), pl.BlockSpec(memory_space=pl.ANY)
    return pl.pallas_call(
        gather_kernel,
        out_shape=(
            jax.ShapeDtypeStruct((2, NY, NZ, ROWS, 2 * width), f32),
            jax.ShapeDtypeStruct((OWNERS, PITCH, HD), f32),
            jax.ShapeDtypeStruct((1, rows), jnp.int32),
            jax.ShapeDtypeStruct((length, LANES), jnp.int32),
            jax.ShapeDtypeStruct((2, rows, 2 * HD), bf16),
        ),
        in_specs=[anywhere, anywhere, vmem, vmem, anywhere],
        out_specs=(anywhere, anywhere, vmem, vmem, vmem),
        scratch_shapes=[
            pltpu.VMEM((2, NY, NZ, ROWS, 2 * width), f32),
            pltpu.VMEM(inputs.shape, f32),
            pltpu.VMEM((length, 2 * width), f32),
            pltpu.VMEM((NY, 8, CLUSTERS), f32),
            pltpu.VMEM((NZ, 8, CLUSTERS), f32),
            pltpu.VMEM((6, 8, LANES), f32),
            pltpu.VMEM((8, rows), bf16),
            pltpu.VMEM((1, rows), jnp.int32),
            pltpu.VMEM((rows, 2 * HD), bf16),
            pltpu.VMEM((OWNERS, PITCH, HD), f32),
            pltpu.SemaphoreType.DMA((3,)),
            pltpu.SemaphoreType.DMA((GATHER_COPIES,)),
            pltpu.SemaphoreType.DMA((GATHER_COPIES,)),
            pltpu.SemaphoreType.DMA((ROUTE_COPIES,)),
            pltpu.SemaphoreType.DMA((ROUTE_COPIES,)),
            pltpu.SemaphoreType.DMA((OWNERS,)),
            pltpu.SemaphoreType.DMA((OWNERS,)),
        ],
        compiler_params=pltpu.CompilerParams(
            collective_id=0, has_side_effects=True, vmem_limit_bytes=60 * 2**20
        ),
        name="gather_and_project",
    )(qk_weight, value_weight, clusters, upstream, inputs)


SCATTER_COPIES = 3 + 12 + 7 + 3 + 7 + 3


def scatter_kernel(
    terms_ref, sums_ref, tokens_out, qk_out, value_out,
    column_in, cross_in, ring_a, ring_b, line_in, plane_in,
    local_sem, send_sem, recv_sem,
):
    rep, y, z = position()
    x = lax.axis_index("tp")
    width = qk_out.shape[1]

    def along_y(step):
        return {"ctx": lax.rem(y + step, NY) * NZ + z}

    def along_z(step):
        return {"ctx": y * NZ + lax.rem(z + step, NZ)}

    def along_x(step):
        return {"tp": lax.rem(x + step, 4)}

    def columns(step):
        start = pl.multiple_of(lax.rem(x + step, 4) * width, width)
        return terms_ref.at[:, pl.ds(start, width)]

    def plane(step):
        return cross_in.at[:, lax.rem(z + step, NZ), pl.ds(0, HALF), :]

    def line(step):
        return cross_in.at[lax.rem(y + step, NY), :, pl.ds(HALF, HALF), :]

    def piece(step):
        return cross_in.at[y, lax.rem(z + step, NZ), pl.ds(HALF, HALF), :]

    right, left, other = along_z(1), along_z(NZ - 1), {"rep": 1 - rep}
    greet(
        [along_y(1), along_y(2), along_y(3), right, left, other]
        + [along_x(1), along_x(2), along_x(3)]
    )
    copies = Copies(send_sem, recv_sem)
    sideways = [
        copies.start(columns(step), column_in.at[step - 1], along_x(step)) for step in (1, 3, 2)
    ]
    own_columns = pltpu.make_async_copy(columns(0), tokens_out, local_sem)
    own_columns.start()

    cross = {}
    for kind, step in (
        ("a", 4), ("a", 5), ("b", 1), ("b", 3), ("b", 2), ("a", 3),
        ("a", 6), ("a", 2), ("a", 7), ("b", 0), ("a", 1), ("a", 0),
    ):
        if kind == "a":
            there = lax.rem(z + step, NZ)
            source = sums_ref.at[1 - rep, :, there, pl.ds(0, HALF), :]
            cross[kind, step] = copies.start(source, plane(step), other)
        else:
            there = lax.rem(y + step, NY)
            source = sums_ref.at[1 - rep, there, :, pl.ds(HALF, HALF), :]
            cross[kind, step] = copies.start(source, line(step), other)

    def add_plane(step):
        cross["a", step].wait_recv()
        there = lax.rem(z + step, NZ)
        cross_in[:, there, pl.ds(0, HALF), :] += sums_ref[rep, :, there, pl.ds(0, HALF), :]

    def add_line(step):
        cross["b", step].wait_recv()
        there = lax.rem(y + step, NY)
        cross_in[there, :, pl.ds(HALF, HALF), :] += sums_ref[
            rep, there, :, pl.ds(HALF, HALF), :
        ]

    add_plane(4)
    right_a = copies.start(plane(4), ring_a.at[0], right)
    add_plane(5)
    left_a = copies.start(plane(5), ring_a.at[4], left)
    lines = []
    for step in (1, 3, 2):
        add_line(step)
        lines.append(copies.start(line(step), line_in.at[step - 1], along_y(step)))

    def pass_a(turn):
        nonlocal right_a, left_a
        add_plane(4 - turn)
        right_a.wait_recv()
        ring_a[turn - 1] += cross_in[:, lax.rem(z + 4 - turn, NZ), pl.ds(0, HALF), :]
        right_a = copies.start(ring_a.at[turn - 1], ring_a.at[turn], right)
        if turn < 3:
            add_plane(5 + turn)
            left_a.wait_recv()
            ring_a[3 + turn] += cross_in[:, lax.rem(z + 5 + turn, NZ), pl.ds(0, HALF), :]
            left_a = copies.start(ring_a.at[3 + turn], ring_a.at[4 + turn], left)

    pass_a(1)
    add_line(0)
    pass_a(2)
    for copy in lines:
        copy.wait_recv()
    cross_in[y, :, pl.ds(HALF, HALF), :] += line_in[0] + line_in[1] + line_in[2]
    right_b = copies.start(piece(4), ring_b.at[0], right)
    left_b = copies.start(piece(5), ring_b.at[4], left)
    pass_a(3)

    def pass_b(turn):
        nonlocal right_b, left_b
        right_b.wait_recv()
        ring_b[turn - 1] += cross_in[y, lax.rem(z + 4 - turn, NZ), pl.ds(HALF, HALF), :]
        right_b = copies.start(ring_b.at[turn - 1], ring_b.at[turn], right)
        if turn < 3:
            left_b.wait_recv()
            ring_b[3 + turn] += cross_in[y, lax.rem(z + 5 + turn, NZ), pl.ds(HALF, HALF), :]
            left_b = copies.start(ring_b.at[3 + turn], ring_b.at[4 + turn], left)

    pass_b(1)
    pass_b(2)
    add_plane(0)
    right_a.wait_recv()
    left_a.wait_recv()
    cross_in[:, z, pl.ds(0, HALF), :] += ring_a[3] + ring_a[6]
    planes = [
        copies.start(
            cross_in.at[lax.rem(y + step, NY), z, pl.ds(0, HALF), :],
            plane_in.at[step - 1],
            along_y(step),
        )
        for step in (1, 3, 2)
    ]
    pass_b(3)
    right_b.wait_recv()
    left_b.wait_recv()
    lower = cross_in[y, z, pl.ds(HALF, HALF), :] + ring_b[3] + ring_b[6]
    qk_out[pl.ds(HALF, HALF), :] = lower[:, :width]
    value_out[pl.ds(HALF, HALF), :] = lower[:, width:]
    for copy in planes:
        copy.wait_recv()
    upper = cross_in[y, z, pl.ds(0, HALF), :] + plane_in[0] + plane_in[1] + plane_in[2]
    qk_out[pl.ds(0, HALF), :] = upper[:, :width]
    value_out[pl.ds(0, HALF), :] = upper[:, width:]
    own_columns.wait()
    for copy in sideways:
        copy.wait_recv()

    @pl.loop(0, tokens_out.shape[0] // 8)
    def _(block):
        here = pl.ds(pl.multiple_of(block * 8, 8), 8)
        tokens_out[here, :] += column_in[0, here, :] + column_in[1, here, :] + column_in[2, here, :]

    copies.finish()
    assert len(copies.all) == SCATTER_COPIES


def scatter_sums(token_terms, weight_terms):
    length = token_terms.shape[0]
    both = weight_terms.shape[1]
    width = both // 2
    return pl.pallas_call(
        scatter_kernel,
        out_shape=(
            jax.ShapeDtypeStruct((length, width), f32),
            jax.ShapeDtypeStruct((ROWS, width), f32),
            jax.ShapeDtypeStruct((ROWS, width), f32),
        ),
        in_specs=[pl.BlockSpec(memory_space=pl.ANY), pl.BlockSpec(memory_space=pltpu.VMEM)],
        out_specs=(pl.BlockSpec(memory_space=pltpu.VMEM),) * 3,
        scratch_shapes=[
            pltpu.VMEM((3, length, width), f32),
            pltpu.VMEM((NY, NZ, ROWS, both), f32),
            pltpu.VMEM((7, NY, HALF, both), f32),
            pltpu.VMEM((7, HALF, both), f32),
            pltpu.VMEM((3, NZ, HALF, both), f32),
            pltpu.VMEM((3, HALF, both), f32),
            pltpu.SemaphoreType.DMA,
            pltpu.SemaphoreType.DMA((SCATTER_COPIES,)),
            pltpu.SemaphoreType.DMA((SCATTER_COPIES,)),
        ],
        compiler_params=pltpu.CompilerParams(
            collective_id=1, has_side_effects=True, vmem_limit_bytes=48 * 2**20
        ),
        name="scatter_sums",
    )(token_terms, weight_terms.reshape(2, NY, NZ, ROWS, both))


def pack_kernel(tokens_ref, full_ref, slots_ref, rows_ref, acc, pay):
    step = pl.program_id(0)
    length, both = acc.shape
    rows = rows_ref.shape[0]

    @pl.when(step == 0)
    def _():
        acc[...] = jnp.zeros_like(acc)

    @pl.when(step < 8)
    def _():
        acc[...] += dot3(halves(tokens_ref[...]), halves(full_ref[...]))

    @pl.when(step == 7)
    def _():
        for head in range(both // (2 * HD)):
            here = pl.ds(head * length, length)
            for part in range(2):
                column = part * both // 2 + head * HD
                upper, lower = halves(acc[:, column : column + HD])
                pay[here, part * HD : (part + 1) * HD] = upper
                pay[here, (2 + part) * HD : (3 + part) * HD] = lower

    @pl.when(step >= 8)
    def _():
        place = lax.broadcasted_iota(jnp.int32, (rows, slots_ref.shape[1]), 0) + (step - 8) * rows
        moved = dot(one(place == slots_ref[...]), pay[...])
        rows_ref[...] = moved[:, : 2 * HD] + moved[:, 2 * HD :]


def pack_rows(inputs, full, slots, room):
    length, depth = inputs.shape
    both = full.shape[1]
    total = slots.shape[1]
    return pl.pallas_call(
        pack_kernel,
        grid=(16,),
        out_shape=jax.ShapeDtypeStruct((OWNERS * room, 2 * HD), f32),
        in_specs=[
            pl.BlockSpec((length, depth // 8), lambda i: (0, jnp.minimum(i, 7))),
            pl.BlockSpec((depth // 8, both), lambda i: (jnp.minimum(i, 7), 0)),
            pl.BlockSpec((1, total), lambda i: (0, 0)),
        ],
        out_specs=pl.BlockSpec((4 * room, 2 * HD), lambda i: (jnp.maximum(i - 8, 0), 0)),
        scratch_shapes=[pltpu.VMEM((length, both), f32), pltpu.VMEM((total, 4 * HD), bf16)],
        compiler_params=pltpu.CompilerParams(vmem_limit_bytes=BIG),
        name="project_and_pack",
    )(inputs, full, slots)


def attend_kernel(marks_ref, rows_ref, early_ref, replies_ref, spread, seats, valid, answer):
    groups = marks_ref.shape[0]
    wide = marks_ref.shape[2]
    owned = spread.shape[1]
    seat = spread.shape[2]
    size = groups * seat

    @pl.loop(0, groups)
    def _(group):
        here = pl.ds(pl.multiple_of(group * wide, wide), wide)
        place = lax.broadcasted_iota(jnp.int32, (TALL, wide), 0)
        chosen = one(place == marks_ref[group])
        seats[group] = chosen
        upper, lower = halves(rows_ref[here, :])
        early = early_ref[pl.ds(group * GROUP, GROUP), pl.ds(0, wide // GROUP), :]
        early_upper, early_lower = halves(early.reshape(wide, HD))
        present = jnp.ones((wide, LANES), bf16)
        moved = dot(
            chosen, jnp.concatenate([upper, early_upper, lower, early_lower, present], axis=1)
        )
        spread[group] = (moved[:, : 3 * HD] + moved[:, 3 * HD : 6 * HD]).reshape(owned, seat, 3 * HD)
        valid[group] = moved[:, 6 * HD :].reshape(owned, seat, LANES)

    @pl.loop(0, owned // 4)
    def _(block):
        for lane in range(4):
            index = block * 4 + lane
            rows = spread[:, index].reshape(size, 3 * HD)
            present = valid[:, index].reshape(size, LANES)[:, :size] > 0.5
            qk = halves(rows[:, :HD])
            value = halves(rows[:, HD : 2 * HD])
            upstream = halves(rows[:, 2 * HD :])
            scores = jnp.where(present, dot3(qk, qk, NT) / HD, masked_score)
            weights = jnp.exp(scores - jnp.max(scores, axis=0, keepdims=True))
            weights = weights / jnp.sum(weights, axis=0, keepdims=True)
            slopes = dot3(value, upstream, NT)
            middle = jnp.sum(weights * slopes, axis=0, keepdims=True)
            slopes = weights * (slopes - middle)
            grad_qk = dot3(halves(slopes + slopes.T), qk) / HD
            grad_value = dot3(halves(weights), upstream)
            answer[:, index] = jnp.concatenate([grad_qk, grad_value], axis=1).reshape(
                groups, seat, 2 * HD
            )

    @pl.loop(0, groups)
    def _(group):
        here = pl.ds(pl.multiple_of(group * wide, wide), wide)
        upper, lower = halves(answer[group].reshape(TALL, 2 * HD))
        moved = dot(seats[group], jnp.concatenate([upper, lower], axis=1), TN)
        replies_ref[here, :] = moved[:, : 2 * HD] + moved[:, 2 * HD :]


def attend(rows, early, marks, room):
    groups = OWNERS // GROUP
    owned = TALL // (3 * GROUP)
    seat = 3 * GROUP
    return pl.pallas_call(
        attend_kernel,
        out_shape=jax.ShapeDtypeStruct((OWNERS * room, 2 * HD), f32),
        in_specs=[pl.BlockSpec(memory_space=pltpu.VMEM)] * 3,
        out_specs=pl.BlockSpec(memory_space=pltpu.VMEM),
        scratch_shapes=[
            pltpu.VMEM((groups, owned, seat, 3 * HD), f32),
            pltpu.VMEM((groups, TALL, GROUP * room), bf16),
            pltpu.VMEM((groups, owned, seat, LANES), f32),
            pltpu.VMEM((groups, owned, seat, 2 * HD), f32),
        ],
        compiler_params=pltpu.CompilerParams(vmem_limit_bytes=BIG),
        name="attend",
    )(marks, rows, early)


def unpack_rows(back, slots_ref, high, low, heads):
    source = jnp.concatenate(halves(back), axis=1)
    length = slots_ref.shape[0]
    for head in range(heads):
        place = lax.broadcasted_iota(jnp.int32, (length, back.shape[0]), 1)
        moved = dot(one(place == slots_ref[:, head : head + 1]), source)
        there = pl.ds(head * HD, HD)
        high[:, there], low[:, there] = halves(moved[:, :HD] + moved[:, HD:])


def line_of_sums(tokens, half, there, gradients):
    per_line = NZ * ROWS
    start = pl.multiple_of((half * NY + there) * per_line, per_line)
    sums = dot3(halves(tokens[:, pl.ds(start, per_line)]), gradients, TN)
    return sums.reshape(NZ, ROWS, sums.shape[1])


QK, VALUE, GRAD_VALUE, GRAD_QK = range(4)


def cluster_kernel(
    pay_ref, slots_ref, marks_ref, early_ref, tall_slots_ref, tokens_ref,
    back_qk_ref, high_ref, low_ref, sums_ref,
    leaving, landed, seats, spread, valid, weights, answer, tokens, away, cross_in, own,
    local_sem, send_sem, recv_sem, cross_send, cross_recv,
):
    me = lax.axis_index("ctx")
    rep, y, _ = position()
    other = {"rep": 1 - rep}
    fetch = pltpu.make_async_copy(tokens_ref, tokens, local_sem.at[4])
    fetch.start()
    groups, _, wide = marks_ref.shape
    owned, seat = spread.shape[2], spread.shape[3]
    size = groups * seat
    rows = 4 * ROOM

    barrier = pltpu.get_barrier_semaphore()

    @pl.loop(1, OWNERS)
    def _(step):
        there = {"ctx": lax.rem(me + step, OWNERS)}
        pl.semaphore_signal(barrier, inc=1, device_id=there, device_id_type=MESH)

    pl.semaphore_signal(barrier, inc=1, device_id=other, device_id_type=MESH)

    def target(kind):
        return back_qk_ref if kind == GRAD_QK else landed.at[kind]

    def remote(kind, step):
        there = lax.rem(me + step, OWNERS)
        return pltpu.make_async_remote_copy(
            src_ref=leaving.at[kind, there],
            dst_ref=target(kind).at[me],
            send_sem=send_sem.at[kind, step],
            recv_sem=recv_sem.at[kind, step],
            device_id={"ctx": there},
            device_id_type=MESH,
        )

    def stay(kind):
        return pltpu.make_async_copy(leaving.at[kind, me], target(kind).at[me], local_sem.at[kind])

    def start(kind, there):
        @pl.when(there == me)
        def _():
            stay(kind).start()

        @pl.when(there != me)
        def _():
            remote(kind, lax.rem(there - me + OWNERS, OWNERS)).start()

    def arrive(kind):
        stay(kind).wait()

        @pl.loop(1, OWNERS)
        def _(step):
            remote(kind, step).wait_recv()

    def pack(kind, block):
        place = lax.broadcasted_iota(jnp.int32, (rows, slots_ref.shape[1]), 0) + block * rows
        moved = dot(one(place == slots_ref[...]), pay_ref[kind])
        moved = moved[:, :HD] + moved[:, HD:]
        for lane in range(4):
            leaving[kind, block * 4 + lane] = moved[lane * ROOM : (lane + 1) * ROOM]

    def take(kind, group, source):
        upper, lower = halves(source)
        moved = dot(seats[group], jnp.concatenate([upper, lower], axis=1))
        spread[kind, group] = (moved[:, :HD] + moved[:, HD:]).reshape(owned, seat, HD)

    def give(kind):
        @pl.loop(0, groups)
        def _(index):
            group = lax.rem(lax.div(me, GROUP) + index, groups)
            upper, lower = halves(answer[group].reshape(TALL, HD))
            moved = dot(seats[group], jnp.concatenate([upper, lower], axis=1), TN)
            moved = (moved[:, :HD] + moved[:, HD:]).reshape(GROUP, ROOM, HD)
            leaving[kind, pl.ds(group * GROUP, GROUP)] = moved
            for lane in range(GROUP):
                start(kind, group * GROUP + lane)

    def first_block():
        return lax.div(me, 4)

    pack(QK, first_block())
    pl.semaphore_wait(barrier, OWNERS)
    for lane in range(4):
        start(QK, first_block() * 4 + lane)

    @pl.loop(1, OWNERS // 4)
    def _(index):
        block = lax.rem(first_block() + index, OWNERS // 4)
        pack(QK, block)
        for lane in range(4):
            start(QK, block * 4 + lane)

    @pl.loop(0, OWNERS // 4)
    def _(block):
        pack(VALUE, block)

    @pl.loop(0, groups)
    def _(group):
        place = lax.broadcasted_iota(jnp.int32, (TALL, wide), 0)
        chosen = one(place == marks_ref[group])
        seats[group] = chosen
        early = early_ref[pl.ds(group * GROUP, GROUP), pl.ds(0, ROOM), :].reshape(wide, HD)
        upper, lower = halves(early)
        present = jnp.ones((wide, LANES), bf16)
        moved = dot(chosen, jnp.concatenate([upper, lower, present], axis=1))
        spread[2, group] = (moved[:, :HD] + moved[:, HD : 2 * HD]).reshape(owned, seat, HD)
        valid[group] = moved[:, 2 * HD :].reshape(owned, seat, LANES)

    arrive(QK)

    @pl.loop(0, OWNERS)
    def _(index):
        start(VALUE, lax.rem(me + index, OWNERS))

    @pl.loop(0, groups)
    def _(group):
        take(QK, group, landed[QK, pl.ds(group * GROUP, GROUP)].reshape(wide, HD))

    def cluster(kind, index):
        return halves(spread[kind, :, index].reshape(size, HD))

    @pl.loop(0, owned // 4)
    def _(block):
        for lane in range(4):
            index = block * 4 + lane
            present = valid[:, index].reshape(size, LANES)[:, :size] > 0.5
            qk = cluster(QK, index)
            scores = jnp.where(present, dot3(qk, qk, NT) / HD, masked_score)
            raised = jnp.exp(scores - jnp.max(scores, axis=0, keepdims=True))
            raised = raised / jnp.sum(raised, axis=0, keepdims=True)
            weights[index] = raised
            answer[:, index] = dot3(halves(raised), cluster(2, index)).reshape(groups, seat, HD)

    give(GRAD_VALUE)
    arrive(VALUE)

    @pl.loop(0, groups)
    def _(group):
        take(VALUE, group, landed[VALUE, pl.ds(group * GROUP, GROUP)].reshape(wide, HD))

    @pl.loop(0, owned // 4)
    def _(block):
        for lane in range(4):
            index = block * 4 + lane
            raised = weights[index]
            slopes = dot3(cluster(VALUE, index), cluster(2, index), NT)
            middle = jnp.sum(raised * slopes, axis=0, keepdims=True)
            slopes = raised * (slopes - middle)
            grad_qk = dot3(halves(slopes + slopes.T), cluster(QK, index)) / HD
            answer[:, index] = grad_qk.reshape(groups, seat, HD)

    give(GRAD_QK)
    arrive(GRAD_VALUE)

    back = landed[GRAD_VALUE].reshape(OWNERS * ROOM, HD)
    unpack_rows(back, tall_slots_ref, high_ref, low_ref, high_ref.shape[1] // HD)
    fetch.wait()

    def cross(step):
        there = lax.rem(y + step, NY)
        return pltpu.make_async_remote_copy(
            src_ref=away.at[there],
            dst_ref=cross_in.at[there],
            send_sem=cross_send.at[step],
            recv_sem=cross_recv.at[step],
            device_id=other,
            device_id_type=MESH,
        )

    @pl.loop(0, NY)
    def _(step):
        there = lax.rem(y + step, NY)
        away[there] = line_of_sums(tokens, 1 - rep, there, (high_ref[...], low_ref[...]))
        cross(step).start()

    @pl.loop(0, NY)
    def _(step):
        there = lax.rem(y + step, NY)
        mine = line_of_sums(tokens, rep, there, (high_ref[...], low_ref[...]))
        cross(step).wait_recv()
        own[there] = mine + cross_in[there]

    save = pltpu.make_async_copy(own, sums_ref, local_sem.at[5])
    save.start()
    arrive(GRAD_QK)
    save.wait()

    @pl.loop(0, NY)
    def _(step):
        cross(step).wait_send()

    @pl.loop(1, OWNERS)
    def _(step):
        for kind in range(4):
            remote(kind, step).wait_send()


def cluster_part(pay, slots, marks, early, tall_slots, inputs):
    groups = OWNERS // GROUP
    owned = TALL // (3 * GROUP)
    seat = 3 * GROUP
    size = groups * seat
    length = inputs.shape[0]
    width = pay.shape[1] // length * HD
    vmem, anywhere = pl.BlockSpec(memory_space=pltpu.VMEM), pl.BlockSpec(memory_space=pl.ANY)
    return pl.pallas_call(
        cluster_kernel,
        out_shape=(
            jax.ShapeDtypeStruct((OWNERS, ROOM, HD), f32),
            jax.ShapeDtypeStruct((length, width), bf16),
            jax.ShapeDtypeStruct((length, width), bf16),
            jax.ShapeDtypeStruct((NY, NZ, ROWS, width), f32),
        ),
        in_specs=[vmem, vmem, vmem, vmem, vmem, anywhere],
        out_specs=(anywhere, vmem, vmem, anywhere),
        scratch_shapes=[
            pltpu.VMEM((4, OWNERS, ROOM, HD), f32),
            pltpu.VMEM((3, OWNERS, ROOM, HD), f32),
            pltpu.VMEM((groups, TALL, GROUP * ROOM), bf16),
            pltpu.VMEM((3, groups, owned, seat, HD), f32),
            pltpu.VMEM((groups, owned, seat, LANES), f32),
            pltpu.VMEM((owned, size, size), f32),
            pltpu.VMEM((groups, owned, seat, HD), f32),
            pltpu.VMEM(inputs.shape, f32),
            pltpu.VMEM((NY, NZ, ROWS, width), f32),
            pltpu.VMEM((NY, NZ, ROWS, width), f32),
            pltpu.VMEM((NY, NZ, ROWS, width), f32),
            pltpu.SemaphoreType.DMA((6,)),
            pltpu.SemaphoreType.DMA((4, OWNERS)),
            pltpu.SemaphoreType.DMA((4, OWNERS)),
            pltpu.SemaphoreType.DMA((NY,)),
            pltpu.SemaphoreType.DMA((NY,)),
        ],
        compiler_params=pltpu.CompilerParams(
            collective_id=2, has_side_effects=True, vmem_limit_bytes=60 * 2**20
        ),
        name="exchange_and_attend",
    )(pay, slots, marks, early, tall_slots, inputs)


def grads_kernel(
    back_qk_ref, back_value_ref, slots_ref, tokens_ref, full_ref, terms_ref, sums_ref, high, low
):
    length = tokens_ref.shape[0]
    width = high.shape[1] // 2
    total = back_qk_ref.shape[0]

    @pl.when(pl.program_id(0) == 0)
    def _():
        qk_upper, qk_lower = halves(back_qk_ref[...])
        upper, lower = halves(back_value_ref[...])
        source = jnp.concatenate([qk_upper, upper, qk_lower, lower], axis=1)
        for head in range(width // HD):
            place = lax.broadcasted_iota(jnp.int32, (length, total), 1)
            chosen = one(place == slots_ref[:, head : head + 1])
            both = dot(chosen, source)
            upper, lower = halves(both[:, : 2 * HD] + both[:, 2 * HD :])
            for part in range(2):
                there = pl.ds(part * width + head * HD, HD)
                high[:, there] = upper[:, part * HD : (part + 1) * HD]
                low[:, there] = lower[:, part * HD : (part + 1) * HD]

    combined = high[...], low[...]
    terms_ref[...] = dot3(combined, halves(full_ref[...]), NT)
    sums_ref[...] = dot3(halves(tokens_ref[...]), combined, TN)


def local_grads(back_qk, back_value, slots, inputs, full):
    length, depth = inputs.shape
    both = full.shape[1]
    total = back_qk.shape[0]
    return pl.pallas_call(
        grads_kernel,
        grid=(8,),
        out_shape=(
            jax.ShapeDtypeStruct((length, depth), f32),
            jax.ShapeDtypeStruct((depth, both), f32),
        ),
        in_specs=[
            pl.BlockSpec((total, HD), lambda i: (0, 0)),
            pl.BlockSpec((total, HD), lambda i: (0, 0)),
            pl.BlockSpec(slots.shape, lambda i: (0, 0)),
            pl.BlockSpec((length, depth // 8), lambda i: (0, i)),
            pl.BlockSpec((depth // 8, both), lambda i: (i, 0)),
        ],
        out_specs=(
            pl.BlockSpec((length, depth // 8), lambda i: (0, i)),
            pl.BlockSpec((depth // 8, both), lambda i: (i, 0)),
        ),
        scratch_shapes=[pltpu.VMEM((length, both), bf16)] * 2,
        compiler_params=pltpu.CompilerParams(vmem_limit_bytes=BIG),
        name="unpack_and_grads",
    )(back_qk, back_value, slots, inputs, full)


FINISH_COPIES = 2 + 14 + 14 + 4 + 6


def finish_kernel(
    back_qk_ref, high_ref, low_ref, sums_ref, slots_ref, tokens_ref, full_ref,
    tokens_out, qk_out, value_out,
    tokens, full, high, low, terms, away, own, cross_in,
    column_in, passing, ring_a, ring_b, line_in, plane_in,
    load_sem, send_sem, recv_sem, cross_send, cross_recv,
    line_send, line_recv,
):
    rep, y, z = position()
    x = lax.axis_index("tp")
    length = tokens.shape[0]
    both = full.shape[1]
    width = both // 2

    def along_y(step):
        return {"ctx": lax.rem(y + step, NY) * NZ + z}

    def along_z(step):
        return {"ctx": y * NZ + lax.rem(z + step, NZ)}

    def along_x(step):
        return {"tp": lax.rem(x + step, 4)}

    loads = [
        pltpu.make_async_copy(tokens_ref, tokens, load_sem.at[0]),
        pltpu.make_async_copy(full_ref, full, load_sem.at[1]),
        pltpu.make_async_copy(sums_ref, own.at[1], load_sem.at[2]),
    ]
    for load in reversed(loads):
        load.start()
    right, left, other = along_z(1), along_z(NZ - 1), {"rep": 1 - rep}
    barrier = pltpu.get_barrier_semaphore()
    partners = [along_y(1), along_y(2), along_y(3), right, left, other]
    partners += [along_x(1), along_x(3)]
    for partner in partners:
        pl.semaphore_signal(barrier, inc=1, device_id=partner, device_id_type=MESH)

    def cross(step):
        there = lax.rem(y + step, NY)
        return pltpu.make_async_remote_copy(
            src_ref=away.at[there],
            dst_ref=cross_in.at[there],
            send_sem=cross_send.at[step],
            recv_sem=cross_recv.at[step],
            device_id=other,
            device_id_type=MESH,
        )

    def line_sum(half, there):
        return line_of_sums(tokens, half, there, (high[:, :width], low[:, :width]))

    def away_lines():
        @pl.loop(0, NY)
        def _(step):
            there = lax.rem(y + step, NY)
            away[there] = line_sum(1 - rep, there)
            cross(step).start()

    def own_lines():
        @pl.loop(0, NY)
        def _(step):
            there = lax.rem(y + step, NY)
            mine = line_sum(rep, there)
            cross(step).wait_recv()
            own[0, there] = mine + cross_in[there]

    def depth(turn):
        return lax.rem(z + turn, NZ)

    def piece(step, turn, part):
        return pltpu.make_async_remote_copy(
            src_ref=own.at[part, lax.rem(y + step, NY), depth(turn), pl.ds(HALF, HALF), :],
            dst_ref=line_in.at[part, step - 1, depth(turn)],
            send_sem=line_send.at[part, step - 1, turn],
            recv_sem=line_recv.at[part, step - 1, turn],
            device_id=along_y(step),
            device_id_type=MESH,
        )

    def send_pieces(part):
        for turn in (4, 5, 3, 6, 2, 7, 1, 0):
            for step in (1, 3, 2):
                piece(step, turn, part).start()

    copies = Copies(send_sem, recv_sem)

    def plane(turn, part):
        return own.at[part, :, depth(turn), pl.ds(0, HALF), :]

    flow_a, flow_b = [None, None], [None, None]

    def turn_a(turn, part):
        ring = ring_a.at[part]
        if turn == 0:
            flow_a[part] = (
                copies.start(plane(4, part), ring.at[0], right),
                copies.start(plane(5, part), ring.at[4], left),
            )
            return
        rightward, leftward = flow_a[part]
        rightward.wait_recv()
        ring_a[part, turn - 1] += plane(4 - turn, part)[...]
        rightward = copies.start(ring.at[turn - 1], ring.at[turn], right)
        if turn < 3:
            leftward.wait_recv()
            ring_a[part, 3 + turn] += plane(5 + turn, part)[...]
            leftward = copies.start(ring.at[3 + turn], ring.at[4 + turn], left)
        flow_a[part] = rightward, leftward

    def along_lines(turn, part):
        for step in (1, 2, 3):
            piece(step, turn, part).wait_recv()
        here = depth(turn)
        return own[part, y, here, pl.ds(HALF, HALF), :] + (
            line_in[part, 0, here] + line_in[part, 1, here] + line_in[part, 2, here]
        )

    def turn_b(turn, part):
        ring = ring_b.at[part]
        if turn == 0:
            first = own.at[part, y, depth(4), pl.ds(HALF, HALF), :]
            second = own.at[part, y, depth(5), pl.ds(HALF, HALF), :]
            first[...] = along_lines(4, part)
            rightward = copies.start(first, ring.at[0], right)
            second[...] = along_lines(5, part)
            flow_b[part] = rightward, copies.start(second, ring.at[4], left)
            return
        rightward, leftward = flow_b[part]
        mine = along_lines(4 - turn, part)
        rightward.wait_recv()
        ring_b[part, turn - 1] += mine
        rightward = copies.start(ring.at[turn - 1], ring.at[turn], right)
        if turn < 3:
            mine = along_lines(5 + turn, part)
            leftward.wait_recv()
            ring_b[part, 3 + turn] += mine
            leftward = copies.start(ring.at[3 + turn], ring.at[4 + turn], left)
        flow_b[part] = rightward, leftward

    planes = [[], []]

    def end_a(part):
        for copy in flow_a[part]:
            copy.wait_recv()
        own[part, :, z, pl.ds(0, HALF), :] = plane(0, part)[...] + (
            ring_a[part, 3] + ring_a[part, 6]
        )
        for step in (1, 3, 2):
            planes[part].append(copies.start(
                own.at[part, lax.rem(y + step, NY), z, pl.ds(0, HALF), :],
                plane_in.at[part, step - 1],
                along_y(step),
            ))

    def end_b(part, out):
        mine = along_lines(0, part)
        for copy in flow_b[part]:
            copy.wait_recv()
        out[pl.ds(HALF, HALF), :] = mine + ring_b[part, 3] + ring_b[part, 6]

    middle = length // 2
    upper_rows, lower_rows = pl.ds(0, middle), pl.ds(middle, middle)

    def columns(step):
        start = pl.multiple_of(lax.rem(x + step, 4) * width, width)
        return dot3((high[...], low[...]), halves(full[pl.ds(start, width), :]), NT)

    pl.semaphore_wait(barrier, len(partners))
    loads[2].wait()
    turn_a(0, 1)
    send_pieces(1)
    high[:, pl.ds(width, width)] = high_ref[...]
    low[:, pl.ds(width, width)] = low_ref[...]
    unpack_rows(back_qk_ref[...], slots_ref, high, low, width // HD)
    loads[0].wait()
    away_lines()
    turn_a(1, 1)
    own_lines()
    turn_a(0, 0)
    send_pieces(0)
    turn_b(0, 1)
    turn_a(2, 1)
    loads[1].wait()
    terms[1] = columns(2)
    by_right = copies.start(terms.at[1, upper_rows], passing.at[0], along_x(1))
    by_left = copies.start(terms.at[1, lower_rows], passing.at[1], along_x(3))
    turn_b(1, 1)
    turn_a(1, 0)
    turn_a(3, 1)
    terms[0] = columns(1)
    sideways = [copies.start(terms.at[0, lower_rows], column_in.at[0, lower_rows], along_x(1))]
    turn_b(0, 0)
    turn_b(2, 1)
    turn_a(2, 0)
    terms[2] = columns(3)
    sideways.append(
        copies.start(terms.at[2, upper_rows], column_in.at[1, upper_rows], along_x(3))
    )
    turn_b(1, 0)
    end_a(1)
    turn_b(3, 1)
    turn_a(3, 0)
    by_right.wait_recv()
    terms[0, upper_rows, :] += passing[0]
    sideways.append(
        copies.start(terms.at[0, upper_rows], column_in.at[0, upper_rows], along_x(1))
    )
    by_left.wait_recv()
    terms[2, lower_rows, :] += passing[1]
    sideways.append(
        copies.start(terms.at[2, lower_rows], column_in.at[1, lower_rows], along_x(3))
    )
    turn_b(2, 0)
    end_b(1, value_out)
    tokens_out[...] = columns(0)
    turn_b(3, 0)
    end_a(0)
    end_b(0, qk_out)
    for copy in sideways:
        copy.wait_recv()

    @pl.loop(0, length // 8)
    def _(block):
        here = pl.ds(pl.multiple_of(block * 8, 8), 8)
        tokens_out[here, :] += column_in[0, here, :] + column_in[1, here, :]

    for part, out in ((1, value_out), (0, qk_out)):
        for copy in planes[part]:
            copy.wait_recv()
        out[pl.ds(0, HALF), :] = own[part, y, z, pl.ds(0, HALF), :] + (
            plane_in[part, 0] + plane_in[part, 1] + plane_in[part, 2]
        )

    @pl.loop(0, NY)
    def _(step):
        cross(step).wait_send()

    @pl.loop(1, NY)
    def _(step):
        for part in range(2):
            for turn in range(NZ):
                piece(step, turn, part).wait_send()

    copies.finish()
    assert len(copies.all) == FINISH_COPIES


def finish(back_qk, high, low, sums, slots, inputs, full):
    length, depth = inputs.shape
    both = full.shape[1]
    width = both // 2
    vmem, anywhere = pl.BlockSpec(memory_space=pltpu.VMEM), pl.BlockSpec(memory_space=pl.ANY)
    return pl.pallas_call(
        finish_kernel,
        out_shape=(
            jax.ShapeDtypeStruct((length, width), f32),
            jax.ShapeDtypeStruct((ROWS, width), f32),
            jax.ShapeDtypeStruct((ROWS, width), f32),
        ),
        in_specs=[vmem, vmem, vmem, anywhere, vmem, anywhere, anywhere],
        out_specs=(vmem,) * 3,
        scratch_shapes=[
            pltpu.VMEM((length, depth), f32),
            pltpu.VMEM((depth, both), f32),
            pltpu.VMEM((length, both), bf16),
            pltpu.VMEM((length, both), bf16),
            pltpu.VMEM((3, length, width), f32),
            pltpu.VMEM((NY, NZ, ROWS, width), f32),
            pltpu.VMEM((2, NY, NZ, ROWS, width), f32),
            pltpu.VMEM((NY, NZ, ROWS, width), f32),
            pltpu.VMEM((2, length, width), f32),
            pltpu.VMEM((2, length // 2, width), f32),
            pltpu.VMEM((2, 7, NY, HALF, width), f32),
            pltpu.VMEM((2, 7, HALF, width), f32),
            pltpu.VMEM((2, 3, NZ, HALF, width), f32),
            pltpu.VMEM((2, 3, HALF, width), f32),
            pltpu.SemaphoreType.DMA((3,)),
            pltpu.SemaphoreType.DMA((FINISH_COPIES,)),
            pltpu.SemaphoreType.DMA((FINISH_COPIES,)),
            pltpu.SemaphoreType.DMA((NY,)),
            pltpu.SemaphoreType.DMA((NY,)),
            pltpu.SemaphoreType.DMA((2, 3, NZ)),
            pltpu.SemaphoreType.DMA((2, 3, NZ)),
        ],
        compiler_params=pltpu.CompilerParams(
            collective_id=3, has_side_effects=True, vmem_limit_bytes=60 * 2**20
        ),
        name="grads_and_scatter",
    )(back_qk, high, low, sums, slots, inputs, full)


def exchange(array):
    return lax.all_to_all(array, "ctx", split_axis=0, concat_axis=0, tiled=True)


def seat_numbers(marks, room):
    marks = marks.astype(jnp.int32) - 1
    source = lax.broadcasted_iota(jnp.int32, marks.shape, 0) % GROUP
    seats = (marks // 3) * (3 * GROUP) + source * 3 + marks % 3
    return jnp.where(marks < 0, -1, seats).reshape(OWNERS // GROUP, 1, GROUP * room)


def snug_part(inputs, full, pay, early, slots, tall_slots):
    marks = early[:, ROOM : ROOM + 2, :ROOM]
    held, place = marks[:, 0], marks[:, 1]
    seats = jnp.where(held > 0.5, (held - 1) * (3 * GROUP) + place, -1.0).astype(jnp.int32)
    seats = seats.reshape(OWNERS // GROUP, 1, GROUP * ROOM)
    back_qk, high, low, sums = cluster_part(pay, slots, seats, early, tall_slots, inputs)
    back_qk = back_qk.reshape(OWNERS * ROOM, HD)
    return finish(back_qk, high, low, sums, tall_slots, inputs, full)


def roomy_part(inputs, full, upstream, cluster):
    heads, length = cluster.shape
    order = jnp.arange(length, dtype=jnp.int32)
    earlier = order[:, None] < order[None, :]
    alike = cluster[:, :, None] == cluster[:, None, :]
    within = jnp.sum((alike & earlier).astype(jnp.int32), axis=1)
    head = jnp.arange(heads, dtype=jnp.int32)[:, None]
    ids = (head * CL_DEV + cluster % CL_DEV) * 3 + within
    slots = cluster // CL_DEV * SLOTS + ids
    marks = jnp.zeros((OWNERS * SLOTS,), f32).at[slots.reshape(-1)].set(
        (ids + 1).astype(f32).reshape(-1)
    )
    rows = upstream.reshape(length, heads, HD).transpose(1, 0, 2).reshape(-1, HD)
    early = jnp.zeros((OWNERS * SLOTS, HD), f32).at[slots.reshape(-1)].set(rows)
    early = exchange(early.reshape(OWNERS, SLOTS, HD))
    marks = exchange(marks.reshape(OWNERS, SLOTS))
    rows = pack_rows(inputs, full, slots.reshape(1, -1), SLOTS)
    rows = exchange(rows.reshape(OWNERS, SLOTS, 2 * HD)).reshape(OWNERS * SLOTS, 2 * HD)
    replies = attend(rows, early, seat_numbers(marks, SLOTS), SLOTS)
    returned = exchange(replies.reshape(OWNERS, SLOTS, 2 * HD)).reshape(OWNERS * SLOTS, 2 * HD)
    return scatter_sums(
        *local_grads(returned[:, :HD], returned[:, HD:], slots.T, inputs, full)
    )


def per_device(tokens, qk_weight, value_weight, grad_out, assign):
    inputs = tokens[0]
    heads_here = qk_weight.shape[1] // HD
    width = heads_here * HD
    cluster = assign[:, 0, :, 0]
    full, early, slots, tall_slots, pay = gather_and_project(
        qk_weight, value_weight, jnp.pad(cluster, ((0, 8 - heads_here), (0, 0))), grad_out[0],
        inputs,
    )
    full = full.reshape(-1, 2 * width)
    fullest = jnp.max(early[:, ROOM, PITCH])

    def snug(inputs, full, upstream, cluster, *routed):
        return snug_part(inputs, full, *routed)

    def roomy(inputs, full, upstream, cluster, *routed):
        return roomy_part(inputs, full, upstream, cluster)

    grad_tokens, grad_qk_weight, grad_value_weight = lax.cond(
        fullest <= ROOM, snug, roomy,
        inputs, full, grad_out[0], cluster, pay, early, slots, tall_slots,
    )
    return (grad_tokens[None], grad_qk_weight, grad_value_weight)


def solution(mesh):
    in_specs = (
        P("rep", "ctx", None),
        P(("rep", "ctx"), "tp"),
        P(("rep", "ctx"), "tp"),
        P("rep", "ctx", "tp"),
        P("tp", "rep", "ctx", None),
    )
    out_specs = (P("rep", "ctx", "tp"), P(("rep", "ctx"), "tp"), P(("rep", "ctx"), "tp"))
    return jax.shard_map(
        per_device, mesh=mesh, in_specs=in_specs, out_specs=out_specs, check_vma=False
    )
```

```python
import jax
import jax.numpy as jnp
from jax import lax
from jax.experimental import pallas as pl
from jax.experimental.pallas import tpu as pltpu
from jax.sharding import PartitionSpec as P

HD = 128
CL_DEV = 8
NY = 4
NZ = 8
ROWS = 32
HALF = 16
MESH = pl.DeviceIdType.MESH

masked_score = -1e30
ROOM = 56
LANES = 128
GROUP = 8
SLOTS = 96
TALL = 768
f32, bf16 = jnp.float32, jnp.bfloat16
NN = (((1,), (0,)), ((), ()))
NT = (((1,), (1,)), ((), ()))
TN = (((0,), (0,)), ((), ()))
BIG = 48 * 2**20


def dot(left, right, dims=NN):
    return lax.dot_general(left, right, dims, preferred_element_type=f32)


def halves(matrix):
    upper = matrix.astype(bf16)
    return upper, (matrix - upper.astype(f32)).astype(bf16)


def dot3(left, right, dims=NN):
    a, b = left
    c, d = right
    first = jnp.concatenate([a, b, a], axis=dims[0][0][0])
    second = jnp.concatenate([c, c, d], axis=dims[0][1][0])
    return dot(first, second, dims)


def position():
    ctx = lax.axis_index("ctx")
    return lax.axis_index("rep"), lax.div(ctx, NZ), lax.rem(ctx, NZ)


def greet(partners):
    barrier = pltpu.get_barrier_semaphore()
    for partner in partners:
        pl.semaphore_signal(barrier, inc=1, device_id=partner, device_id_type=MESH)
    pl.semaphore_wait(barrier, len(partners))


class Copies:
    def __init__(self, send_sem, recv_sem):
        self.send_sem, self.recv_sem = send_sem, recv_sem
        self.all = []

    def start(self, source, target, device):
        index = len(self.all)
        copy = pltpu.make_async_remote_copy(
            src_ref=source,
            dst_ref=target,
            send_sem=self.send_sem.at[index],
            recv_sem=self.recv_sem.at[index],
            device_id=device,
            device_id_type=MESH,
        )
        copy.start()
        self.all.append(copy)
        return copy

    def finish(self):
        for copy in self.all:
            copy.wait_send()


GATHER_COPIES = 6 + 7 + 14 + 21 + 16 + 4
ROUTE_COPIES = 3 + 7 + 3 + 1
CLUSTERS = 256
OWNERS = 32
PITCH = 64


def count_rows(cluster_ref, heads):
    length = cluster_ref.shape[1]
    line = lax.broadcasted_iota(jnp.int32, (8, length), 0)
    counts = jnp.zeros((8, CLUSTERS), f32)
    for head in range(heads):
        counts += dot(one(line == head), members(cluster_ref, head), NT)
    return counts


def one(condition):
    return jnp.where(condition, 1.0, 0.0).astype(bf16)


def members(cluster_ref, head):
    length = cluster_ref.shape[1]
    label = lax.broadcasted_iota(jnp.int32, (CLUSTERS, length), 0)
    return one(label == cluster_ref[head : head + 1, :])


def deal_order(counts):
    lane = lax.broadcasted_iota(jnp.int32, counts.shape, 1)
    return counts * CLUSTERS + (CLUSTERS - 1 - lane).astype(f32)


def route_head(cluster_ref, head, keys, tall_keys, earlier, base):
    larger = jnp.where(tall_keys[:, head : head + 1] > keys[head : head + 1, :], 1.0, 0.0)
    place = jnp.sum(larger, axis=0, keepdims=True).astype(jnp.int32)
    turn = place // OWNERS
    seat = place % OWNERS
    seat = jnp.where(turn % 2 == 0, seat, OWNERS - 1 - seat)
    seat = (seat + 8 * head) % OWNERS
    line = lax.broadcasted_iota(jnp.int32, (8, CLUSTERS), 0)
    table = jnp.where(line == 0, seat, jnp.where(line == 1, turn, 0)).astype(f32).astype(bf16)
    chosen = members(cluster_ref, head)
    looked = dot(table, chosen).astype(jnp.int32)
    owner, turn = looked[0:1, :], looked[1:2, :]
    within = jnp.sum(chosen.astype(f32) * dot(chosen, earlier), axis=0, keepdims=True)
    label = lax.broadcasted_iota(jnp.int32, (OWNERS, owner.shape[1]), 0)
    owned = one(label == owner)
    many = owned.astype(f32)
    rank = jnp.sum(many * (dot(owned, earlier) + base), axis=0, keepdims=True)
    base = base + jnp.sum(many, axis=1, keepdims=True)
    return owner, rank.astype(jnp.int32), head * CL_DEV + turn, within, base


def gather_kernel(
    qk_ref, value_ref, cluster_ref, grad_ref, tokens_ref,
    full_ref, early_ref, slots_ref, tall_slots_ref, pay_ref,
    out_ref, tokens, acc, counts_y, counts_z, most, ids_row, slots_row, pay, early_out,
    local_sem, send_sem, recv_sem, route_send, route_recv, early_send, early_recv,
):
    rep, y, z = position()
    me = lax.axis_index("ctx")
    x = lax.axis_index("tp")
    width = qk_ref.shape[1]
    heads = width // HD
    length = cluster_ref.shape[1]

    def along_y(step):
        return {"ctx": lax.rem(y + step, NY) * NZ + z}

    def along_z(step):
        return {"ctx": y * NZ + lax.rem(z + step, NZ)}

    def along_x(step):
        return {"tp": lax.rem(x + step, 4)}

    def around(step):
        return {"ctx": lax.rem(me + step, OWNERS)}

    def plane(step, part):
        there = pl.ds(part * width, width)
        return out_ref.at[rep, :, lax.rem(z + step, NZ), pl.ds(0, HALF), there]

    def piece(step):
        return out_ref.at[rep, y, lax.rem(z + step, NZ), pl.ds(HALF, HALF), :]

    def line(step):
        return out_ref.at[rep, lax.rem(y + step, NY), :, pl.ds(HALF, HALF), :]

    right, left, other = along_z(1), along_z(NZ - 1), {"rep": 1 - rep}
    mine = out_ref.at[rep, y, z]
    fetch = pltpu.make_async_copy(tokens_ref, tokens, local_sem.at[2])
    fetch.start()
    first = pltpu.make_async_copy(qk_ref, mine.at[:, pl.ds(0, width)], local_sem.at[0])
    second = pltpu.make_async_copy(value_ref, mine.at[:, pl.ds(width, width)], local_sem.at[1])
    first.start()
    second.start()
    barrier = pltpu.get_barrier_semaphore()

    @pl.loop(1, OWNERS)
    def _(step):
        pl.semaphore_signal(barrier, inc=1, device_id=around(step), device_id_type=MESH)

    for partner in (other, along_x(1), along_x(2), along_x(3)):
        pl.semaphore_signal(barrier, inc=1, device_id=partner, device_id_type=MESH)
    counts_y[0] = count_rows(cluster_ref, heads)
    pl.semaphore_wait(barrier, OWNERS - 1 + 4)

    routes = Copies(route_send, route_recv)
    counted = [
        routes.start(counts_y.at[0], counts_y.at[step], along_y(step)) for step in (1, 2, 3)
    ]
    first.wait()
    second.wait()
    copies = Copies(send_sem, recv_sem)
    top, bottom = mine.at[pl.ds(0, HALF), :], mine.at[pl.ds(HALF, HALF), :]
    shared = [copies.start(top, top, along_y(step)) for step in (1, 3, 2)]
    pieces = [(copies.start(piece(0), piece(0), right), copies.start(piece(0), piece(0), left))]

    below = [copies.start(bottom, bottom, along_y(step)) for step in (1, 3, 2)]

    for head in range(heads):
        upper, lower = halves(grad_ref[:, head * HD : (head + 1) * HD])
        pay[pl.ds(head * length, length), :HD] = upper
        pay[pl.ds(head * length, length), HD:] = lower

    for copy in counted:
        copy.wait_recv()
    counts_z[0] = counts_y[0] + counts_y[1] + counts_y[2] + counts_y[3]
    counted = [
        routes.start(counts_z.at[0], counts_z.at[step], along_z(step)) for step in range(1, NZ)
    ]
    for copy in shared:
        copy.wait_recv()
    planes = []
    for part in range(2):
        here = plane(0, part)
        planes.append([(copies.start(here, here, right), copies.start(here, here, left))])
    across = [copies.start(plane(0, part), plane(0, part), other) for part in range(2)]
    passed = {1: [], 2: [], 3: []}

    def pass_on(here):
        for step in (1, 3, 2):
            passed[step].append(copies.start(here, here, along_y(step)))

    def turn_pieces(step):
        rightward, leftward = pieces[step]
        after, before = piece(NZ - 1 - step), piece(1 + step)
        rightward.wait_recv()
        if leftward is not None:
            leftward.wait_recv()
        if step < 3:
            pieces.append((
                copies.start(after, after, right),
                copies.start(before, before, left) if step < 2 else None,
            ))
        pass_on(after)
        if leftward is not None:
            pass_on(before)

    def turn_planes(step):
        for part in range(2):
            turn_plane(step, part)

    def turn_plane(step, part):
        rightward, leftward = planes[part][step]
        after, before = plane(NZ - 1 - step, part), plane(1 + step, part)
        rightward.wait_recv()
        if step < 3:
            going = copies.start(after, after, right)
        if leftward is not None:
            leftward.wait_recv()
            coming = copies.start(before, before, left) if step < 2 else None
        if step < 3:
            planes[part].append((going, coming if step < 2 else None))
        across.append(copies.start(after, after, other))
        if leftward is not None:
            across.append(copies.start(before, before, other))

    turn_pieces(0)
    for copy in counted:
        copy.wait_recv()
    total = counts_z[0]
    for step in range(1, NZ):
        total += counts_z[step]
    keys = deal_order(total)
    tall_keys = jnp.concatenate([keys] + [jnp.zeros_like(keys)] * 15, axis=0).T
    earlier = one(
        lax.broadcasted_iota(jnp.int32, (length, length), 0)
        < lax.broadcasted_iota(jnp.int32, (length, length), 1)
    )
    base = jnp.zeros((OWNERS, 1), f32)
    highest = jnp.zeros((1, 1), f32)
    row = lax.broadcasted_iota(jnp.int32, (8, length), 0)
    slots_list = []
    for head in range(heads):
        owner, rank, held, within, base = route_head(
            cluster_ref, head, keys, tall_keys, earlier, base
        )
        highest = jnp.maximum(highest, jnp.max(rank.astype(f32), axis=1, keepdims=True) + 1)
        here = pl.ds(head * length, length)
        slots_ref[:, here] = jnp.where(rank < ROOM, owner * ROOM + rank, -1)
        slots_row[:, here] = jnp.where(rank < ROOM, owner * PITCH + rank, -1)
        within = within + (3 * lax.rem(me, GROUP)).astype(f32)
        marked = jnp.where(row == 0, (held + 1).astype(f32), jnp.where(row == 1, within, 0.0))
        ids_row[:, here] = marked.astype(bf16)
        slots_list.append(jnp.where(rank < ROOM, owner * ROOM + rank, -1))
    most[0] = jnp.broadcast_to(highest, (8, LANES))
    tall = jnp.concatenate(
        slots_list + [jnp.zeros((LANES - heads, length), jnp.int32)], axis=0
    )
    tall_slots_ref[...] = tall.astype(f32).T.astype(jnp.int32)
    fullest = [routes.start(most.at[0], most.at[step], along_x(step)) for step in (1, 2, 3)]
    turn_pieces(1)
    turn_planes(0)

    def pack_early(block):
        rows = 4 * PITCH
        place = lax.broadcasted_iota(jnp.int32, (rows, heads * length), 0) + block * rows
        chosen = one(place == slots_row[...])
        both = dot(chosen, pay[...])
        both = both[:, :HD] + both[:, HD:]
        marks = dot(ids_row[...], chosen, NT)
        for lane in range(4):
            early_out[block * 4 + lane] = both[lane * PITCH : (lane + 1) * PITCH]
            early_out[block * 4 + lane, pl.ds(ROOM, 8), pl.ds(0, PITCH)] = marks[
                :, lane * PITCH : (lane + 1) * PITCH
            ]

    @pl.loop(0, OWNERS // 8)
    def _(block):
        pack_early(block)

    for copy in fullest:
        copy.wait_recv()
    most[4] = jnp.maximum(jnp.maximum(most[0], most[1]), jnp.maximum(most[2], most[3]))
    fullest = routes.start(most.at[4], most.at[5], other)
    turn_pieces(2)

    @pl.loop(OWNERS // 8, OWNERS // 4)
    def _(block):
        pack_early(block)

    turn_pieces(3)
    turn_planes(1)
    across.append(copies.start(line(0), line(0), other))
    fullest.wait_recv()
    overall = jnp.maximum(most[4], most[5])[:, :PITCH]

    @pl.loop(0, OWNERS)
    def _(block):
        early_out[block, pl.ds(ROOM, 8), pl.ds(PITCH, PITCH)] = overall

    def early(step):
        there = lax.rem(me + step, OWNERS)
        return pltpu.make_async_remote_copy(
            src_ref=early_out.at[there],
            dst_ref=early_ref.at[me],
            send_sem=early_send.at[step],
            recv_sem=early_recv.at[step],
            device_id={"ctx": there},
            device_id_type=MESH,
        )

    @pl.loop(1, OWNERS // 4)
    def _(step):
        early(step).start()

    stay = pltpu.make_async_copy(early_out.at[me], early_ref.at[me], local_sem.at[0])
    stay.start()
    turn_planes(2)
    turn_planes(3)

    @pl.loop(OWNERS // 4, OWNERS)
    def _(step):
        early(step).start()

    for copy in below:
        copy.wait_recv()
    for step in (1, 3, 2):
        for copy in passed[step]:
            copy.wait_recv()
        across.append(copies.start(line(NY - step), line(NY - step), other))
    fetch.wait()

    def project(half, there):
        start = pl.multiple_of((half * NY + there) * (NZ * ROWS), NZ * ROWS)
        some = halves(tokens[:, pl.ds(start, NZ * ROWS)])
        return dot3(some, halves(out_ref[half, there].reshape(NZ * ROWS, 2 * width)))

    acc[...] = project(rep, 0)

    @pl.loop(1, NY)
    def _(there):
        acc[...] += project(rep, there)

    for copy in across:
        copy.wait_recv()
    save = pltpu.make_async_copy(out_ref, full_ref, local_sem.at[1])
    save.start()

    @pl.loop(0, NY)
    def _(there):
        acc[...] += project(1 - rep, there)

    for part in range(2):
        for head in range(heads):
            here = pl.ds(head * length, length)
            column = part * width + head * HD
            upper, lower = halves(acc[:, column : column + HD])
            pay_ref[part, here, :HD] = upper
            pay_ref[part, here, HD:] = lower
    copies.finish()
    routes.finish()
    stay.wait()
    save.wait()

    @pl.loop(1, OWNERS)
    def _(step):
        early(step).wait()

    assert len(copies.all) == GATHER_COPIES and len(routes.all) == ROUTE_COPIES


def gather_and_project(qk_weight, value_weight, clusters, upstream, inputs):
    width = qk_weight.shape[1]
    length = clusters.shape[1]
    rows = width // HD * length
    vmem, anywhere = pl.BlockSpec(memory_space=pltpu.VMEM), pl.BlockSpec(memory_space=pl.ANY)
    return pl.pallas_call(
        gather_kernel,
        out_shape=(
            jax.ShapeDtypeStruct((2, NY, NZ, ROWS, 2 * width), f32),
            jax.ShapeDtypeStruct((OWNERS, PITCH, HD), f32),
            jax.ShapeDtypeStruct((1, rows), jnp.int32),
            jax.ShapeDtypeStruct((length, LANES), jnp.int32),
            jax.ShapeDtypeStruct((2, rows, 2 * HD), bf16),
        ),
        in_specs=[anywhere, anywhere, vmem, vmem, anywhere],
        out_specs=(anywhere, anywhere, vmem, vmem, vmem),
        scratch_shapes=[
            pltpu.VMEM((2, NY, NZ, ROWS, 2 * width), f32),
            pltpu.VMEM(inputs.shape, f32),
            pltpu.VMEM((length, 2 * width), f32),
            pltpu.VMEM((NY, 8, CLUSTERS), f32),
            pltpu.VMEM((NZ, 8, CLUSTERS), f32),
            pltpu.VMEM((6, 8, LANES), f32),
            pltpu.VMEM((8, rows), bf16),
            pltpu.VMEM((1, rows), jnp.int32),
            pltpu.VMEM((rows, 2 * HD), bf16),
            pltpu.VMEM((OWNERS, PITCH, HD), f32),
            pltpu.SemaphoreType.DMA((3,)),
            pltpu.SemaphoreType.DMA((GATHER_COPIES,)),
            pltpu.SemaphoreType.DMA((GATHER_COPIES,)),
            pltpu.SemaphoreType.DMA((ROUTE_COPIES,)),
            pltpu.SemaphoreType.DMA((ROUTE_COPIES,)),
            pltpu.SemaphoreType.DMA((OWNERS,)),
            pltpu.SemaphoreType.DMA((OWNERS,)),
        ],
        compiler_params=pltpu.CompilerParams(
            collective_id=0, has_side_effects=True, vmem_limit_bytes=60 * 2**20
        ),
        name="gather_and_project",
    )(qk_weight, value_weight, clusters, upstream, inputs)


SCATTER_COPIES = 3 + 12 + 7 + 3 + 7 + 3


def scatter_kernel(
    terms_ref, sums_ref, tokens_out, qk_out, value_out,
    column_in, cross_in, ring_a, ring_b, line_in, plane_in,
    local_sem, send_sem, recv_sem,
):
    rep, y, z = position()
    x = lax.axis_index("tp")
    width = qk_out.shape[1]

    def along_y(step):
        return {"ctx": lax.rem(y + step, NY) * NZ + z}

    def along_z(step):
        return {"ctx": y * NZ + lax.rem(z + step, NZ)}

    def along_x(step):
        return {"tp": lax.rem(x + step, 4)}

    def columns(step):
        start = pl.multiple_of(lax.rem(x + step, 4) * width, width)
        return terms_ref.at[:, pl.ds(start, width)]

    def plane(step):
        return cross_in.at[:, lax.rem(z + step, NZ), pl.ds(0, HALF), :]

    def line(step):
        return cross_in.at[lax.rem(y + step, NY), :, pl.ds(HALF, HALF), :]

    def piece(step):
        return cross_in.at[y, lax.rem(z + step, NZ), pl.ds(HALF, HALF), :]

    right, left, other = along_z(1), along_z(NZ - 1), {"rep": 1 - rep}
    greet(
        [along_y(1), along_y(2), along_y(3), right, left, other]
        + [along_x(1), along_x(2), along_x(3)]
    )
    copies = Copies(send_sem, recv_sem)
    sideways = [
        copies.start(columns(step), column_in.at[step - 1], along_x(step)) for step in (1, 3, 2)
    ]
    own_columns = pltpu.make_async_copy(columns(0), tokens_out, local_sem)
    own_columns.start()

    cross = {}
    for kind, step in (
        ("a", 4), ("a", 5), ("b", 1), ("b", 3), ("b", 2), ("a", 3),
        ("a", 6), ("a", 2), ("a", 7), ("b", 0), ("a", 1), ("a", 0),
    ):
        if kind == "a":
            there = lax.rem(z + step, NZ)
            source = sums_ref.at[1 - rep, :, there, pl.ds(0, HALF), :]
            cross[kind, step] = copies.start(source, plane(step), other)
        else:
            there = lax.rem(y + step, NY)
            source = sums_ref.at[1 - rep, there, :, pl.ds(HALF, HALF), :]
            cross[kind, step] = copies.start(source, line(step), other)

    def add_plane(step):
        cross["a", step].wait_recv()
        there = lax.rem(z + step, NZ)
        cross_in[:, there, pl.ds(0, HALF), :] += sums_ref[rep, :, there, pl.ds(0, HALF), :]

    def add_line(step):
        cross["b", step].wait_recv()
        there = lax.rem(y + step, NY)
        cross_in[there, :, pl.ds(HALF, HALF), :] += sums_ref[
            rep, there, :, pl.ds(HALF, HALF), :
        ]

    add_plane(4)
    right_a = copies.start(plane(4), ring_a.at[0], right)
    add_plane(5)
    left_a = copies.start(plane(5), ring_a.at[4], left)
    lines = []
    for step in (1, 3, 2):
        add_line(step)
        lines.append(copies.start(line(step), line_in.at[step - 1], along_y(step)))

    def pass_a(turn):
        nonlocal right_a, left_a
        add_plane(4 - turn)
        right_a.wait_recv()
        ring_a[turn - 1] += cross_in[:, lax.rem(z + 4 - turn, NZ), pl.ds(0, HALF), :]
        right_a = copies.start(ring_a.at[turn - 1], ring_a.at[turn], right)
        if turn < 3:
            add_plane(5 + turn)
            left_a.wait_recv()
            ring_a[3 + turn] += cross_in[:, lax.rem(z + 5 + turn, NZ), pl.ds(0, HALF), :]
            left_a = copies.start(ring_a.at[3 + turn], ring_a.at[4 + turn], left)

    pass_a(1)
    add_line(0)
    pass_a(2)
    for copy in lines:
        copy.wait_recv()
    cross_in[y, :, pl.ds(HALF, HALF), :] += line_in[0] + line_in[1] + line_in[2]
    right_b = copies.start(piece(4), ring_b.at[0], right)
    left_b = copies.start(piece(5), ring_b.at[4], left)
    pass_a(3)

    def pass_b(turn):
        nonlocal right_b, left_b
        right_b.wait_recv()
        ring_b[turn - 1] += cross_in[y, lax.rem(z + 4 - turn, NZ), pl.ds(HALF, HALF), :]
        right_b = copies.start(ring_b.at[turn - 1], ring_b.at[turn], right)
        if turn < 3:
            left_b.wait_recv()
            ring_b[3 + turn] += cross_in[y, lax.rem(z + 5 + turn, NZ), pl.ds(HALF, HALF), :]
            left_b = copies.start(ring_b.at[3 + turn], ring_b.at[4 + turn], left)

    pass_b(1)
    pass_b(2)
    add_plane(0)
    right_a.wait_recv()
    left_a.wait_recv()
    cross_in[:, z, pl.ds(0, HALF), :] += ring_a[3] + ring_a[6]
    planes = [
        copies.start(
            cross_in.at[lax.rem(y + step, NY), z, pl.ds(0, HALF), :],
            plane_in.at[step - 1],
            along_y(step),
        )
        for step in (1, 3, 2)
    ]
    pass_b(3)
    right_b.wait_recv()
    left_b.wait_recv()
    lower = cross_in[y, z, pl.ds(HALF, HALF), :] + ring_b[3] + ring_b[6]
    qk_out[pl.ds(HALF, HALF), :] = lower[:, :width]
    value_out[pl.ds(HALF, HALF), :] = lower[:, width:]
    for copy in planes:
        copy.wait_recv()
    upper = cross_in[y, z, pl.ds(0, HALF), :] + plane_in[0] + plane_in[1] + plane_in[2]
    qk_out[pl.ds(0, HALF), :] = upper[:, :width]
    value_out[pl.ds(0, HALF), :] = upper[:, width:]
    own_columns.wait()
    for copy in sideways:
        copy.wait_recv()

    @pl.loop(0, tokens_out.shape[0] // 8)
    def _(block):
        here = pl.ds(pl.multiple_of(block * 8, 8), 8)
        tokens_out[here, :] += column_in[0, here, :] + column_in[1, here, :] + column_in[2, here, :]

    copies.finish()
    assert len(copies.all) == SCATTER_COPIES


def scatter_sums(token_terms, weight_terms):
    length = token_terms.shape[0]
    both = weight_terms.shape[1]
    width = both // 2
    return pl.pallas_call(
        scatter_kernel,
        out_shape=(
            jax.ShapeDtypeStruct((length, width), f32),
            jax.ShapeDtypeStruct((ROWS, width), f32),
            jax.ShapeDtypeStruct((ROWS, width), f32),
        ),
        in_specs=[pl.BlockSpec(memory_space=pl.ANY), pl.BlockSpec(memory_space=pltpu.VMEM)],
        out_specs=(pl.BlockSpec(memory_space=pltpu.VMEM),) * 3,
        scratch_shapes=[
            pltpu.VMEM((3, length, width), f32),
            pltpu.VMEM((NY, NZ, ROWS, both), f32),
            pltpu.VMEM((7, NY, HALF, both), f32),
            pltpu.VMEM((7, HALF, both), f32),
            pltpu.VMEM((3, NZ, HALF, both), f32),
            pltpu.VMEM((3, HALF, both), f32),
            pltpu.SemaphoreType.DMA,
            pltpu.SemaphoreType.DMA((SCATTER_COPIES,)),
            pltpu.SemaphoreType.DMA((SCATTER_COPIES,)),
        ],
        compiler_params=pltpu.CompilerParams(
            collective_id=1, has_side_effects=True, vmem_limit_bytes=48 * 2**20
        ),
        name="scatter_sums",
    )(token_terms, weight_terms.reshape(2, NY, NZ, ROWS, both))


def pack_kernel(tokens_ref, full_ref, slots_ref, rows_ref, acc, pay):
    step = pl.program_id(0)
    length, both = acc.shape
    rows = rows_ref.shape[0]

    @pl.when(step == 0)
    def _():
        acc[...] = jnp.zeros_like(acc)

    @pl.when(step < 8)
    def _():
        acc[...] += dot3(halves(tokens_ref[...]), halves(full_ref[...]))

    @pl.when(step == 7)
    def _():
        for head in range(both // (2 * HD)):
            here = pl.ds(head * length, length)
            for part in range(2):
                column = part * both // 2 + head * HD
                upper, lower = halves(acc[:, column : column + HD])
                pay[here, part * HD : (part + 1) * HD] = upper
                pay[here, (2 + part) * HD : (3 + part) * HD] = lower

    @pl.when(step >= 8)
    def _():
        place = lax.broadcasted_iota(jnp.int32, (rows, slots_ref.shape[1]), 0) + (step - 8) * rows
        moved = dot(one(place == slots_ref[...]), pay[...])
        rows_ref[...] = moved[:, : 2 * HD] + moved[:, 2 * HD :]


def pack_rows(inputs, full, slots, room):
    length, depth = inputs.shape
    both = full.shape[1]
    total = slots.shape[1]
    return pl.pallas_call(
        pack_kernel,
        grid=(16,),
        out_shape=jax.ShapeDtypeStruct((OWNERS * room, 2 * HD), f32),
        in_specs=[
            pl.BlockSpec((length, depth // 8), lambda i: (0, jnp.minimum(i, 7))),
            pl.BlockSpec((depth // 8, both), lambda i: (jnp.minimum(i, 7), 0)),
            pl.BlockSpec((1, total), lambda i: (0, 0)),
        ],
        out_specs=pl.BlockSpec((4 * room, 2 * HD), lambda i: (jnp.maximum(i - 8, 0), 0)),
        scratch_shapes=[pltpu.VMEM((length, both), f32), pltpu.VMEM((total, 4 * HD), bf16)],
        compiler_params=pltpu.CompilerParams(vmem_limit_bytes=BIG),
        name="project_and_pack",
    )(inputs, full, slots)


def attend_kernel(marks_ref, rows_ref, early_ref, replies_ref, spread, seats, valid, answer):
    groups = marks_ref.shape[0]
    wide = marks_ref.shape[2]
    owned = spread.shape[1]
    seat = spread.shape[2]
    size = groups * seat

    @pl.loop(0, groups)
    def _(group):
        here = pl.ds(pl.multiple_of(group * wide, wide), wide)
        place = lax.broadcasted_iota(jnp.int32, (TALL, wide), 0)
        chosen = one(place == marks_ref[group])
        seats[group] = chosen
        upper, lower = halves(rows_ref[here, :])
        early = early_ref[pl.ds(group * GROUP, GROUP), pl.ds(0, wide // GROUP), :]
        early_upper, early_lower = halves(early.reshape(wide, HD))
        present = jnp.ones((wide, LANES), bf16)
        moved = dot(
            chosen, jnp.concatenate([upper, early_upper, lower, early_lower, present], axis=1)
        )
        spread[group] = (moved[:, : 3 * HD] + moved[:, 3 * HD : 6 * HD]).reshape(owned, seat, 3 * HD)
        valid[group] = moved[:, 6 * HD :].reshape(owned, seat, LANES)

    @pl.loop(0, owned // 4)
    def _(block):
        for lane in range(4):
            index = block * 4 + lane
            rows = spread[:, index].reshape(size, 3 * HD)
            present = valid[:, index].reshape(size, LANES)[:, :size] > 0.5
            qk = halves(rows[:, :HD])
            value = halves(rows[:, HD : 2 * HD])
            upstream = halves(rows[:, 2 * HD :])
            scores = jnp.where(present, dot3(qk, qk, NT) / HD, masked_score)
            weights = jnp.exp(scores - jnp.max(scores, axis=0, keepdims=True))
            weights = weights / jnp.sum(weights, axis=0, keepdims=True)
            slopes = dot3(value, upstream, NT)
            middle = jnp.sum(weights * slopes, axis=0, keepdims=True)
            slopes = weights * (slopes - middle)
            grad_qk = dot3(halves(slopes + slopes.T), qk) / HD
            grad_value = dot3(halves(weights), upstream)
            answer[:, index] = jnp.concatenate([grad_qk, grad_value], axis=1).reshape(
                groups, seat, 2 * HD
            )

    @pl.loop(0, groups)
    def _(group):
        here = pl.ds(pl.multiple_of(group * wide, wide), wide)
        upper, lower = halves(answer[group].reshape(TALL, 2 * HD))
        moved = dot(seats[group], jnp.concatenate([upper, lower], axis=1), TN)
        replies_ref[here, :] = moved[:, : 2 * HD] + moved[:, 2 * HD :]


def attend(rows, early, marks, room):
    groups = OWNERS // GROUP
    owned = TALL // (3 * GROUP)
    seat = 3 * GROUP
    return pl.pallas_call(
        attend_kernel,
        out_shape=jax.ShapeDtypeStruct((OWNERS * room, 2 * HD), f32),
        in_specs=[pl.BlockSpec(memory_space=pltpu.VMEM)] * 3,
        out_specs=pl.BlockSpec(memory_space=pltpu.VMEM),
        scratch_shapes=[
            pltpu.VMEM((groups, owned, seat, 3 * HD), f32),
            pltpu.VMEM((groups, TALL, GROUP * room), bf16),
            pltpu.VMEM((groups, owned, seat, LANES), f32),
            pltpu.VMEM((groups, owned, seat, 2 * HD), f32),
        ],
        compiler_params=pltpu.CompilerParams(vmem_limit_bytes=BIG),
        name="attend",
    )(marks, rows, early)


def unpack_rows(back, slots_ref, high, low, heads):
    source = jnp.concatenate(halves(back), axis=1)
    length = slots_ref.shape[0]
    for head in range(heads):
        place = lax.broadcasted_iota(jnp.int32, (length, back.shape[0]), 1)
        moved = dot(one(place == slots_ref[:, head : head + 1]), source)
        there = pl.ds(head * HD, HD)
        high[:, there], low[:, there] = halves(moved[:, :HD] + moved[:, HD:])


def line_of_sums(tokens, half, there, gradients):
    per_line = NZ * ROWS
    start = pl.multiple_of((half * NY + there) * per_line, per_line)
    sums = dot3(halves(tokens[:, pl.ds(start, per_line)]), gradients, TN)
    return sums.reshape(NZ, ROWS, sums.shape[1])


QK, VALUE, GRAD_VALUE, GRAD_QK = range(4)


def cluster_kernel(
    pay_ref, slots_ref, marks_ref, early_ref, tall_slots_ref, tokens_ref,
    back_qk_ref, high_ref, low_ref, own_ref,
    leaving, landed, seats, spread, valid, weights, answer, tokens, away, cross_in,
    local_sem, send_sem, recv_sem, cross_send, cross_recv,
):
    me = lax.axis_index("ctx")
    rep, y, _ = position()
    other = {"rep": 1 - rep}
    fetch = pltpu.make_async_copy(tokens_ref, tokens, local_sem.at[4])
    fetch.start()
    groups, _, wide = marks_ref.shape
    owned, seat = spread.shape[2], spread.shape[3]
    size = groups * seat
    rows = 4 * ROOM

    barrier = pltpu.get_barrier_semaphore()

    @pl.loop(1, OWNERS)
    def _(step):
        there = {"ctx": lax.rem(me + step, OWNERS)}
        pl.semaphore_signal(barrier, inc=1, device_id=there, device_id_type=MESH)

    pl.semaphore_signal(barrier, inc=1, device_id=other, device_id_type=MESH)

    def target(kind):
        return back_qk_ref if kind == GRAD_QK else landed.at[kind]

    def remote(kind, step):
        there = lax.rem(me + step, OWNERS)
        return pltpu.make_async_remote_copy(
            src_ref=leaving.at[kind, there],
            dst_ref=target(kind).at[me],
            send_sem=send_sem.at[kind, step],
            recv_sem=recv_sem.at[kind, step],
            device_id={"ctx": there},
            device_id_type=MESH,
        )

    def stay(kind):
        return pltpu.make_async_copy(leaving.at[kind, me], target(kind).at[me], local_sem.at[kind])

    def start(kind, there):
        @pl.when(there == me)
        def _():
            stay(kind).start()

        @pl.when(there != me)
        def _():
            remote(kind, lax.rem(there - me + OWNERS, OWNERS)).start()

    def arrive(kind):
        stay(kind).wait()

        @pl.loop(1, OWNERS)
        def _(step):
            remote(kind, step).wait_recv()

    def pack(kind, block):
        place = lax.broadcasted_iota(jnp.int32, (rows, slots_ref.shape[1]), 0) + block * rows
        moved = dot(one(place == slots_ref[...]), pay_ref[kind])
        moved = moved[:, :HD] + moved[:, HD:]
        for lane in range(4):
            leaving[kind, block * 4 + lane] = moved[lane * ROOM : (lane + 1) * ROOM]

    def take(kind, group, source):
        upper, lower = halves(source)
        moved = dot(seats[group], jnp.concatenate([upper, lower], axis=1))
        spread[kind, group] = (moved[:, :HD] + moved[:, HD:]).reshape(owned, seat, HD)

    def give(kind):
        @pl.loop(0, groups)
        def _(index):
            group = lax.rem(lax.div(me, GROUP) + index, groups)
            upper, lower = halves(answer[group].reshape(TALL, HD))
            moved = dot(seats[group], jnp.concatenate([upper, lower], axis=1), TN)
            moved = (moved[:, :HD] + moved[:, HD:]).reshape(GROUP, ROOM, HD)
            leaving[kind, pl.ds(group * GROUP, GROUP)] = moved
            for lane in range(GROUP):
                start(kind, group * GROUP + lane)

    def first_block():
        return lax.div(me, 4)

    pack(QK, first_block())
    pl.semaphore_wait(barrier, OWNERS)
    for lane in range(4):
        start(QK, first_block() * 4 + lane)

    @pl.loop(1, OWNERS // 4)
    def _(index):
        block = lax.rem(first_block() + index, OWNERS // 4)
        pack(QK, block)
        for lane in range(4):
            start(QK, block * 4 + lane)

    @pl.loop(0, OWNERS // 4)
    def _(block):
        pack(VALUE, block)

    @pl.loop(0, groups)
    def _(group):
        place = lax.broadcasted_iota(jnp.int32, (TALL, wide), 0)
        chosen = one(place == marks_ref[group])
        seats[group] = chosen
        early = early_ref[pl.ds(group * GROUP, GROUP), pl.ds(0, ROOM), :].reshape(wide, HD)
        upper, lower = halves(early)
        present = jnp.ones((wide, LANES), bf16)
        moved = dot(chosen, jnp.concatenate([upper, lower, present], axis=1))
        spread[2, group] = (moved[:, :HD] + moved[:, HD : 2 * HD]).reshape(owned, seat, HD)
        valid[group] = moved[:, 2 * HD :].reshape(owned, seat, LANES)

    arrive(QK)

    @pl.loop(0, OWNERS)
    def _(index):
        start(VALUE, lax.rem(me + index, OWNERS))

    @pl.loop(0, groups)
    def _(group):
        take(QK, group, landed[QK, pl.ds(group * GROUP, GROUP)].reshape(wide, HD))

    def cluster(kind, index):
        return halves(spread[kind, :, index].reshape(size, HD))

    @pl.loop(0, owned // 4)
    def _(block):
        for lane in range(4):
            index = block * 4 + lane
            present = valid[:, index].reshape(size, LANES)[:, :size] > 0.5
            qk = cluster(QK, index)
            scores = jnp.where(present, dot3(qk, qk, NT) / HD, masked_score)
            raised = jnp.exp(scores - jnp.max(scores, axis=0, keepdims=True))
            raised = raised / jnp.sum(raised, axis=0, keepdims=True)
            weights[index] = raised
            answer[:, index] = dot3(halves(raised), cluster(2, index)).reshape(groups, seat, HD)

    give(GRAD_VALUE)
    arrive(VALUE)

    @pl.loop(0, groups)
    def _(group):
        take(VALUE, group, landed[VALUE, pl.ds(group * GROUP, GROUP)].reshape(wide, HD))

    @pl.loop(0, owned // 4)
    def _(block):
        for lane in range(4):
            index = block * 4 + lane
            raised = weights[index]
            slopes = dot3(cluster(VALUE, index), cluster(2, index), NT)
            middle = jnp.sum(raised * slopes, axis=0, keepdims=True)
            slopes = raised * (slopes - middle)
            grad_qk = dot3(halves(slopes + slopes.T), cluster(QK, index)) / HD
            answer[:, index] = grad_qk.reshape(groups, seat, HD)

    give(GRAD_QK)
    arrive(GRAD_VALUE)

    back = landed[GRAD_VALUE].reshape(OWNERS * ROOM, HD)
    unpack_rows(back, tall_slots_ref, high_ref, low_ref, high_ref.shape[1] // HD)
    fetch.wait()

    def cross(step):
        there = lax.rem(y + step, NY)
        return pltpu.make_async_remote_copy(
            src_ref=away.at[there],
            dst_ref=cross_in.at[there],
            send_sem=cross_send.at[step],
            recv_sem=cross_recv.at[step],
            device_id=other,
            device_id_type=MESH,
        )

    @pl.loop(0, NY)
    def _(step):
        there = lax.rem(y + step, NY)
        away[there] = line_of_sums(tokens, 1 - rep, there, (high_ref[...], low_ref[...]))
        cross(step).start()

    @pl.loop(0, NY)
    def _(step):
        there = lax.rem(y + step, NY)
        mine = line_of_sums(tokens, rep, there, (high_ref[...], low_ref[...]))
        cross(step).wait_recv()
        own_ref[there] = mine + cross_in[there]

    arrive(GRAD_QK)

    @pl.loop(0, NY)
    def _(step):
        cross(step).wait_send()

    @pl.loop(1, OWNERS)
    def _(step):
        for kind in range(4):
            remote(kind, step).wait_send()


def cluster_part(pay, slots, marks, early, tall_slots, inputs):
    groups = OWNERS // GROUP
    owned = TALL // (3 * GROUP)
    seat = 3 * GROUP
    size = groups * seat
    length = inputs.shape[0]
    width = pay.shape[1] // length * HD
    vmem, anywhere = pl.BlockSpec(memory_space=pltpu.VMEM), pl.BlockSpec(memory_space=pl.ANY)
    return pl.pallas_call(
        cluster_kernel,
        out_shape=(
            jax.ShapeDtypeStruct((OWNERS, ROOM, HD), f32),
            jax.ShapeDtypeStruct((length, width), bf16),
            jax.ShapeDtypeStruct((length, width), bf16),
            jax.ShapeDtypeStruct((NY, NZ, ROWS, width), f32),
        ),
        in_specs=[vmem, vmem, vmem, vmem, vmem, anywhere],
        out_specs=(anywhere, vmem, vmem, vmem),
        scratch_shapes=[
            pltpu.VMEM((4, OWNERS, ROOM, HD), f32),
            pltpu.VMEM((3, OWNERS, ROOM, HD), f32),
            pltpu.VMEM((groups, TALL, GROUP * ROOM), bf16),
            pltpu.VMEM((3, groups, owned, seat, HD), f32),
            pltpu.VMEM((groups, owned, seat, LANES), f32),
            pltpu.VMEM((owned, size, size), f32),
            pltpu.VMEM((groups, owned, seat, HD), f32),
            pltpu.VMEM(inputs.shape, f32),
            pltpu.VMEM((NY, NZ, ROWS, width), f32),
            pltpu.VMEM((NY, NZ, ROWS, width), f32),
            pltpu.SemaphoreType.DMA((5,)),
            pltpu.SemaphoreType.DMA((4, OWNERS)),
            pltpu.SemaphoreType.DMA((4, OWNERS)),
            pltpu.SemaphoreType.DMA((NY,)),
            pltpu.SemaphoreType.DMA((NY,)),
        ],
        compiler_params=pltpu.CompilerParams(
            collective_id=2, has_side_effects=True, vmem_limit_bytes=BIG
        ),
        name="exchange_and_attend",
    )(pay, slots, marks, early, tall_slots, inputs)


def grads_kernel(
    back_qk_ref, back_value_ref, slots_ref, tokens_ref, full_ref, terms_ref, sums_ref, high, low
):
    length = tokens_ref.shape[0]
    width = high.shape[1] // 2
    total = back_qk_ref.shape[0]

    @pl.when(pl.program_id(0) == 0)
    def _():
        qk_upper, qk_lower = halves(back_qk_ref[...])
        upper, lower = halves(back_value_ref[...])
        source = jnp.concatenate([qk_upper, upper, qk_lower, lower], axis=1)
        for head in range(width // HD):
            place = lax.broadcasted_iota(jnp.int32, (length, total), 1)
            chosen = one(place == slots_ref[:, head : head + 1])
            both = dot(chosen, source)
            upper, lower = halves(both[:, : 2 * HD] + both[:, 2 * HD :])
            for part in range(2):
                there = pl.ds(part * width + head * HD, HD)
                high[:, there] = upper[:, part * HD : (part + 1) * HD]
                low[:, there] = lower[:, part * HD : (part + 1) * HD]

    combined = high[...], low[...]
    terms_ref[...] = dot3(combined, halves(full_ref[...]), NT)
    sums_ref[...] = dot3(halves(tokens_ref[...]), combined, TN)


def local_grads(back_qk, back_value, slots, inputs, full):
    length, depth = inputs.shape
    both = full.shape[1]
    total = back_qk.shape[0]
    return pl.pallas_call(
        grads_kernel,
        grid=(8,),
        out_shape=(
            jax.ShapeDtypeStruct((length, depth), f32),
            jax.ShapeDtypeStruct((depth, both), f32),
        ),
        in_specs=[
            pl.BlockSpec((total, HD), lambda i: (0, 0)),
            pl.BlockSpec((total, HD), lambda i: (0, 0)),
            pl.BlockSpec(slots.shape, lambda i: (0, 0)),
            pl.BlockSpec((length, depth // 8), lambda i: (0, i)),
            pl.BlockSpec((depth // 8, both), lambda i: (i, 0)),
        ],
        out_specs=(
            pl.BlockSpec((length, depth // 8), lambda i: (0, i)),
            pl.BlockSpec((depth // 8, both), lambda i: (i, 0)),
        ),
        scratch_shapes=[pltpu.VMEM((length, both), bf16)] * 2,
        compiler_params=pltpu.CompilerParams(vmem_limit_bytes=BIG),
        name="unpack_and_grads",
    )(back_qk, back_value, slots, inputs, full)


FINISH_COPIES = 2 + 14 + 14 + 4 + 6


def finish_kernel(
    back_qk_ref, high_ref, low_ref, sums_ref, slots_ref, tokens_ref, full_ref,
    tokens_out, qk_out, value_out,
    tokens, full, high, low, terms, away, own, cross_in,
    column_in, passing, ring_a, ring_b, line_in, plane_in,
    load_sem, send_sem, recv_sem, cross_send, cross_recv,
    line_send, line_recv,
):
    rep, y, z = position()
    x = lax.axis_index("tp")
    length = tokens.shape[0]
    both = full.shape[1]
    width = both // 2

    def along_y(step):
        return {"ctx": lax.rem(y + step, NY) * NZ + z}

    def along_z(step):
        return {"ctx": y * NZ + lax.rem(z + step, NZ)}

    def along_x(step):
        return {"tp": lax.rem(x + step, 4)}

    loads = [
        pltpu.make_async_copy(tokens_ref, tokens, load_sem.at[0]),
        pltpu.make_async_copy(full_ref, full, load_sem.at[1]),
        pltpu.make_async_copy(sums_ref, own.at[1], load_sem.at[2]),
    ]
    for load in reversed(loads):
        load.start()
    right, left, other = along_z(1), along_z(NZ - 1), {"rep": 1 - rep}
    barrier = pltpu.get_barrier_semaphore()
    partners = [along_y(1), along_y(2), along_y(3), right, left, other]
    partners += [along_x(1), along_x(3)]
    for partner in partners:
        pl.semaphore_signal(barrier, inc=1, device_id=partner, device_id_type=MESH)

    def cross(step):
        there = lax.rem(y + step, NY)
        return pltpu.make_async_remote_copy(
            src_ref=away.at[there],
            dst_ref=cross_in.at[there],
            send_sem=cross_send.at[step],
            recv_sem=cross_recv.at[step],
            device_id=other,
            device_id_type=MESH,
        )

    def line_sum(half, there):
        return line_of_sums(tokens, half, there, (high[:, :width], low[:, :width]))

    def away_lines():
        @pl.loop(0, NY)
        def _(step):
            there = lax.rem(y + step, NY)
            away[there] = line_sum(1 - rep, there)
            cross(step).start()

    def own_lines():
        @pl.loop(0, NY)
        def _(step):
            there = lax.rem(y + step, NY)
            mine = line_sum(rep, there)
            cross(step).wait_recv()
            own[0, there] = mine + cross_in[there]

    def depth(turn):
        return lax.rem(z + turn, NZ)

    def piece(step, turn, part):
        return pltpu.make_async_remote_copy(
            src_ref=own.at[part, lax.rem(y + step, NY), depth(turn), pl.ds(HALF, HALF), :],
            dst_ref=line_in.at[part, step - 1, depth(turn)],
            send_sem=line_send.at[part, step - 1, turn],
            recv_sem=line_recv.at[part, step - 1, turn],
            device_id=along_y(step),
            device_id_type=MESH,
        )

    def send_pieces(part):
        for turn in (4, 5, 3, 6, 2, 7, 1, 0):
            for step in (1, 3, 2):
                piece(step, turn, part).start()

    copies = Copies(send_sem, recv_sem)

    def plane(turn, part):
        return own.at[part, :, depth(turn), pl.ds(0, HALF), :]

    flow_a, flow_b = [None, None], [None, None]

    def turn_a(turn, part):
        ring = ring_a.at[part]
        if turn == 0:
            flow_a[part] = (
                copies.start(plane(4, part), ring.at[0], right),
                copies.start(plane(5, part), ring.at[4], left),
            )
            return
        rightward, leftward = flow_a[part]
        rightward.wait_recv()
        ring_a[part, turn - 1] += plane(4 - turn, part)[...]
        rightward = copies.start(ring.at[turn - 1], ring.at[turn], right)
        if turn < 3:
            leftward.wait_recv()
            ring_a[part, 3 + turn] += plane(5 + turn, part)[...]
            leftward = copies.start(ring.at[3 + turn], ring.at[4 + turn], left)
        flow_a[part] = rightward, leftward

    def along_lines(turn, part):
        for step in (1, 2, 3):
            piece(step, turn, part).wait_recv()
        here = depth(turn)
        return own[part, y, here, pl.ds(HALF, HALF), :] + (
            line_in[part, 0, here] + line_in[part, 1, here] + line_in[part, 2, here]
        )

    def turn_b(turn, part):
        ring = ring_b.at[part]
        if turn == 0:
            first = own.at[part, y, depth(4), pl.ds(HALF, HALF), :]
            second = own.at[part, y, depth(5), pl.ds(HALF, HALF), :]
            first[...] = along_lines(4, part)
            rightward = copies.start(first, ring.at[0], right)
            second[...] = along_lines(5, part)
            flow_b[part] = rightward, copies.start(second, ring.at[4], left)
            return
        rightward, leftward = flow_b[part]
        mine = along_lines(4 - turn, part)
        rightward.wait_recv()
        ring_b[part, turn - 1] += mine
        rightward = copies.start(ring.at[turn - 1], ring.at[turn], right)
        if turn < 3:
            mine = along_lines(5 + turn, part)
            leftward.wait_recv()
            ring_b[part, 3 + turn] += mine
            leftward = copies.start(ring.at[3 + turn], ring.at[4 + turn], left)
        flow_b[part] = rightward, leftward

    planes = [[], []]

    def end_a(part):
        for copy in flow_a[part]:
            copy.wait_recv()
        own[part, :, z, pl.ds(0, HALF), :] = plane(0, part)[...] + (
            ring_a[part, 3] + ring_a[part, 6]
        )
        for step in (1, 3, 2):
            planes[part].append(copies.start(
                own.at[part, lax.rem(y + step, NY), z, pl.ds(0, HALF), :],
                plane_in.at[part, step - 1],
                along_y(step),
            ))

    def end_b(part, out):
        mine = along_lines(0, part)
        for copy in flow_b[part]:
            copy.wait_recv()
        out[pl.ds(HALF, HALF), :] = mine + ring_b[part, 3] + ring_b[part, 6]

    middle = length // 2
    upper_rows, lower_rows = pl.ds(0, middle), pl.ds(middle, middle)

    def columns(step):
        start = pl.multiple_of(lax.rem(x + step, 4) * width, width)
        return dot3((high[...], low[...]), halves(full[pl.ds(start, width), :]), NT)

    pl.semaphore_wait(barrier, len(partners))
    loads[2].wait()
    turn_a(0, 1)
    send_pieces(1)
    high[:, pl.ds(width, width)] = high_ref[...]
    low[:, pl.ds(width, width)] = low_ref[...]
    unpack_rows(back_qk_ref[...], slots_ref, high, low, width // HD)
    loads[0].wait()
    away_lines()
    turn_a(1, 1)
    own_lines()
    turn_a(0, 0)
    send_pieces(0)
    turn_b(0, 1)
    turn_a(2, 1)
    loads[1].wait()
    terms[1] = columns(2)
    by_right = copies.start(terms.at[1, upper_rows], passing.at[0], along_x(1))
    by_left = copies.start(terms.at[1, lower_rows], passing.at[1], along_x(3))
    turn_b(1, 1)
    turn_a(1, 0)
    turn_a(3, 1)
    terms[0] = columns(1)
    sideways = [copies.start(terms.at[0, lower_rows], column_in.at[0, lower_rows], along_x(1))]
    turn_b(0, 0)
    turn_b(2, 1)
    turn_a(2, 0)
    terms[2] = columns(3)
    sideways.append(
        copies.start(terms.at[2, upper_rows], column_in.at[1, upper_rows], along_x(3))
    )
    turn_b(1, 0)
    end_a(1)
    turn_b(3, 1)
    turn_a(3, 0)
    by_right.wait_recv()
    terms[0, upper_rows, :] += passing[0]
    sideways.append(
        copies.start(terms.at[0, upper_rows], column_in.at[0, upper_rows], along_x(1))
    )
    by_left.wait_recv()
    terms[2, lower_rows, :] += passing[1]
    sideways.append(
        copies.start(terms.at[2, lower_rows], column_in.at[1, lower_rows], along_x(3))
    )
    turn_b(2, 0)
    end_b(1, value_out)
    tokens_out[...] = columns(0)
    turn_b(3, 0)
    end_a(0)
    end_b(0, qk_out)
    for copy in sideways:
        copy.wait_recv()

    @pl.loop(0, length // 8)
    def _(block):
        here = pl.ds(pl.multiple_of(block * 8, 8), 8)
        tokens_out[here, :] += column_in[0, here, :] + column_in[1, here, :]

    for part, out in ((1, value_out), (0, qk_out)):
        for copy in planes[part]:
            copy.wait_recv()
        out[pl.ds(0, HALF), :] = own[part, y, z, pl.ds(0, HALF), :] + (
            plane_in[part, 0] + plane_in[part, 1] + plane_in[part, 2]
        )

    @pl.loop(0, NY)
    def _(step):
        cross(step).wait_send()

    @pl.loop(1, NY)
    def _(step):
        for part in range(2):
            for turn in range(NZ):
                piece(step, turn, part).wait_send()

    copies.finish()
    assert len(copies.all) == FINISH_COPIES


def finish(back_qk, high, low, sums, slots, inputs, full):
    length, depth = inputs.shape
    both = full.shape[1]
    width = both // 2
    vmem, anywhere = pl.BlockSpec(memory_space=pltpu.VMEM), pl.BlockSpec(memory_space=pl.ANY)
    return pl.pallas_call(
        finish_kernel,
        out_shape=(
            jax.ShapeDtypeStruct((length, width), f32),
            jax.ShapeDtypeStruct((ROWS, width), f32),
            jax.ShapeDtypeStruct((ROWS, width), f32),
        ),
        in_specs=[vmem, vmem, vmem, vmem, vmem, anywhere, anywhere],
        out_specs=(vmem,) * 3,
        scratch_shapes=[
            pltpu.VMEM((length, depth), f32),
            pltpu.VMEM((depth, both), f32),
            pltpu.VMEM((length, both), bf16),
            pltpu.VMEM((length, both), bf16),
            pltpu.VMEM((3, length, width), f32),
            pltpu.VMEM((NY, NZ, ROWS, width), f32),
            pltpu.VMEM((2, NY, NZ, ROWS, width), f32),
            pltpu.VMEM((NY, NZ, ROWS, width), f32),
            pltpu.VMEM((2, length, width), f32),
            pltpu.VMEM((2, length // 2, width), f32),
            pltpu.VMEM((2, 7, NY, HALF, width), f32),
            pltpu.VMEM((2, 7, HALF, width), f32),
            pltpu.VMEM((2, 3, NZ, HALF, width), f32),
            pltpu.VMEM((2, 3, HALF, width), f32),
            pltpu.SemaphoreType.DMA((3,)),
            pltpu.SemaphoreType.DMA((FINISH_COPIES,)),
            pltpu.SemaphoreType.DMA((FINISH_COPIES,)),
            pltpu.SemaphoreType.DMA((NY,)),
            pltpu.SemaphoreType.DMA((NY,)),
            pltpu.SemaphoreType.DMA((2, 3, NZ)),
            pltpu.SemaphoreType.DMA((2, 3, NZ)),
        ],
        compiler_params=pltpu.CompilerParams(
            collective_id=3, has_side_effects=True, vmem_limit_bytes=52 * 2**20
        ),
        name="grads_and_scatter",
    )(back_qk, high, low, sums, slots, inputs, full)


def exchange(array):
    return lax.all_to_all(array, "ctx", split_axis=0, concat_axis=0, tiled=True)


def seat_numbers(marks, room):
    marks = marks.astype(jnp.int32) - 1
    source = lax.broadcasted_iota(jnp.int32, marks.shape, 0) % GROUP
    seats = (marks // 3) * (3 * GROUP) + source * 3 + marks % 3
    return jnp.where(marks < 0, -1, seats).reshape(OWNERS // GROUP, 1, GROUP * room)


def snug_part(inputs, full, pay, early, slots, tall_slots):
    marks = early[:, ROOM : ROOM + 2, :ROOM]
    held, place = marks[:, 0], marks[:, 1]
    seats = jnp.where(held > 0.5, (held - 1) * (3 * GROUP) + place, -1.0).astype(jnp.int32)
    seats = seats.reshape(OWNERS // GROUP, 1, GROUP * ROOM)
    back_qk, high, low, sums = cluster_part(pay, slots, seats, early, tall_slots, inputs)
    back_qk = back_qk.reshape(OWNERS * ROOM, HD)
    return finish(back_qk, high, low, sums, tall_slots, inputs, full)


def roomy_part(inputs, full, upstream, cluster):
    heads, length = cluster.shape
    order = jnp.arange(length, dtype=jnp.int32)
    earlier = order[:, None] < order[None, :]
    alike = cluster[:, :, None] == cluster[:, None, :]
    within = jnp.sum((alike & earlier).astype(jnp.int32), axis=1)
    head = jnp.arange(heads, dtype=jnp.int32)[:, None]
    ids = (head * CL_DEV + cluster % CL_DEV) * 3 + within
    slots = cluster // CL_DEV * SLOTS + ids
    marks = jnp.zeros((OWNERS * SLOTS,), f32).at[slots.reshape(-1)].set(
        (ids + 1).astype(f32).reshape(-1)
    )
    rows = upstream.reshape(length, heads, HD).transpose(1, 0, 2).reshape(-1, HD)
    early = jnp.zeros((OWNERS * SLOTS, HD), f32).at[slots.reshape(-1)].set(rows)
    early = exchange(early.reshape(OWNERS, SLOTS, HD))
    marks = exchange(marks.reshape(OWNERS, SLOTS))
    rows = pack_rows(inputs, full, slots.reshape(1, -1), SLOTS)
    rows = exchange(rows.reshape(OWNERS, SLOTS, 2 * HD)).reshape(OWNERS * SLOTS, 2 * HD)
    replies = attend(rows, early, seat_numbers(marks, SLOTS), SLOTS)
    returned = exchange(replies.reshape(OWNERS, SLOTS, 2 * HD)).reshape(OWNERS * SLOTS, 2 * HD)
    return scatter_sums(
        *local_grads(returned[:, :HD], returned[:, HD:], slots.T, inputs, full)
    )


def per_device(tokens, qk_weight, value_weight, grad_out, assign):
    inputs = tokens[0]
    heads_here = qk_weight.shape[1] // HD
    width = heads_here * HD
    cluster = assign[:, 0, :, 0]
    full, early, slots, tall_slots, pay = gather_and_project(
        qk_weight, value_weight, jnp.pad(cluster, ((0, 8 - heads_here), (0, 0))), grad_out[0],
        inputs,
    )
    full = full.reshape(-1, 2 * width)
    fullest = jnp.max(early[:, ROOM, PITCH])

    def snug(inputs, full, upstream, cluster, *routed):
        return snug_part(inputs, full, *routed)

    def roomy(inputs, full, upstream, cluster, *routed):
        return roomy_part(inputs, full, upstream, cluster)

    grad_tokens, grad_qk_weight, grad_value_weight = lax.cond(
        fullest <= ROOM, snug, roomy,
        inputs, full, grad_out[0], cluster, pay, early, slots, tall_slots,
    )
    return (grad_tokens[None], grad_qk_weight, grad_value_weight)


def solution(mesh):
    in_specs = (
        P("rep", "ctx", None),
        P(("rep", "ctx"), "tp"),
        P(("rep", "ctx"), "tp"),
        P("rep", "ctx", "tp"),
        P("tp", "rep", "ctx", None),
    )
    out_specs = (P("rep", "ctx", "tp"), P(("rep", "ctx"), "tp"), P(("rep", "ctx"), "tp"))
    return jax.shard_map(
        per_device, mesh=mesh, in_specs=in_specs, out_specs=out_specs, check_vma=False
    )
```
